32 devices in a mesh: dp: 4 (over y, x), tensor: 8 (over z, core).
Axes of the slice: x: 2, y: 2, z: 4, core: 2. Of those that a mesh axis runs over, the one named last changes fastest.
Arguments:
- inputs: bfloat16 [8192, 2048], P(('dp', 'tensor')), may hold values from -6 to 6
- out_grad: bfloat16 [8192, 2048], P(('dp', 'tensor')), may hold values from -6 to 6
- segments: int32 [4, 2048], P('dp'), may hold values from 0 to 3, never falling along the last dimension, each value on 1 to 1024 neighbouring positions
- w_qkv: float32 [3, 2048, 2048], P(None, 'dp', 'tensor'), may hold values from -0.125 to 0.125
- w_out: float32 [2048, 2048], P('tensor', 'dp'), may hold values from -2 to 2
- w_gate_up: float32 [2, 2048, 5632], P(None, 'dp', 'tensor'), may hold values from -0.125 to 0.125
- w_down: float32 [5632, 2048], P('tensor', 'dp'), may hold values from -0.15625 to 0.15625
- qkv_bias: float32 [3, 2048], P(None, 'tensor'), may hold values from -3 to 3
- norm_gain: float32 [2, 2048], replicated, may hold values from 0.5 to 1.5
- norm_bias: float32 [2, 2048], replicated, may hold values from -2 to 2
- first_qkv: float32 [3, 2048, 2048], P(None, 'dp', 'tensor'), may hold values from -271.529 to 271.529
- first_out: float32 [2048, 2048], P('tensor', 'dp'), may hold values from -54.3058 to 54.3058
- first_gate_up: float32 [2, 2048, 5632], P(None, 'dp', 'tensor'), may hold values from -54.3058 to 54.3058
- first_down: float32 [5632, 2048], P('tensor', 'dp'), may hold values from -54.3058 to 54.3058
- first_bias: float32 [3, 2048], P(None, 'tensor'), may hold values from -271.529 to 271.529
- first_gain: float32 [2, 2048], replicated, may hold values from -271.529 to 271.529
- first_shift: float32 [2, 2048], replicated, may hold values from -271.529 to 271.529
- second_qkv: float32 [3, 2048, 2048], P(None, 'dp', 'tensor'), may hold values from 163.84 to 1638.4
- second_out: float32 [2048, 2048], P('tensor', 'dp'), may hold values from 8.192 to 32.768
- second_gate_up: float32 [2, 2048, 5632], P(None, 'dp', 'tensor'), may hold values from 8.192 to 32.768
- second_down: float32 [5632, 2048], P('tensor', 'dp'), may hold values from 8.192 to 32.768
- second_bias: float32 [3, 2048], P(None, 'tensor'), may hold values from 16.384 to 163.84
- second_gain: float32 [2, 2048], replicated, may hold values from 16.384 to 163.84
- second_shift: float32 [2, 2048], replicated, may hold values from 16.384 to 163.84
Outputs:
- outputs: bfloat16 [8192, 2048], P(('dp', 'tensor'))
- input_grad: bfloat16 [8192, 2048], P(('dp', 'tensor'))
- grad_w_qkv: float32 [3, 2048, 2048], P(None, 'dp', 'tensor')
- grad_w_out: float32 [2048, 2048], P('tensor', 'dp')
- grad_w_gate_up: float32 [2, 2048, 5632], P(None, 'dp', 'tensor')
- grad_w_down: float32 [5632, 2048], P('tensor', 'dp')
- grad_qkv_bias: float32 [3, 2048], P(None, 'tensor')
- grad_norm_gain: float32 [2, 2048], replicated
- grad_norm_bias: float32 [2, 2048], replicated
- new_w_qkv: float32 [3, 2048, 2048], P(None, 'dp', 'tensor')
- new_w_out: float32 [2048, 2048], P('tensor', 'dp')
- new_w_gate_up: float32 [2, 2048, 5632], P(None, 'dp', 'tensor')
- new_w_down: float32 [5632, 2048], P('tensor', 'dp')
- new_qkv_bias: float32 [3, 2048], P(None, 'tensor')
- new_norm_gain: float32 [2, 2048], replicated
- new_norm_bias: float32 [2, 2048], replicated
- new_first_qkv: float32 [3, 2048, 2048], P(None, 'dp', 'tensor')
- new_first_out: float32 [2048, 2048], P('tensor', 'dp')
- new_first_gate_up: float32 [2, 2048, 5632], P(None, 'dp', 'tensor')
- new_first_down: float32 [5632, 2048], P('tensor', 'dp')
- new_first_bias: float32 [3, 2048], P(None, 'tensor')
- new_first_gain: float32 [2, 2048], replicated
- new_first_shift: float32 [2, 2048], replicated
- new_second_qkv: float32 [3, 2048, 2048], P(None, 'dp', 'tensor')
- new_second_out: float32 [2048, 2048], P('tensor', 'dp')
- new_second_gate_up: float32 [2, 2048, 5632], P(None, 'dp', 'tensor')
- new_second_down: float32 [5632, 2048], P('tensor', 'dp')
- new_second_bias: float32 [3, 2048], P(None, 'tensor')
- new_second_gain: float32 [2, 2048], replicated
- new_second_shift: float32 [2, 2048], replicated
The draws below stay inside these ranges and needn't reach their ends.
Inputs may be any that keep to these rules, and one draw needn't show every extreme that they name: `segments`: segment numbers never fall along a sequence; a document has at most 1024 tokens.
All inputs are finite; a program needn't handle non-finite values.
Results may differ from the reference program's by a relative error of at most 0.019.
Values may be sent and summed in bfloat16 or wider, within the bound.
A program may use at most 192 MiB of HBM per device.

```python
import math
import jax
import jax.numpy as jnp
import numpy as np
from jax import lax

D = 2048
HEADS = 32
HD = 64
ROT = 16
FF = 5632
SEQ_LEN = 2048
STEP = 10
NSEQ = 4
TOKENS = 8192


def shard_levels(own_key, extent, cuts, smallest, largest):
    def one(position, parts):
        draws = jax.random.uniform(jax.random.fold_in(jax.random.fold_in(own_key, 6), position), (parts,), jnp.float32, smallest / len(cuts), largest / len(cuts))
        return jnp.repeat(jnp.exp(draws), extent[position] // parts).reshape((-1,) + (1,) * (len(extent) - position - 1))

    level = one(*cuts[0])
    for cut in cuts[1:]:
        level = level * one(*cut)
    return level


def split_up(count, total, most, slope):
    weights = [(1 << 20) // math.isqrt(standing ** slope) + 1 for standing in range(2, count + 1)]
    surplus, counts = total - most - (count - 1), [1] * (count - 1)
    while surplus > 0:
        candidates = [i for i in range(count - 1) if counts[i] < most]
        pool, left = sum([weights[i] for i in candidates]), surplus
        for i in candidates:
            extra = min(most - counts[i], max(1, left * weights[i] // pool), surplus)
            counts[i] = counts[i] + extra
            surplus = surplus - extra
    return np.array([most] + counts)


def ragged(stream_key, amount, total, bound, skew):
    if amount == 2:
        one = jax.random.randint(stream_key, (), max(1, total - bound), min(bound, total - 1) + 1)
        return jnp.stack([one, total - one])
    lengths = jnp.asarray(split_up(amount, total, bound, skew), jnp.int32)
    pairs = (amount - 1) // 2
    giver, taker = lengths[1:1 + 2 * pairs:2], lengths[2:2 + 2 * pairs:2]
    margin = jnp.minimum(giver - 1, bound - taker)
    shifted = jax.random.randint(jax.random.fold_in(stream_key, 1), (pairs,), 0, 1 << 20) % (margin + 1)
    lengths = lengths.at[1:1 + 2 * pairs:2].set(giver - shifted).at[2:2 + 2 * pairs:2].set(taker + shifted)
    return lengths[jax.random.permutation(jax.random.fold_in(stream_key, 2), amount)]


def bell_draw(key, dims, deviation, bound, pieces=(), kind=jnp.bfloat16):
    loudness = shard_levels(key, dims, pieces, -0.22, 0.18) if pieces else 1.0
    drawn = jax.random.normal(key, dims, jnp.float32) * deviation * loudness
    return jnp.minimum(jnp.maximum(drawn, -bound), bound).astype(kind)


def setup_inputs(seed: int = 0) -> dict:
    keys = jax.random.split(jax.random.key(seed), 25)
    return {
        "inputs": bell_draw(keys[0], (TOKENS, D), 1.0, 6.0, ((0, 32),)),
        "out_grad": bell_draw(keys[1], (TOKENS, D), 1.0, 6.0, ((0, 32),)),
        "segments": jax.vmap(lambda own: jnp.searchsorted(jnp.cumsum(ragged(own, 4, SEQ_LEN, SEQ_LEN // 2, 0)), jnp.arange(SEQ_LEN), side="right"))(jax.random.split(keys[2], NSEQ)).reshape((NSEQ, SEQ_LEN)).astype(jnp.int32),
        "w_qkv": bell_draw(keys[3], (3, D, HEADS * HD), D ** -0.5, 0.125, ((1, 4), (2, 8)), jnp.float32),
        "w_out": bell_draw(keys[4], (HEADS * HD, D), (HEADS * HD // 256) ** -0.5, 2.0, ((0, 8), (1, 4)), jnp.float32),
        "w_gate_up": bell_draw(keys[5], (2, D, FF), D ** -0.5, 0.125, ((1, 4), (2, 8)), jnp.float32),
        "w_down": bell_draw(keys[6], (FF, D), (FF // 4) ** -0.5, 0.15625, ((0, 8), (1, 4)), jnp.float32),
        "qkv_bias": bell_draw(keys[7], (3, HEADS * HD), 0.5, 3.0, ((1, 8),), jnp.float32),
        "norm_gain": jnp.clip(1.0 + 0.1 * jax.random.normal(keys[8], (2, D), jnp.float32), 0.5, 1.5),
        "norm_bias": bell_draw(keys[9], (2, D), 0.3, 2.0, (), jnp.float32),
        "first_qkv": bell_draw(keys[10], (3, D, HEADS * HD), (0.5 * TOKENS ** 0.5), 271.529, ((1, 4), (2, 8)), jnp.float32),
        "first_out": bell_draw(keys[11], (HEADS * HD, D), (0.1 * TOKENS ** 0.5), 54.3058, ((0, 8), (1, 4)), jnp.float32),
        "first_gate_up": bell_draw(keys[12], (2, D, FF), (0.1 * TOKENS ** 0.5), 54.3058, ((1, 4), (2, 8)), jnp.float32),
        "first_down": bell_draw(keys[13], (FF, D), (0.1 * TOKENS ** 0.5), 54.3058, ((0, 8), (1, 4)), jnp.float32),
        "first_bias": bell_draw(keys[14], (3, HEADS * HD), (0.5 * TOKENS ** 0.5), 271.529, ((1, 8),), jnp.float32),
        "first_gain": bell_draw(keys[15], (2, D), (0.5 * TOKENS ** 0.5), 271.529, (), jnp.float32),
        "first_shift": bell_draw(keys[16], (2, D), (0.5 * TOKENS ** 0.5), 271.529, (), jnp.float32),
        "second_qkv": jnp.clip(jnp.exp(math.log(1638.4) - 2.3025851 * jax.random.uniform(keys[17], (3, D, HEADS * HD), jnp.float32) ** shard_levels(keys[17], (3, D, HEADS * HD), ((1, 4), (2, 8)), -0.2, 0.2)), 163.84, 1638.4),
        "second_out": jnp.clip(jnp.exp(math.log(32.768) - 1.3862944 * jax.random.uniform(keys[18], (HEADS * HD, D), jnp.float32) ** shard_levels(keys[18], (HEADS * HD, D), ((0, 8), (1, 4)), -0.2, 0.2)), 8.192, 32.768),
        "second_gate_up": jnp.clip(jnp.exp(math.log(32.768) - 1.3862944 * jax.random.uniform(keys[19], (2, D, FF), jnp.float32) ** shard_levels(keys[19], (2, D, FF), ((1, 4), (2, 8)), -0.2, 0.2)), 8.192, 32.768),
        "second_down": jnp.clip(jnp.exp(math.log(32.768) - 1.3862944 * jax.random.uniform(keys[20], (FF, D), jnp.float32) ** shard_levels(keys[20], (FF, D), ((0, 8), (1, 4)), -0.2, 0.2)), 8.192, 32.768),
        "second_bias": jnp.clip(jnp.exp(math.log(163.84) - 2.30258502 * jax.random.uniform(keys[21], (3, HEADS * HD), jnp.float32) ** shard_levels(keys[21], (3, HEADS * HD), ((1, 8),), -0.2, 0.2)), 16.384, 163.84),
        "second_gain": jnp.clip(jnp.exp(jax.random.uniform(keys[22], (2, D), jnp.float32, math.log(16.384), math.log(163.84))), 16.384, 163.84),
        "second_shift": jnp.clip(jnp.exp(jax.random.uniform(keys[23], (2, D), jnp.float32, math.log(16.384), math.log(163.84))), 16.384, 163.84),
    }


@jax.custom_vjp
def low(v):
    return lax.optimization_barrier(v.astype(jnp.bfloat16)).astype(jnp.float32)

@jax.custom_vjp
def low_back(v):
    return v

def low_keep(v):
    return (low(v), None)

def low_pass(kept, grad):
    return (grad,)

def back_keep(v):
    return (v, None)

def back_low(kept, grad):
    return (low(grad),)
low.defvjp(low_keep, low_pass)
low_back.defvjp(back_keep, back_low)

def product(left, right):
    return jnp.dot(left, right, precision=lax.Precision.HIGHEST)

def layer_norm(values, gain_row, shift_row):
    average = lax.optimization_barrier(jnp.mean(values, axis=-1, keepdims=True))
    centred = values - average
    spread = lax.optimization_barrier(jnp.mean(centred * centred, axis=-1, keepdims=True))
    return centred * lax.rsqrt(spread + 1e-05) * gain_row + shift_row

def positions(segment_ids):
    length = segment_ids.shape[-1]
    indices = jnp.broadcast_to(jnp.arange(length, dtype=jnp.int32), segment_ids.shape)
    before = jnp.concatenate([jnp.full(segment_ids.shape[:-1] + (1,), -1, jnp.int32), segment_ids[..., :-1]], axis=-1)
    starts = lax.cummax(jnp.where(segment_ids != before, indices, 0), axis=segment_ids.ndim - 1)
    return indices - starts

def rotary_tables(position_ids, float_type):
    half_rot = ROT // 2
    frequency = 10000.0 ** (-(2.0 * jnp.arange(half_rot, dtype=float_type)) / ROT)
    angles = position_ids.astype(float_type)[..., None] * frequency
    return (jnp.cos(angles)[..., None, :], jnp.sin(angles)[..., None, :])

def rotate(values, cosine, sine):
    half_rot = ROT // 2
    lower_half = values[..., :half_rot]
    upper_half = values[..., half_rot:ROT]
    return jnp.concatenate([lower_half * cosine - upper_half * sine, upper_half * cosine + lower_half * sine, values[..., ROT:]], axis=-1)

def sequence_forward(weights, tokens_in, segment_row):
    qkv_low, out_low, gate_up_low, down_low, bias_three, gain_pair, shift_pair = weights
    length = tokens_in.shape[0]
    cosine, sine = rotary_tables(positions(segment_row), jnp.float32)
    normed_one = low(layer_norm(tokens_in, gain_pair[0], shift_pair[0]))
    query_lin = low_back(product(normed_one, qkv_low[0]) + bias_three[0])
    key_lin = low_back(product(normed_one, qkv_low[1]) + bias_three[1])
    value_low = low(low_back(product(normed_one, qkv_low[2]) + bias_three[2]))
    query_low = low(rotate(query_lin.reshape(length, HEADS, HD), cosine, sine))
    key_low = low(rotate(key_lin.reshape(length, HEADS, HD), cosine, sine))
    value_low = value_low.reshape(length, HEADS, HD)
    indices = jnp.arange(length, dtype=jnp.int32)
    visible = (segment_row[:, None] == segment_row[None, :]) & (indices[:, None] >= indices[None, :])

    def one_head(triple):
        query_head, key_head, value_head = triple
        scores = low_back(product(query_head, key_head.T) * 0.125)
        scores = jnp.where(visible, scores, -1e+30)
        attention = low(jax.nn.softmax(scores, axis=-1))
        return low(low_back(product(attention, value_head)))
    context = lax.map(jax.checkpoint(one_head), (jnp.swapaxes(query_low, 0, 1), jnp.swapaxes(key_low, 0, 1), jnp.swapaxes(value_low, 0, 1)))
    context = jnp.swapaxes(context, 0, 1).reshape(length, HEADS * HD)
    middle = tokens_in + low_back(product(context, out_low))
    normed_two = low(layer_norm(middle, gain_pair[1], shift_pair[1]))
    gate_proj = low_back(product(normed_two, gate_up_low[0]))
    up_proj = low_back(product(normed_two, gate_up_low[1]))
    hidden_low = low(jax.nn.silu(gate_proj) * up_proj)
    return middle + low_back(product(hidden_low, down_low))

def layer_forward(weights, tokens_all, segments):
    rounded = (low(weights[0]), low(weights[1]), low(weights[2]), low(weights[3]), weights[4], weights[5], weights[6])
    return lax.map(lambda pair: sequence_forward(rounded, pair[0], pair[1]), (tokens_all, segments))

def adam_update(master, gradient, moment_one, moment_two, correct_one, correct_two, rate):
    one_new = 0.9 * moment_one + 0.1 * gradient
    two_new = 0.999 * moment_two + 0.001 * gradient * gradient
    change = one_new / correct_one / (jnp.sqrt(two_new / correct_two) + 1e-08) + 0.1 * master
    return (master - rate * change, one_new, two_new)

def reference(inputs, out_grad, segments, w_qkv, w_out, w_gate_up, w_down, qkv_bias, norm_gain, norm_bias, first_qkv, first_out, first_gate_up, first_down, first_bias, first_gain, first_shift, second_qkv, second_out, second_gate_up, second_down, second_bias, second_gain, second_shift):
    tokens_all = inputs.astype(jnp.float32).reshape(NSEQ, SEQ_LEN, D)
    weights = (w_qkv, w_out, w_gate_up, w_down, qkv_bias, norm_gain, norm_bias)
    result, pullback = jax.vjp(lambda params, tokens: layer_forward(params, tokens, segments), weights, tokens_all)
    grads, tokens_grad = pullback(out_grad.astype(jnp.float32).reshape(NSEQ, SEQ_LEN, D))
    correct_one = 1.0 - 0.9 ** STEP
    correct_two = 1.0 - 0.999 ** STEP
    rates = (0.02, 0.3, 0.02, 0.02, 0.3, 0.3, 0.3)
    firsts = (first_qkv, first_out, first_gate_up, first_down, first_bias, first_gain, first_shift)
    seconds = (second_qkv, second_out, second_gate_up, second_down, second_bias, second_gain, second_shift)
    updated = [adam_update(weights[number], grads[number], firsts[number], seconds[number], correct_one, correct_two, rates[number]) for number in range(7)]
    outputs = result.reshape(TOKENS, D).astype(jnp.bfloat16)
    input_grad = tokens_grad.reshape(TOKENS, D).astype(jnp.bfloat16)
    return (outputs, input_grad, grads[0], grads[1], grads[2], grads[3], grads[4], grads[5], grads[6], updated[0][0], updated[1][0], updated[2][0], updated[3][0], updated[4][0], updated[5][0], updated[6][0], updated[0][1], updated[1][1], updated[2][1], updated[3][1], updated[4][1], updated[5][1], updated[6][1], updated[0][2], updated[1][2], updated[2][2], updated[3][2], updated[4][2], updated[5][2], updated[6][2])
```

```python
import jax
import jax.numpy as jnp
from jax import lax
from jax.experimental import pallas as pl
from jax.experimental.pallas import tpu as pltpu
from jax.sharding import PartitionSpec as P

HD = 64
ROT = 16
STEP = 10


def layer_norm_parts(values, gain_row, shift_row):
    average = jnp.mean(values, axis=-1, keepdims=True)
    centred = values - average
    inverse = lax.rsqrt(jnp.mean(centred * centred, axis=-1, keepdims=True) + 1e-05)
    normed = centred * inverse
    return (normed * gain_row + shift_row, normed, inverse)


def layer_norm_back(incoming, normed, inverse, gain_row):
    scaled = incoming * gain_row
    inner = (
        scaled
        - jnp.mean(scaled, axis=-1, keepdims=True)
        - normed * jnp.mean(scaled * normed, axis=-1, keepdims=True)
    )
    return (inner * inverse, jnp.sum(incoming * normed, axis=0), jnp.sum(incoming, axis=0))


def positions(segment_ids):
    length = segment_ids.shape[-1]
    indices = jnp.broadcast_to(jnp.arange(length, dtype=jnp.int32), segment_ids.shape)
    before = jnp.concatenate(
        [jnp.full(segment_ids.shape[:-1] + (1,), -1, jnp.int32), segment_ids[..., :-1]], axis=-1
    )
    starts = lax.cummax(jnp.where(segment_ids != before, indices, 0), axis=segment_ids.ndim - 1)
    return indices - starts


def rotary_tables(position_ids, width):
    half_rot = ROT // 2
    frequency = 10000.0 ** (-(2.0 * jnp.arange(half_rot, dtype=jnp.float32)) / ROT)
    angles = position_ids.astype(jnp.float32)[:, None] * frequency
    cosine, sine = jnp.cos(angles), jnp.sin(angles)
    zeros = jnp.zeros((angles.shape[0], HD - ROT), jnp.float32)
    blank = jnp.zeros_like(sine)
    copies = width // HD
    return tuple(
        jnp.tile(jnp.concatenate(parts, axis=1), (1, copies))
        for parts in (
            (cosine, cosine, zeros + 1.0),
            (-sine, blank, zeros),
            (blank, sine, zeros),
        )
    )


def rope_whole(values, tables):
    cosine, sine_low, sine_high = tables
    ahead = jnp.roll(values, -(ROT // 2), axis=1)
    behind = jnp.roll(values, ROT // 2, axis=1)
    return values * cosine + ahead * sine_low + behind * sine_high


NEG = -1e30
BLK = 256
NT = (((1,), (1,)), ((), ()))
NN = (((1,), (0,)), ((), ()))


def dot(left, right, dims=NN, precision=None):
    return lax.dot_general(
        left, right, dims, preferred_element_type=jnp.float32, precision=precision
    )


def head_masks(width, dtype):
    lane = lax.broadcasted_iota(jnp.int32, (1, width), 1)
    return [(lane // HD == h).astype(dtype) for h in range(width // HD)]


def rope_tile(tile, cosine, sine_low, sine_high, sign):
    width = tile.shape[-1]
    ahead = pltpu.roll(tile, width - ROT // 2, 1)
    behind = pltpu.roll(tile, ROT // 2, 1)
    return tile * cosine + sign * (ahead * sine_low + behind * sine_high)


def forward_kernel(low_ref, q_ref, k_ref, v_ref, start_ref, ctx_ref, lse_ref, v_turned, acc, stats):
    block = pl.program_id(0)
    length, width = k_ref.shape
    heads = width // HD

    @pl.when(block == 0)
    def _():
        for part in range(length // BLK):
            rows = slice(part * BLK, (part + 1) * BLK)
            v_turned[:, rows] = v_ref[rows, :].T

    queries = q_ref[pl.ds(pl.multiple_of(block * BLK, BLK), BLK), :] * 0.125
    queries = queries.astype(jnp.bfloat16)
    masked = [queries * m for m in head_masks(width, jnp.bfloat16)]
    start = start_ref[...]
    query_ids = block * BLK + lax.broadcasted_iota(jnp.int32, (1, BLK), 1)
    acc[...] = jnp.zeros_like(acc)
    stats[0:8, :] = jnp.full((8, BLK), NEG, jnp.float32)
    stats[8:16, :] = jnp.zeros((8, BLK), jnp.float32)

    def step(number, _):
        base = pl.multiple_of(number * BLK, BLK)
        keys = k_ref[pl.ds(base, BLK), :]
        key_ids = base + lax.broadcasted_iota(jnp.int32, (BLK, BLK), 0)
        visible = (key_ids >= start) & (key_ids <= query_ids)
        for h in range(heads):
            scores = jnp.where(visible, dot(keys, masked[h], NT), NEG)
            peak_old = stats[h : h + 1, :]
            peak = jnp.maximum(peak_old, jnp.max(scores, axis=0, keepdims=True))
            fade = jnp.exp(peak_old - peak)
            prob = jnp.exp(scores - peak)
            stats[h : h + 1, :] = peak
            stats[8 + h : 9 + h, :] = stats[8 + h : 9 + h, :] * fade + jnp.sum(
                prob, axis=0, keepdims=True
            )
            rows = slice(h * HD, (h + 1) * HD)
            acc[rows, :] = acc[rows, :] * fade + dot(
                v_turned[rows, pl.ds(base, BLK)], prob.astype(jnp.bfloat16)
            )
        return 0

    lax.fori_loop(low_ref[block], block + 1, step, 0)
    for h in range(heads):
        rows = slice(h * HD, (h + 1) * HD)
        acc[rows, :] = acc[rows, :] / stats[8 + h : 9 + h, :]
    ctx_ref[...] = acc[...].T.astype(ctx_ref.dtype)
    total = jnp.where(stats[8:16, :] > 0, stats[8:16, :], 1.0)
    lse_ref[...] = stats[0:8, :] + jnp.log(total)


def attention_forward(low_blocks, queries, keys, values, start):
    length, width = queries.shape
    whole = pl.BlockSpec((length, width), lambda i, low: (0, 0))
    return pl.pallas_call(
        forward_kernel,
        grid_spec=pltpu.PrefetchScalarGridSpec(
            num_scalar_prefetch=1,
            grid=(length // BLK,),
            in_specs=[whole, whole, whole, pl.BlockSpec((1, BLK), lambda i, low: (0, i))],
            out_specs=[
                pl.BlockSpec((BLK, width), lambda i, low: (i, 0)),
                pl.BlockSpec((8, BLK), lambda i, low: (0, i)),
            ],
            scratch_shapes=[
                pltpu.VMEM((width, length), jnp.bfloat16),
                pltpu.VMEM((width, BLK), jnp.float32),
                pltpu.VMEM((16, BLK), jnp.float32),
            ],
        ),
        out_shape=[
            jax.ShapeDtypeStruct((length, width), jnp.bfloat16),
            jax.ShapeDtypeStruct((8, length), jnp.float32),
        ],
        compiler_params=pltpu.CompilerParams(vmem_limit_bytes=32 << 20),
        name="attention_forward",
    )(low_blocks, queries, keys, values, start)


def backward_kernel(
    low_ref,
    q_ref,
    k_ref,
    v_ref,
    start_ref,
    lse_ref,
    ctx_ref,
    grad_ref,
    cos_ref,
    sin_low_ref,
    sin_high_ref,
    dq_ref,
    dk_ref,
    dv_ref,
    bias_ref,
    k_turned,
    dq_acc,
    dk_acc,
    dv_acc,
):
    block = pl.program_id(0)
    last = pl.num_programs(0) - 1
    length, width = k_ref.shape
    heads = width // HD
    tile = min(width, 128)

    @pl.when(block == 0)
    def _():
        for part in range(length // BLK):
            rows = slice(part * BLK, (part + 1) * BLK)
            k_turned[:, rows] = k_ref[rows, :].T
        dk_acc[...] = jnp.zeros_like(dk_acc)
        dv_acc[...] = jnp.zeros_like(dv_acc)
        bias_ref[...] = jnp.zeros_like(bias_ref)

    here = pl.ds(pl.multiple_of(block * BLK, BLK), BLK)
    masks = head_masks(width, jnp.bfloat16)
    queries = (q_ref[here, :] * 0.125).astype(jnp.bfloat16)
    masked = [queries * m for m in masks]
    grads = grad_ref[...]
    grads_masked = [grads * m for m in masks]
    product = grads.astype(jnp.float32) * ctx_ref[...].astype(jnp.float32)
    select = (
        lax.broadcasted_iota(jnp.int32, (8, width), 1) // HD
        == lax.broadcasted_iota(jnp.int32, (8, width), 0)
    ).astype(jnp.float32)
    delta = dot(select, product, NT, lax.Precision.HIGHEST)
    start = start_ref[...]
    query_ids = block * BLK + lax.broadcasted_iota(jnp.int32, (1, BLK), 1)
    dq_acc[...] = jnp.zeros_like(dq_acc)

    def step(number, _):
        base = pl.multiple_of(number * BLK, BLK)
        rows_k = pl.ds(base, BLK)
        keys = k_ref[rows_k, :]
        vals = v_ref[rows_k, :]
        key_ids = base + lax.broadcasted_iota(jnp.int32, (BLK, BLK), 0)
        visible = (key_ids >= start) & (key_ids <= query_ids)
        dk = dk_acc[rows_k, :]
        dv = dv_acc[rows_k, :]
        for h in range(heads):
            scores = dot(keys, masked[h], NT)
            prob = jnp.where(visible, jnp.exp(scores - lse_ref[h : h + 1, :]), 0.0)
            dprob = dot(vals, grads_masked[h], NT)
            dscore = (prob * (dprob - delta[h : h + 1, :])).astype(jnp.bfloat16)
            dv = dv + dot(prob.astype(jnp.bfloat16), grads_masked[h])
            dk = dk + dot(dscore, masked[h])
            rows = slice(h * HD, (h + 1) * HD)
            dq_acc[rows, :] += dot(k_turned[rows, rows_k], dscore)
        dk_acc[rows_k, :] = dk
        dv_acc[rows_k, :] = dv
        return 0

    lax.fori_loop(low_ref[block], block + 1, step, 0)

    def turn_back(values, rows):
        parts = []
        for t in range(width // tile):
            parts.append(
                rope_tile(
                    values[:, t * tile : (t + 1) * tile],
                    cos_ref[rows, :],
                    sin_low_ref[rows, :],
                    sin_high_ref[rows, :],
                    -1.0,
                )
            )
        return jnp.concatenate(parts, axis=1) if len(parts) > 1 else parts[0]

    dq = turn_back(dq_acc[...].T * 0.125, here).astype(jnp.bfloat16)
    dq_ref[...] = dq
    bias_ref[0:1, :] += jnp.sum(dq.astype(jnp.float32), axis=0, keepdims=True)

    @pl.when(block == last)
    def _():
        def finish(part, _):
            rows = pl.ds(pl.multiple_of(part * BLK, BLK), BLK)
            dk = turn_back(dk_acc[rows, :], rows).astype(jnp.bfloat16)
            dv = dv_acc[rows, :].astype(jnp.bfloat16)
            dk_ref[rows, :] = dk
            dv_ref[rows, :] = dv
            bias_ref[1:2, :] += jnp.sum(dk.astype(jnp.float32), axis=0, keepdims=True)
            bias_ref[2:3, :] += jnp.sum(dv.astype(jnp.float32), axis=0, keepdims=True)
            return 0

        lax.fori_loop(0, length // BLK, finish, 0)


def attention_backward(low_blocks, queries, keys, values, start, lse, context, grads, tables):
    length, width = queries.shape
    whole = pl.BlockSpec((length, width), lambda i, low: (0, 0))
    rows = pl.BlockSpec((BLK, width), lambda i, low: (i, 0))
    table = pl.BlockSpec(tables[0].shape, lambda i, low: (0, 0))
    return pl.pallas_call(
        backward_kernel,
        grid_spec=pltpu.PrefetchScalarGridSpec(
            num_scalar_prefetch=1,
            grid=(length // BLK,),
            in_specs=[
                whole,
                whole,
                whole,
                pl.BlockSpec((1, BLK), lambda i, low: (0, i)),
                pl.BlockSpec((8, BLK), lambda i, low: (0, i)),
                rows,
                rows,
                table,
                table,
                table,
            ],
            out_specs=[rows, whole, whole, pl.BlockSpec((8, width), lambda i, low: (0, 0))],
            scratch_shapes=[
                pltpu.VMEM((width, length), jnp.bfloat16),
                pltpu.VMEM((width, BLK), jnp.float32),
                pltpu.VMEM((length, width), jnp.float32),
                pltpu.VMEM((length, width), jnp.float32),
            ],
        ),
        out_shape=[jax.ShapeDtypeStruct((length, width), jnp.bfloat16)] * 3
        + [jax.ShapeDtypeStruct((8, width), jnp.float32)],
        compiler_params=pltpu.CompilerParams(vmem_limit_bytes=40 << 20),
        name="attention_backward",
    )(low_blocks, queries, keys, values, start, lse, context, grads, *tables)


def adam_update(master, gradient, moment_one, moment_two, correct_one, correct_two, rate):
    one_new = 0.9 * moment_one + 0.1 * gradient
    two_new = 0.999 * moment_two + 0.001 * gradient * gradient
    change = one_new / correct_one / (jnp.sqrt(two_new / correct_two) + 1e-08) + 0.1 * master
    return (master - rate * change, one_new, two_new)


def per_device(
    inputs,
    out_grad,
    segments,
    w_qkv,
    w_out,
    w_gate_up,
    w_down,
    qkv_bias,
    norm_gain,
    norm_bias,
    first_qkv,
    first_out,
    first_gate_up,
    first_down,
    first_bias,
    first_gain,
    first_shift,
    second_qkv,
    second_out,
    second_gate_up,
    second_down,
    second_bias,
    second_gain,
    second_shift,
):
    low_type = jnp.bfloat16
    full_type = jnp.float32
    qkv_all, gate_up_all, out_all, down_all = (
        lax.all_gather(w_qkv.astype(low_type), "dp", axis=1, tiled=True),
        lax.all_gather(w_gate_up.astype(low_type), "dp", axis=1, tiled=True),
        lax.all_gather(w_out.astype(low_type), "dp", axis=1, tiled=True),
        lax.all_gather(w_down.astype(low_type), "dp", axis=1, tiled=True),
    )
    length = segments.shape[1]
    head_width = w_qkv.shape[2]
    inputs_full = inputs.astype(full_type)
    normed_one, plain_one, inverse_one = layer_norm_parts(inputs_full, norm_gain[0], norm_bias[0])
    normed_one = normed_one.astype(low_type)
    normed_all = lax.all_gather(normed_one, "tensor", axis=0, tiled=True)
    projected = jnp.einsum("rd,cdh->crh", normed_all, qkv_all, preferred_element_type=full_type)
    place = positions(segments)[0]
    start = jnp.arange(length, dtype=jnp.int32) - place
    low_blocks = start[::BLK] // BLK
    start = start[None, :]
    tables = rotary_tables(place, head_width)
    half_tables = tuple(t[:, : min(head_width, 128)] for t in tables)
    query_low = rope_whole(projected[0] + qkv_bias[0], tables).astype(low_type)
    key_low = rope_whole(projected[1] + qkv_bias[1], tables).astype(low_type)
    value_low = (projected[2] + qkv_bias[2]).astype(low_type)
    context_flat, lse = attention_forward(low_blocks, query_low, key_low, value_low, start)
    middle = inputs_full + lax.psum_scatter(
        jnp.dot(context_flat, out_all, preferred_element_type=full_type).astype(low_type),
        "tensor",
        scatter_dimension=0,
        tiled=True,
    ).astype(full_type)
    normed_two, plain_two, inverse_two = layer_norm_parts(middle, norm_gain[1], norm_bias[1])
    normed_two = normed_two.astype(low_type)
    gate_pair = jnp.einsum(
        "rd,cdf->rcf",
        lax.all_gather(normed_two, "tensor", axis=0, tiled=True),
        gate_up_all,
        preferred_element_type=full_type,
    )
    gate_parts = (gate_pair,)
    gate_proj = gate_parts[0][:, 0]
    up_proj = gate_parts[0][:, 1]
    sigmoid_gate = jax.nn.sigmoid(gate_proj)
    activated = gate_proj * sigmoid_gate
    hidden_low = (activated * up_proj).astype(low_type)
    outputs = (
        middle
        + lax.psum_scatter(
            jnp.dot(hidden_low, down_all, preferred_element_type=full_type).astype(jnp.bfloat16),
            "tensor",
            scatter_dimension=0,
            tiled=True,
        ).astype(jnp.float32)
    ).astype(low_type)
    mlp_grad = lax.all_gather(out_grad, "tensor", axis=0, tiled=True)
    grad_down = jnp.einsum("rf,rd->fd", hidden_low, mlp_grad, preferred_element_type=full_type)
    hidden_grad = jnp.einsum("rd,fd->rf", mlp_grad, down_all, preferred_element_type=full_type)
    gate_grad = hidden_grad * up_proj * (sigmoid_gate * (1.0 + gate_proj * (1.0 - sigmoid_gate)))
    up_grad = hidden_grad * activated
    pair_grad = jnp.stack([gate_grad, up_grad], axis=1).astype(low_type)
    normed_two_grad = lax.psum_scatter(
        jnp.einsum("rcf,cdf->rd", pair_grad, gate_up_all, preferred_element_type=full_type).astype(
            low_type
        ),
        "tensor",
        scatter_dimension=0,
        tiled=True,
    ).astype(full_type)
    rows_grad = pair_grad
    grad_gate_up = jnp.einsum(
        "rd,rcf->cdf",
        lax.all_gather(normed_two, "tensor", axis=0, tiled=True),
        rows_grad,
        preferred_element_type=full_type,
    )
    middle_ln_grad, gain_two_grad, shift_two_grad = layer_norm_back(
        normed_two_grad, plain_two, inverse_two, norm_gain[1]
    )
    middle_grad = out_grad.astype(full_type) + middle_ln_grad
    attn_grad_all = lax.all_gather(middle_grad.astype(low_type), "tensor", axis=0, tiled=True)
    grad_out = jnp.einsum(
        "rh,rd->hd", context_flat, attn_grad_all, preferred_element_type=full_type
    )
    context_grad = jnp.einsum(
        "rd,hd->rh", attn_grad_all, out_all, preferred_element_type=full_type
    ).astype(low_type)
    query_grad, key_grad, value_grad, bias_sums = attention_backward(
        low_blocks,
        query_low,
        key_low,
        value_low,
        start,
        lse,
        context_flat,
        context_grad,
        half_tables,
    )
    triple_grad = jnp.stack([query_grad, key_grad, value_grad], axis=1)
    grad_bias = bias_sums[:3]
    normed_one_grad = lax.psum_scatter(
        jnp.einsum("rch,cdh->rd", triple_grad, qkv_all, preferred_element_type=full_type).astype(
            jnp.bfloat16
        ),
        "tensor",
        scatter_dimension=0,
        tiled=True,
    ).astype(jnp.float32)
    rows_grad = triple_grad
    grad_qkv = jnp.einsum(
        "rd,rch->cdh",
        lax.all_gather(normed_one, "tensor", axis=0, tiled=True),
        rows_grad,
        preferred_element_type=full_type,
    )
    input_ln_grad, gain_one_grad, shift_one_grad = layer_norm_back(
        normed_one_grad, plain_one, inverse_one, norm_gain[0]
    )
    input_grad = (middle_grad + input_ln_grad).astype(low_type)
    grad_qkv, grad_gate_up, grad_out, grad_down = (
        lax.psum_scatter(
            grad_qkv.astype(jnp.bfloat16), "dp", scatter_dimension=1, tiled=True
        ).astype(jnp.float32),
        lax.psum_scatter(
            grad_gate_up.astype(jnp.bfloat16), "dp", scatter_dimension=1, tiled=True
        ).astype(jnp.float32),
        lax.psum_scatter(
            grad_out.astype(jnp.bfloat16), "dp", scatter_dimension=1, tiled=True
        ).astype(jnp.float32),
        lax.psum_scatter(
            grad_down.astype(jnp.bfloat16), "dp", scatter_dimension=1, tiled=True
        ).astype(jnp.float32),
    )
    grad_bias = lax.psum(grad_bias, "dp")
    grad_gain, grad_shift = lax.psum(
        (jnp.stack([gain_one_grad, gain_two_grad]), jnp.stack([shift_one_grad, shift_two_grad])),
        ("dp", "tensor"),
    )
    correct_one = 1.0 - 0.9**STEP
    correct_two = 1.0 - 0.999**STEP
    rates = (0.02, 0.3, 0.02, 0.02, 0.3, 0.3, 0.3)
    masters = (w_qkv, w_out, w_gate_up, w_down, qkv_bias, norm_gain, norm_bias)
    gradients = (grad_qkv, grad_out, grad_gate_up, grad_down, grad_bias, grad_gain, grad_shift)
    firsts = (first_qkv, first_out, first_gate_up, first_down, first_bias, first_gain, first_shift)
    seconds = (
        second_qkv,
        second_out,
        second_gate_up,
        second_down,
        second_bias,
        second_gain,
        second_shift,
    )
    updated = [
        adam_update(
            masters[number],
            gradients[number],
            firsts[number],
            seconds[number],
            correct_one,
            correct_two,
            rates[number],
        )
        for number in range(7)
    ]
    return (
        outputs,
        input_grad,
        grad_qkv,
        grad_out,
        grad_gate_up,
        grad_down,
        grad_bias,
        grad_gain,
        grad_shift,
        updated[0][0],
        updated[1][0],
        updated[2][0],
        updated[3][0],
        updated[4][0],
        updated[5][0],
        updated[6][0],
        updated[0][1],
        updated[1][1],
        updated[2][1],
        updated[3][1],
        updated[4][1],
        updated[5][1],
        updated[6][1],
        updated[0][2],
        updated[1][2],
        updated[2][2],
        updated[3][2],
        updated[4][2],
        updated[5][2],
        updated[6][2],
    )


def solution(mesh):
    in_specs = (
        P(("dp", "tensor"), None),
        P(("dp", "tensor"), None),
        P("dp", None),
        P(None, "dp", "tensor"),
        P("tensor", "dp"),
        P(None, "dp", "tensor"),
        P("tensor", "dp"),
        P(None, "tensor"),
        P(),
        P(),
        P(None, "dp", "tensor"),
        P("tensor", "dp"),
        P(None, "dp", "tensor"),
        P("tensor", "dp"),
        P(None, "tensor"),
        P(),
        P(),
        P(None, "dp", "tensor"),
        P("tensor", "dp"),
        P(None, "dp", "tensor"),
        P("tensor", "dp"),
        P(None, "tensor"),
        P(),
        P(),
    )
    out_specs = (
        P(("dp", "tensor"), None),
        P(("dp", "tensor"), None),
        P(None, "dp", "tensor"),
        P("tensor", "dp"),
        P(None, "dp", "tensor"),
        P("tensor", "dp"),
        P(None, "tensor"),
        P(),
        P(),
        P(None, "dp", "tensor"),
        P("tensor", "dp"),
        P(None, "dp", "tensor"),
        P("tensor", "dp"),
        P(None, "tensor"),
        P(),
        P(),
        P(None, "dp", "tensor"),
        P("tensor", "dp"),
        P(None, "dp", "tensor"),
        P("tensor", "dp"),
        P(None, "tensor"),
        P(),
        P(),
        P(None, "dp", "tensor"),
        P("tensor", "dp"),
        P(None, "dp", "tensor"),
        P("tensor", "dp"),
        P(None, "tensor"),
        P(),
        P(),
    )
    return jax.shard_map(
        per_device, mesh=mesh, in_specs=in_specs, out_specs=out_specs, check_vma=False
    )
```

```python
import functools

import jax
import jax.numpy as jnp
from jax import lax
from jax.experimental import pallas as pl
from jax.experimental.pallas import tpu as pltpu
from jax.sharding import PartitionSpec as P

HD = 64
ROT = 16
STEP = 10


def layer_norm_parts(values, gain_row, shift_row):
    average = jnp.mean(values, axis=-1, keepdims=True)
    centred = values - average
    inverse = lax.rsqrt(jnp.mean(centred * centred, axis=-1, keepdims=True) + 1e-05)
    normed = centred * inverse
    return (normed * gain_row + shift_row, normed, inverse)


def layer_norm_back(incoming, normed, inverse, gain_row):
    scaled = incoming * gain_row
    inner = (
        scaled
        - jnp.mean(scaled, axis=-1, keepdims=True)
        - normed * jnp.mean(scaled * normed, axis=-1, keepdims=True)
    )
    return (inner * inverse, jnp.sum(incoming * normed, axis=0), jnp.sum(incoming, axis=0))


def positions(segment_ids):
    length = segment_ids.shape[-1]
    indices = jnp.broadcast_to(jnp.arange(length, dtype=jnp.int32), segment_ids.shape)
    before = jnp.concatenate(
        [jnp.full(segment_ids.shape[:-1] + (1,), -1, jnp.int32), segment_ids[..., :-1]], axis=-1
    )
    starts = lax.cummax(jnp.where(segment_ids != before, indices, 0), axis=segment_ids.ndim - 1)
    return indices - starts


def rotary_tables(position_ids, width):
    half_rot = ROT // 2
    frequency = 10000.0 ** (-(2.0 * jnp.arange(half_rot, dtype=jnp.float32)) / ROT)
    angles = position_ids.astype(jnp.float32)[:, None] * frequency
    cosine, sine = jnp.cos(angles), jnp.sin(angles)
    zeros = jnp.zeros((angles.shape[0], HD - ROT), jnp.float32)
    blank = jnp.zeros_like(sine)
    copies = width // HD
    return tuple(
        jnp.tile(jnp.concatenate(parts, axis=1), (1, copies))
        for parts in (
            (cosine, cosine, zeros + 1.0),
            (-sine, blank, zeros),
            (blank, sine, zeros),
        )
    )


NEG = -1e30
BLK = 256
NT = (((1,), (1,)), ((), ()))
NN = (((1,), (0,)), ((), ()))


def dot(left, right, dims=NN, precision=None):
    return lax.dot_general(
        left, right, dims, preferred_element_type=jnp.float32, precision=precision
    )


def head_masks(width, dtype):
    lane = lax.broadcasted_iota(jnp.int32, (1, width), 1)
    return [(lane // HD == h).astype(dtype) for h in range(width // HD)]


def rope_tile(tile, cosine, sine_low, sine_high, sign):
    width = tile.shape[-1]
    ahead = pltpu.roll(tile, width - ROT // 2, 1)
    behind = pltpu.roll(tile, ROT // 2, 1)
    return tile * cosine + sign * (ahead * sine_low + behind * sine_high)


def attend(number, size, k_ref, v_turned, masked, starts, query_ids, acc, stats):
    base = pl.multiple_of(number * size, size)
    keys = k_ref[pl.ds(base, size), :]
    key_ids = base + lax.broadcasted_iota(jnp.int32, (size, size), 0)
    visible = (key_ids >= starts) & (key_ids <= query_ids)
    for h, queries in enumerate(masked):
        scores = jnp.where(visible, dot(keys, queries, NT), NEG)
        peak_old = stats[h : h + 1, :]
        peak = jnp.maximum(peak_old, jnp.max(scores, axis=0, keepdims=True))
        fade = jnp.exp(peak_old - peak)
        prob = jnp.exp(scores - peak)
        stats[h : h + 1, :] = peak
        stats[8 + h : 9 + h, :] = stats[8 + h : 9 + h, :] * fade + jnp.sum(
            prob, axis=0, keepdims=True
        )
        band = slice(h * HD, (h + 1) * HD)
        acc[band, :] = acc[band, :] * fade + dot(
            v_turned[band, pl.ds(base, size)], prob.astype(jnp.bfloat16)
        )


def backward_kernel(
    low_ref,
    q_ref,
    k_ref,
    v_ref,
    start_ref,
    lse_ref,
    ctx_ref,
    grad_ref,
    cos_ref,
    sin_low_ref,
    sin_high_ref,
    dq_ref,
    dk_ref,
    dv_ref,
    bias_ref,
    k_turned,
    dq_acc,
    dk_acc,
    dv_acc,
):
    block = pl.program_id(0)
    last = pl.num_programs(0) - 1
    length, width = k_ref.shape
    heads = width // HD
    tile = min(width, 128)

    @pl.when(block == 0)
    def _():
        for part in range(length // BLK):
            rows = slice(part * BLK, (part + 1) * BLK)
            k_turned[:, rows] = k_ref[rows, :].T
        dk_acc[...] = jnp.zeros_like(dk_acc)
        dv_acc[...] = jnp.zeros_like(dv_acc)
        bias_ref[...] = jnp.zeros_like(bias_ref)

    here = pl.ds(pl.multiple_of(block * BLK, BLK), BLK)
    masks = head_masks(width, jnp.bfloat16)
    queries = (q_ref[here, :] * 0.125).astype(jnp.bfloat16)
    masked = [queries * m for m in masks]
    grads = grad_ref[...]
    grads_masked = [grads * m for m in masks]
    product = grads.astype(jnp.float32) * ctx_ref[...].astype(jnp.float32)
    select = (
        lax.broadcasted_iota(jnp.int32, (8, width), 1) // HD
        == lax.broadcasted_iota(jnp.int32, (8, width), 0)
    ).astype(jnp.float32)
    delta = dot(select, product, NT, lax.Precision.HIGHEST)
    start = start_ref[...]
    query_ids = block * BLK + lax.broadcasted_iota(jnp.int32, (1, BLK), 1)
    dq_acc[...] = jnp.zeros_like(dq_acc)

    def step(number, _):
        base = pl.multiple_of(number * BLK, BLK)
        rows_k = pl.ds(base, BLK)
        keys = k_ref[rows_k, :]
        vals = v_ref[rows_k, :]
        key_ids = base + lax.broadcasted_iota(jnp.int32, (BLK, BLK), 0)
        visible = (key_ids >= start) & (key_ids <= query_ids)
        dk = dk_acc[rows_k, :]
        dv = dv_acc[rows_k, :]
        for h in range(heads):
            scores = dot(keys, masked[h], NT)
            prob = jnp.where(visible, jnp.exp(scores - lse_ref[h : h + 1, :]), 0.0)
            dprob = dot(vals, grads_masked[h], NT)
            dscore = (prob * (dprob - delta[h : h + 1, :])).astype(jnp.bfloat16)
            dv = dv + dot(prob.astype(jnp.bfloat16), grads_masked[h])
            dk = dk + dot(dscore, masked[h])
            rows = slice(h * HD, (h + 1) * HD)
            dq_acc[rows, :] += dot(k_turned[rows, rows_k], dscore)
        dk_acc[rows_k, :] = dk
        dv_acc[rows_k, :] = dv
        return 0

    lax.fori_loop(low_ref[block], block + 1, step, 0)

    def turn_back(values, rows):
        parts = []
        for t in range(width // tile):
            parts.append(
                rope_tile(
                    values[:, t * tile : (t + 1) * tile],
                    cos_ref[rows, :],
                    sin_low_ref[rows, :],
                    sin_high_ref[rows, :],
                    -1.0,
                )
            )
        return jnp.concatenate(parts, axis=1) if len(parts) > 1 else parts[0]

    dq = turn_back(dq_acc[...].T * 0.125, here).astype(jnp.bfloat16)
    dq_ref[...] = dq
    bias_ref[0:1, :] += jnp.sum(dq.astype(jnp.float32), axis=0, keepdims=True)

    @pl.when(block == last)
    def _():
        def finish(part, _):
            rows = pl.ds(pl.multiple_of(part * BLK, BLK), BLK)
            dk = turn_back(dk_acc[rows, :], rows).astype(jnp.bfloat16)
            dv = dv_acc[rows, :].astype(jnp.bfloat16)
            dk_ref[rows, :] = dk
            dv_ref[rows, :] = dv
            bias_ref[1:2, :] += jnp.sum(dk.astype(jnp.float32), axis=0, keepdims=True)
            bias_ref[2:3, :] += jnp.sum(dv.astype(jnp.float32), axis=0, keepdims=True)
            return 0

        lax.fori_loop(0, length // BLK, finish, 0)


def attention_backward(low_blocks, queries, keys, values, start, lse, context, grads, tables):
    length, width = queries.shape
    whole = pl.BlockSpec((length, width), lambda i, low: (0, 0))
    rows = pl.BlockSpec((BLK, width), lambda i, low: (i, 0))
    table = pl.BlockSpec(tables[0].shape, lambda i, low: (0, 0))
    return pl.pallas_call(
        backward_kernel,
        grid_spec=pltpu.PrefetchScalarGridSpec(
            num_scalar_prefetch=1,
            grid=(length // BLK,),
            in_specs=[
                whole,
                whole,
                whole,
                pl.BlockSpec((1, BLK), lambda i, low: (0, i)),
                pl.BlockSpec((8, BLK), lambda i, low: (0, i)),
                rows,
                rows,
                table,
                table,
                table,
            ],
            out_specs=[rows, whole, whole, pl.BlockSpec((8, width), lambda i, low: (0, 0))],
            scratch_shapes=[
                pltpu.VMEM((width, length), jnp.bfloat16),
                pltpu.VMEM((width, BLK), jnp.float32),
                pltpu.VMEM((length, width), jnp.float32),
                pltpu.VMEM((length, width), jnp.float32),
            ],
        ),
        out_shape=[jax.ShapeDtypeStruct((length, width), jnp.bfloat16)] * 3
        + [jax.ShapeDtypeStruct((8, width), jnp.float32)],
        compiler_params=pltpu.CompilerParams(vmem_limit_bytes=40 << 20),
        name="attention_backward",
    )(low_blocks, queries, keys, values, start, lse, context, grads, *tables)


MESH = pl.DeviceIdType.MESH
VMEM_BYTES = 62 << 20
LONGEST = 1024
TN = (((0,), (0,)), ((), ()))
LOW = jnp.bfloat16


def remote(source, target, send, receive, device):
    return pltpu.make_async_remote_copy(
        src_ref=source,
        dst_ref=target,
        send_sem=send,
        recv_sem=receive,
        device_id=device,
        device_id_type=MESH,
    )


class Place:
    def __init__(self, groups, chips):
        self.groups, self.chips = groups, chips
        self.group = lax.axis_index("dp")
        self.spot = lax.axis_index("tensor")
        self.chip, self.core = self.spot // 2, self.spot % 2

    def at(self, chip, core):
        return (self.group, chip * 2 + core)

    def peer(self, offset):
        return (lax.rem(self.group + offset, self.groups), self.spot)

    def partners(self):
        found = []
        bit = 1
        while bit < self.groups:
            found.append((self.group + bit - 2 * bit * (self.group // bit % 2), self.spot))
            bit *= 2
        bit = 1
        while bit < 2 * self.chips:
            found.append((self.group, self.spot + bit - 2 * bit * (self.spot // bit % 2)))
            bit *= 2
        return found

    def barrier(self, with_groups=False, with_partners=False):
        semaphore = pltpu.get_barrier_semaphore()

        def greet(target):
            pl.semaphore_signal(semaphore, inc=1, device_id=target, device_id_type=MESH)

        greet(self.at(self.chip, 1 - self.core))
        pl.when(self.chip > 0)(lambda: greet(self.at(self.chip - 1, self.core)))
        pl.when(self.chip < self.chips - 1)(lambda: greet(self.at(self.chip + 1, self.core)))
        count = 1 + jnp.where(self.chip > 0, 1, 0) + jnp.where(self.chip < self.chips - 1, 1, 0)
        if with_groups:
            for offset in range(1, self.groups):
                greet(self.peer(offset))
            count = count + self.groups - 1
        if with_partners:
            partners = self.partners()
            for partner in partners:
                greet(partner)
            count = count + len(partners)
        pl.semaphore_wait(semaphore, count)


class Gather:
    SEMS = 5

    def __init__(self, place, full, sems):
        self.place, self.full = place, full
        self.line_in, self.core_in, self.right_out, self.left_out, self.core_out = sems
        self.rows = full.shape[0] // (2 * place.chips)

    @classmethod
    def scratch(cls, chips):
        return [pltpu.SemaphoreType.DMA((chips,)) for _ in range(cls.SEMS)]

    def block(self, chip, core):
        base = pl.multiple_of((chip * 2 + core) * self.rows, self.rows)
        return self.full.at[pl.ds(base, self.rows), :]

    def own(self):
        return self.block(self.place.chip, self.place.core)

    def right(self, which):
        place, part = self.place, self.block(which, self.place.core)
        target = place.at(jnp.minimum(place.chip + 1, place.chips - 1), place.core)
        return remote(part, part, self.right_out.at[which], self.line_in.at[which], target)

    def left(self, which):
        place, part = self.place, self.block(which, self.place.core)
        target = place.at(jnp.maximum(place.chip - 1, 0), place.core)
        return remote(part, part, self.left_out.at[which], self.line_in.at[which], target)

    def across(self, which, core):
        place, part = self.place, self.block(which, core)
        target = place.at(place.chip, 1 - place.core)
        return remote(part, part, self.core_out.at[which], self.core_in.at[which], target)

    def begin(self):
        chip, chips = self.place.chip, self.place.chips
        pl.when(chip < chips - 1)(lambda: self.right(chip).start())
        pl.when(chip > 0)(lambda: self.left(chip).start())
        self.across(chip, self.place.core).start()

    def pass_on(self, step):
        chip, chips, core = self.place.chip, self.place.chips, self.place.core
        low, high = chip - 1 - step, chip + 1 + step

        @pl.when(low >= 0)
        def _():
            self.right(low).wait_recv()
            pl.when(chip < chips - 1)(lambda: self.right(low).start())
            self.across(low, core).start()

        @pl.when(high < chips)
        def _():
            self.left(high).wait_recv()
            pl.when(chip > 0)(lambda: self.left(high).start())
            self.across(high, core).start()

    def wait_chip(self, which):
        self.across(which, 1 - self.place.core).wait_recv()

    def each_new(self, step, use):
        low, high = self.place.chip - 1 - step, self.place.chip + 1 + step

        @pl.when(low >= 0)
        def _():
            self.wait_chip(low)
            use(low)

        @pl.when(high < self.place.chips)
        def _():
            self.wait_chip(high)
            use(high)

    def drain(self):
        chip, chips, core = self.place.chip, self.place.chips, self.place.core

        def one(which, _):
            self.across(which, core).wait_send()
            pl.when((which <= chip) & (chip < chips - 1))(lambda: self.right(which).wait_send())
            pl.when((which >= chip) & (chip > 0))(lambda: self.left(which).wait_send())
            return 0

        lax.fori_loop(0, chips, one, 0)


class Scatter:
    def __init__(self, place, work, scratch):
        self.place, self.work = place, work
        self.out, self.side, self.line = scratch[:3]
        self.core_out, self.core_in, self.line_out, self.line_in = scratch[3:]
        chip, chips = place.chip, place.chips
        self.near = jnp.minimum(chip, chips - 1 - chip)
        self.alone = chips - 1 - 2 * self.near
        self.flip = jnp.where(chip * 2 < chips, 0, 1)
        self.lag = jnp.where(self.near > 0, 1, 0)

    @staticmethod
    def scratch(chips, rows, width):
        return [
            pltpu.VMEM((chips, rows, width), LOW),
            pltpu.VMEM((chips, rows, width), LOW),
            pltpu.VMEM((chips + 1, rows, width), LOW),
            pltpu.SemaphoreType.DMA((chips,)),
            pltpu.SemaphoreType.DMA((chips,)),
            pltpu.SemaphoreType.DMA((chips,)),
            pltpu.SemaphoreType.DMA((chips + 1,)),
        ]

    SCRATCH = 7

    def order(self, turn):
        chips = self.place.chips
        later = jnp.maximum(turn - self.alone, 0)
        pair = later // 2
        far = jnp.where(turn < self.alone, chips - 1 - turn, chips - 1 - self.alone - pair)
        which = jnp.where((turn >= self.alone) & (later % 2 == 1), pair, far)
        which = jnp.where(turn == chips - 1, self.near, which)
        return jnp.where(self.flip == 1, chips - 1 - which, which)

    def across(self, which):
        place = self.place
        return remote(
            self.out.at[which],
            self.side.at[which],
            self.core_out.at[which],
            self.core_in.at[which],
            place.at(place.chip, 1 - place.core),
        )

    def right(self, which):
        place = self.place
        slot = jnp.where(which == place.chip + 1, place.chips, which)
        return remote(
            self.out.at[which],
            self.line.at[slot],
            self.line_out.at[which],
            self.line_in.at[slot],
            place.at(jnp.minimum(place.chip + 1, place.chips - 1), place.core),
        )

    def left(self, which):
        place = self.place
        return remote(
            self.out.at[which],
            self.line.at[which],
            self.line_out.at[which],
            self.line_in.at[which],
            place.at(jnp.maximum(place.chip - 1, 0), place.core),
        )

    def arrived(self, slot):
        place = self.place
        part = self.line.at[slot]
        other = place.at(place.chip, 1 - place.core)
        remote(part, part, self.line_out.at[0], self.line_in.at[slot], other).wait_recv()

    def produce(self, turn):
        which = self.order(turn)
        self.out[which] = self.work(which, 1 - self.place.core).astype(LOW)
        self.across(which).start()

    def chip_sum(self, which):
        mine = self.work(which, self.place.core)
        self.across(which).wait()
        return mine + self.side[which].astype(jnp.float32)

    def send(self, which, upstream, copy):
        total = self.chip_sum(which)

        @pl.when(upstream)
        def _():
            self.arrived(which)
            self.out[which] = (total + self.line[which].astype(jnp.float32)).astype(LOW)

        @pl.when(jnp.logical_not(upstream))
        def _():
            self.out[which] = total.astype(LOW)

        copy(which).start()

    def first(self):
        pl.when(self.lag == 1)(lambda: self.produce(0))

    def slot(self, number):
        chip, chips = self.place.chip, self.place.chips
        self.produce(number + self.lag)
        right = chips - 1 - (number - chip)
        left = number - (chips - 1 - chip)
        pl.when((number >= chip) & (right > chip))(
            lambda: self.send(right, chip > 0, self.right)
        )
        pl.when((left >= 0) & (left < chip))(
            lambda: self.send(left, chip < chips - 1, self.left)
        )

    def last(self):
        pl.when(self.lag == 0)(lambda: self.produce(self.place.chips - 1))

    def own(self, total):
        chip, chips = self.place.chip, self.place.chips
        total[...] = self.chip_sum(chip)

        @pl.when(chip > 0)
        def _():
            self.arrived(chips)
            total[...] += self.line[chips].astype(jnp.float32)

        @pl.when(chip < chips - 1)
        def _():
            self.arrived(chip)
            total[...] += self.line[chip].astype(jnp.float32)

    def drain(self):
        chip = self.place.chip

        def one(which, _):
            pl.when(which > chip)(lambda: self.right(which).wait_send())
            pl.when(which < chip)(lambda: self.left(which).wait_send())
            return 0

        lax.fori_loop(0, self.place.chips, one, 0)


class Spread:
    def __init__(self, place, shard, whole, axis, sems):
        self.place, self.whole, self.sems = place, whole, sems
        size = shard.shape[axis]
        here = pl.ds(pl.multiple_of(place.group * size, size), size)
        index = tuple(here if a == axis else slice(None) for a in range(len(shard.shape)))
        self.mine = whole.at[index]
        self.mine[...] = shard[...].astype(LOW)

    @staticmethod
    def scratch(groups):
        return [pltpu.SemaphoreType.DMA((groups,)), pltpu.SemaphoreType.DMA((groups,))]

    def copy(self, offset):
        return remote(
            self.mine,
            self.mine,
            self.sems[0].at[offset],
            self.sems[1].at[offset],
            self.place.peer(offset),
        )

    def start(self):
        for offset in range(1, self.place.groups):
            self.copy(offset).start()

    def wait(self):
        for offset in range(1, self.place.groups):
            self.copy(offset).wait()


class Exchange:
    def __init__(self, place, staged, landed, sems):
        self.place, self.staged, self.landed = place, staged, landed
        self.send, self.receive = sems

    def copy(self, offset):
        return remote(
            self.staged.at[offset],
            self.landed.at[offset],
            self.send.at[offset],
            self.receive.at[offset],
            self.place.peer(offset),
        )

    def stay(self):
        return pltpu.make_async_copy(self.staged.at[0], self.landed.at[0], self.send.at[0])

    def wait(self):
        def one(offset, _):
            self.copy(offset).wait()
            return 0

        lax.fori_loop(1, self.place.groups, one, 0)
        self.stay().wait()


def pieces(number, slots, groups, fill):
    low = 1 + number * (groups - 1) // slots
    high = 1 + (number + 1) * (groups - 1) // slots

    def one(offset, _):
        fill(offset)
        return 0

    lax.fori_loop(low, high, one, 0)


def line_call(kernel, name, number, operands, out_shape, scratch, flops, in_hbm=(), from_hbm=()):
    whole, hbm = pl.BlockSpec(memory_space=pltpu.VMEM), pl.BlockSpec(memory_space=pl.ANY)
    ins = [hbm if n in from_hbm else whole for n in range(len(operands))]
    outs = [hbm if n in in_hbm else whole for n in range(len(out_shape))]
    return pl.pallas_call(
        kernel,
        out_shape=out_shape,
        in_specs=ins,
        out_specs=outs,
        scratch_shapes=scratch,
        compiler_params=pltpu.CompilerParams(
            collective_id=number, has_side_effects=True, vmem_limit_bytes=VMEM_BYTES
        ),
        cost_estimate=pl.CostEstimate(flops=flops, bytes_accessed=0, transcendentals=0),
        name=name,
    )(*operands)


COST_FLOPS = 80_000_000_000


def shape(dims, kind=LOW):
    return jax.ShapeDtypeStruct(dims, kind)


def split_refs(refs, *counts):
    parts, at = [], 0
    for count in counts:
        parts.append(refs[at : at + count])
        at += count
    return parts


def gather_project(groups, chips, tokens, gain, shift, shards, bias, tables):
    rows, width = tokens.shape
    length = rows * 2 * chips
    qkv_shard, out_shard, gate_shard = shards
    out_width = qkv_shard.shape[2]
    hidden = gate_shard.shape[1]
    tile = tables[0].shape[1]

    def kernel(
        x_ref, gain_ref, shift_ref, qkv_ref, out_ref, gate_ref, bias_ref,
        cos_ref, sin_low_ref, sin_high_ref,
        full, weights, out_whole, gate_whole, q_ref, k_ref, v_ref, *sems
    ):
        place = Place(groups, chips)
        line, one, two, three = split_refs(sems, Gather.SEMS, 2, 2, 2)
        gather = Gather(place, full, line)
        normed, _, _ = layer_norm_parts(
            x_ref[...].astype(jnp.float32), gain_ref[...], shift_ref[...]
        )
        gather.own()[...] = normed.astype(LOW)
        spread_qkv = Spread(place, qkv_ref, weights, 1, one)
        place.barrier(True)
        gather.begin()
        spread_qkv.start()
        spread_out = Spread(place, out_ref, out_whole, 1, two)
        spread_out.start()
        spread_gate = Spread(place, gate_ref, gate_whole, 0, three)
        spread_gate.start()

        def work(chip):
            base = pl.multiple_of(chip * 2 * rows, 2 * rows)
            here = pl.ds(base, 2 * rows)
            values = full[here, :]
            for number, ref in enumerate((q_ref, k_ref, v_ref)):
                result = dot(values, weights[number]) + bias_ref[number : number + 1, :]
                if number < 2:
                    parts = [
                        rope_tile(
                            result[:, t * tile : (t + 1) * tile],
                            cos_ref[here, :],
                            sin_low_ref[here, :],
                            sin_high_ref[here, :],
                            1.0,
                        )
                        for t in range(out_width // tile)
                    ]
                    result = jnp.concatenate(parts, axis=1) if len(parts) > 1 else parts[0]
                ref[here, :] = result.astype(LOW)

        gather.pass_on(0)
        spread_qkv.wait()
        gather.wait_chip(place.chip)
        work(place.chip)

        def step(number, _):
            pl.when(number > 0)(lambda: gather.pass_on(number))
            gather.each_new(number, work)
            return 0

        lax.fori_loop(0, chips - 1, step, 0)
        gather.drain()
        spread_out.wait()
        spread_gate.wait()

    head_shape = shape((length, out_width))
    return line_call(
        kernel,
        "gather_project",
        1,
        (tokens, gain, shift, *shards, bias, *tables),
        [
            shape((length, width)),
            shape((3, width, out_width)),
            shape((out_width, width)),
            shape((width, hidden)),
            head_shape,
            head_shape,
            head_shape,
        ],
        Gather.scratch(chips) + Spread.scratch(groups) * 3,
        COST_FLOPS,
    )


def scatter_heads(groups, chips, qkv, start, weight, tokens, grads, shards):
    rows, width = tokens.shape
    queries = qkv[0]
    length, head_width = queries.shape
    heads = head_width // HD
    up_shard, down_shard = shards

    def kernel(
        q_ref, k_ref, v_ref, start_ref, w_ref, x_ref, og_ref, up_ref, down_ref,
        mid_ref, ctx_ref, lse_ref, full, up_whole, down_whole,
        v_turned, acc, stats, *rest
    ):
        place = Place(groups, chips)
        for part in range(length // BLK):
            here = slice(part * BLK, (part + 1) * BLK)
            v_turned[:, here] = v_ref[here, :].T
        scratch, line, one, two = split_refs(rest, Scatter.SCRATCH, Gather.SEMS, 2, 2)
        gather = Gather(place, full, line)
        gather.own()[...] = og_ref[...]
        spread_up = Spread(place, up_ref, up_whole, 0, one)
        spread_down = Spread(place, down_ref, down_whole, 1, two)
        place.barrier(True)
        gather.begin()
        spread_up.start()
        spread_down.start()
        masks = head_masks(head_width, LOW)

        def work(chip, core):
            block = chip * 2 + core
            base = pl.multiple_of(block * rows, rows)
            here = pl.ds(base, rows)
            values = (q_ref[here, :] * 0.125).astype(LOW)
            masked = [values * m for m in masks]
            starts = start_ref[:, here]
            query_ids = base + lax.broadcasted_iota(jnp.int32, (1, rows), 1)
            acc[...] = jnp.zeros_like(acc)
            stats[0:8, :] = jnp.full((8, rows), NEG, jnp.float32)
            stats[8:16, :] = jnp.zeros((8, rows), jnp.float32)

            def step(number, _):
                attend(number, rows, k_ref, v_turned, masked, starts, query_ids, acc, stats)
                return 0

            lax.fori_loop(jnp.maximum(block - LONGEST // rows, 0), block + 1, step, 0)
            for h in range(heads):
                band = slice(h * HD, (h + 1) * HD)
                acc[band, :] = acc[band, :] / stats[8 + h : 9 + h, :]
            context = acc[...].T.astype(LOW)
            ctx_ref[here, :] = context
            total = jnp.where(stats[8:16, :] > 0, stats[8:16, :], 1.0)
            lse_ref[:, here] = stats[0:8, :] + jnp.log(total)
            return dot(context, w_ref[...])

        scatter = Scatter(place, work, scratch)
        scatter.first()

        def step(number, _):
            scatter.slot(number)
            gather.pass_on(number)
            return 0

        lax.fori_loop(0, chips - 1, step, 0)
        scatter.last()
        scatter.own(mid_ref)
        mid_ref[...] += x_ref[...].astype(jnp.float32)

        def here_too(which, _):
            gather.wait_chip(which)
            return 0

        lax.fori_loop(0, chips, here_too, 0)
        gather.drain()
        scatter.drain()
        spread_up.wait()
        spread_down.wait()

    return line_call(
        kernel,
        "scatter_heads",
        2,
        (*qkv, start, weight, tokens, grads, *shards),
        [
            shape((rows, width), jnp.float32),
            shape((length, head_width)),
            shape((8, length), jnp.float32),
            shape((length, width)),
            shape((width, up_shard.shape[1])),
            shape((down_shard.shape[0], width)),
        ],
        [
            pltpu.VMEM((head_width, length), LOW),
            pltpu.VMEM((head_width, rows), jnp.float32),
            pltpu.VMEM((16, rows), jnp.float32),
        ]
        + Scatter.scratch(chips, rows, width)
        + Gather.scratch(chips)
        + Spread.scratch(groups) * 2,
        COST_FLOPS,
    )


def gather_hidden(groups, chips, middle, gain, shift, gate_weight, up_weight):
    rows, width = middle.shape
    length = rows * 2 * chips
    hidden = gate_weight.shape[1]

    def kernel(mid_ref, gain_ref, shift_ref, wg_ref, wu_ref, full, hid_ref, one_ref, two_ref, *line):
        place = Place(groups, chips)
        gather = Gather(place, full, line)
        normed, _, _ = layer_norm_parts(mid_ref[...], gain_ref[...], shift_ref[...])
        gather.own()[...] = normed.astype(LOW)
        place.barrier()
        gather.begin()

        def work(chip):
            for half in range(2):
                here = pl.ds(pl.multiple_of((chip * 2 + half) * rows, rows), rows)
                values = full[here, :]
                gate = dot(values, wg_ref[...])
                up = dot(values, wu_ref[...])
                sigmoid = 1.0 / (1.0 + jnp.exp(-gate))
                activated = gate * sigmoid
                hid_ref[here, :] = (activated * up).astype(LOW)
                slope = sigmoid * (1.0 + gate * (1.0 - sigmoid))
                one_ref[here, :] = (up * slope).astype(LOW)
                two_ref[here, :] = activated.astype(LOW)

        gather.wait_chip(place.chip)
        work(place.chip)

        def step(number, _):
            gather.pass_on(number)
            gather.each_new(number, work)
            return 0

        lax.fori_loop(0, chips - 1, step, 0)
        gather.drain()

    hidden_shape = shape((length, hidden))
    return line_call(
        kernel,
        "gather_hidden",
        3,
        (middle, gain, shift, gate_weight, up_weight),
        [shape((length, width)), hidden_shape, hidden_shape, hidden_shape],
        Gather.scratch(chips),
        COST_FLOPS,
    )


def scatter_hidden(groups, chips, grads, hidden_low, factors, down, gate_weight, up_weight):
    length, width = grads.shape
    rows = length // (2 * chips)
    hidden = down.shape[0]
    part = width // groups

    def kernel(
        og_ref, hid_ref, one_ref, two_ref, down_ref, wg_ref, wu_ref,
        gg_ref, ug_ref, sum_ref, landed, staged, *rest
    ):
        place = Place(groups, chips)
        scratch, sems = split_refs(rest, Scatter.SCRATCH, 2)
        place.barrier(True)

        def work(chip, core):
            here = pl.ds(pl.multiple_of((chip * 2 + core) * rows, rows), rows)
            hidden_grad = dot(og_ref[here, :], down_ref[...], NT)
            gate_grad = (hidden_grad * one_ref[here, :].astype(jnp.float32)).astype(LOW)
            up_grad = (hidden_grad * two_ref[here, :].astype(jnp.float32)).astype(LOW)
            gg_ref[here, :] = gate_grad
            ug_ref[here, :] = up_grad
            return dot(gate_grad, wg_ref[...], NT) + dot(up_grad, wu_ref[...], NT)

        exchange = Exchange(place, staged, landed, sems)

        def fill(offset):
            block = lax.rem(place.group + offset, groups)
            columns = pl.ds(pl.multiple_of(block * part, part), part)
            staged[offset] = dot(hid_ref[...], og_ref[:, columns], TN).astype(LOW)

        def fill_send(offset):
            fill(offset)
            exchange.copy(offset).start()

        scatter = Scatter(place, work, scratch)
        scatter.first()

        def step(number, _):
            scatter.slot(number)
            pieces(number, chips - 1, groups, fill_send)
            return 0

        lax.fori_loop(0, chips - 1, step, 0)
        scatter.last()
        fill(0)
        exchange.stay().start()
        scatter.own(sum_ref)
        scatter.drain()
        exchange.wait()

    return line_call(
        kernel,
        "scatter_hidden",
        4,
        (grads, hidden_low, *factors, down, gate_weight, up_weight),
        [
            shape((length, hidden)),
            shape((length, hidden)),
            shape((rows, width), jnp.float32),
            shape((groups, hidden, part)),
        ],
        [pltpu.VMEM((groups, hidden, part), LOW)]
        + Scatter.scratch(chips, rows, width)
        + Spread.scratch(groups),
        COST_FLOPS,
        in_hbm=(3,),
    )


def gather_context(
    groups, chips, middle, normed_grad, out_grad, gain, shift, weight, hidden_low, down, normed, pair
):
    rows, width = middle.shape
    length = rows * 2 * chips
    out_width = weight.shape[0]
    hidden = down.shape[0]
    part = width // groups

    def kernel(
        mid_ref, ng_ref, og_ref, gain_ref, shift_ref, w_ref, hid_ref, down_ref, a_ref, gg_ref, ug_ref,
        full, cg_ref, mg_ref, sums_ref, out_ref, landed_gate, landed_up,
        total, staged_gate, staged_up, columns_in, load, *rest
    ):
        place = Place(groups, chips)
        scratch, line, one, two = split_refs(rest, Scatter.SCRATCH, Gather.SEMS, 2, 2)

        def fetch(offset):
            block = lax.rem(place.group + offset, groups)
            columns = pl.ds(pl.multiple_of(block * part, part), part)
            slot = lax.rem(offset, 2)
            return pltpu.make_async_copy(a_ref.at[:, columns], columns_in.at[slot], load.at[slot])

        arrive = pltpu.make_async_copy(ng_ref, total, load.at[3])
        arrive.start()
        fetch(1).start()
        gather = Gather(place, full, line)
        _, plain, inverse = layer_norm_parts(mid_ref[...], gain_ref[...], shift_ref[...])
        arrive.wait()
        back, gain_grad, shift_grad = layer_norm_back(total[...], plain, inverse, gain_ref[...])
        mid_grad = og_ref[...].astype(jnp.float32) + back
        total[...] = mid_grad
        keep = pltpu.make_async_copy(total, mg_ref, load.at[2])
        keep.start()
        sums_ref[0:1, :] = gain_grad[None, :]
        sums_ref[1:2, :] = shift_grad[None, :]
        gather.own()[...] = mid_grad.astype(LOW)
        place.barrier(True)
        gather.begin()

        def back_work(chip):
            here = pl.ds(pl.multiple_of(chip * 2 * rows, 2 * rows), 2 * rows)
            cg_ref[here, :] = dot(full[here, :], w_ref[...], NT).astype(LOW)

        def out_work(chip, core):
            here = pl.ds(pl.multiple_of((chip * 2 + core) * rows, rows), rows)
            return dot(hid_ref[here, :], down_ref[...])

        exchange_gate = Exchange(place, staged_gate, landed_gate, one)
        exchange_up = Exchange(place, staged_up, landed_up, two)

        def fill(offset):
            fetch(offset).wait()
            pl.when(offset > 0)(lambda: fetch(lax.rem(offset + 1, groups)).start())
            values = columns_in[lax.rem(offset, 2)]
            staged_gate[offset] = dot(values, gg_ref[...], TN).astype(LOW)
            staged_up[offset] = dot(values, ug_ref[...], TN).astype(LOW)

        def fill_send(offset):
            fill(offset)
            exchange_gate.copy(offset).start()
            exchange_up.copy(offset).start()

        scatter = Scatter(place, out_work, scratch)
        scatter.first()

        def step(number, _):
            scatter.slot(number)
            pieces(number, chips - 1, groups, fill_send)
            gather.pass_on(number)

            @pl.when(number == 0)
            def _():
                gather.wait_chip(place.chip)
                back_work(place.chip)

            gather.each_new(number, back_work)
            return 0

        lax.fori_loop(0, chips - 1, step, 0)
        scatter.last()
        fill(jnp.int32(0))
        exchange_gate.stay().start()
        exchange_up.stay().start()
        keep.wait()
        scatter.own(total)
        out_ref[...] = (mid_ref[...] + total[...]).astype(LOW)
        gather.drain()
        scatter.drain()
        exchange_gate.wait()
        exchange_up.wait()

    return line_call(
        kernel,
        "gather_context",
        5,
        (middle, normed_grad, out_grad, gain, shift, weight, hidden_low, down, normed, *pair),
        [
            shape((length, width)),
            shape((length, out_width)),
            shape((rows, width), jnp.float32),
            shape((2, width), jnp.float32),
            shape((rows, width)),
            shape((groups, part, hidden)),
            shape((groups, part, hidden)),
        ],
        [
            pltpu.VMEM((rows, width), jnp.float32),
            pltpu.VMEM((groups, part, hidden), LOW),
            pltpu.VMEM((groups, part, hidden), LOW),
            pltpu.VMEM((2, length, part), LOW),
            pltpu.SemaphoreType.DMA((4,)),
        ]
        + Scatter.scratch(chips, rows, width)
        + Gather.scratch(chips)
        + Spread.scratch(groups) * 2,
        COST_FLOPS,
        in_hbm=(2, 5, 6),
        from_hbm=(1, 8),
    )


def scatter_triple(
    groups, chips, triple, weights, tokens, gain, shift, mid_grad, sums, bias_sums, normed, context, grads
):
    length, in_width = triple[0].shape
    rows = length // (2 * chips)
    width = weights.shape[1]
    part = width // groups

    def kernel(
        q_ref, k_ref, v_ref, w_ref, x_ref, gain_ref, shift_ref, mg_ref, sums_ref, bias_ref,
        a_ref, ctx_ref, full_ref,
        in_ref, small_ref, landed_qkv, landed_out,
        total, staged_qkv, staged_out, small_in, small_out, small_recv, *rest
    ):
        place = Place(groups, chips)
        scratch, one, two = split_refs(rest, Scatter.SCRATCH, 2, 2)
        place.barrier(True, True)

        def work(chip, core):
            here = pl.ds(pl.multiple_of((chip * 2 + core) * rows, rows), rows)
            term = dot(q_ref[here, :], w_ref[0], NT)
            term = term + dot(k_ref[here, :], w_ref[1], NT)
            return term + dot(v_ref[here, :], w_ref[2], NT)

        exchange_qkv = Exchange(place, staged_qkv, landed_qkv, one)
        exchange_out = Exchange(place, staged_out, landed_out, two)

        def fill(offset):
            block = lax.rem(place.group + offset, groups)
            columns = pl.ds(pl.multiple_of(block * part, part), part)
            values = a_ref[:, columns]
            for number, ref in enumerate((q_ref, k_ref, v_ref)):
                staged_qkv[offset, number] = dot(values, ref[...], TN).astype(LOW)
            staged_out[offset] = dot(ctx_ref[...], full_ref[:, columns], TN).astype(LOW)

        def fill_send(offset):
            fill(offset)
            exchange_qkv.copy(offset).start()
            exchange_out.copy(offset).start()

        scatter = Scatter(place, work, scratch)
        scatter.first()

        def step(number, _):
            scatter.slot(number)
            pieces(number, chips - 1, groups, fill_send)
            return 0

        lax.fori_loop(0, chips - 1, step, 0)
        scatter.last()
        fill(0)
        exchange_qkv.stay().start()
        exchange_out.stay().start()
        scatter.own(total)
        _, plain, inverse = layer_norm_parts(
            x_ref[...].astype(jnp.float32), gain_ref[...], shift_ref[...]
        )
        back, gain_grad, shift_grad = layer_norm_back(total[...], plain, inverse, gain_ref[...])
        in_ref[...] = (mg_ref[...] + back).astype(LOW)
        small_ref[...] = jnp.zeros_like(small_ref)
        small_ref[0:1, :] = gain_grad[None, :]
        small_ref[1:2, :] = sums_ref[0:1, :]
        small_ref[2:3, :] = shift_grad[None, :]
        small_ref[3:4, :] = sums_ref[1:2, :]
        small_ref[4:7, 0:in_width] = bias_ref[0:3, :]
        for number, partner in enumerate(place.partners()):
            swap = remote(
                small_ref,
                small_in.at[number],
                small_out.at[number],
                small_recv.at[number],
                partner,
            )
            swap.start()
            swap.wait()
            kept = 8 if 2**number < groups else 4
            small_ref[0:kept, :] += small_in[number, 0:kept, :]
        scatter.drain()
        exchange_qkv.wait()
        exchange_out.wait()

    doublings = (groups.bit_length() - 1) + (2 * chips).bit_length() - 1
    return line_call(
        kernel,
        "scatter_triple",
        6,
        (*triple, weights, tokens, gain, shift, mid_grad, sums, bias_sums, normed, context, grads),
        [
            shape((rows, width)),
            shape((8, width), jnp.float32),
            shape((groups, 3, part, in_width)),
            shape((groups, in_width, part)),
        ],
        [
            pltpu.VMEM((rows, width), jnp.float32),
            pltpu.VMEM((groups, 3, part, in_width), LOW),
            pltpu.VMEM((groups, in_width, part), LOW),
            pltpu.VMEM((doublings, 8, width), jnp.float32),
            pltpu.SemaphoreType.DMA((doublings,)),
            pltpu.SemaphoreType.DMA((doublings,)),
        ]
        + Scatter.scratch(chips, rows, width)
        + Spread.scratch(groups) * 2,
        COST_FLOPS,
        in_hbm=(2, 3),
    )


def adam_update(master, gradient, moment_one, moment_two, correct_one, correct_two, rate):
    one_new = 0.9 * moment_one + 0.1 * gradient
    two_new = 0.999 * moment_two + 0.001 * gradient * gradient
    change = one_new / correct_one / (jnp.sqrt(two_new / correct_two) + 1e-08) + 0.1 * master
    return (master - rate * change, one_new, two_new)


def per_device(
    groups,
    chips,
    inputs,
    out_grad,
    segments,
    w_qkv,
    w_out,
    w_gate_up,
    w_down,
    qkv_bias,
    norm_gain,
    norm_bias,
    first_qkv,
    first_out,
    first_gate_up,
    first_down,
    first_bias,
    first_gain,
    first_shift,
    second_qkv,
    second_out,
    second_gate_up,
    second_down,
    second_bias,
    second_gain,
    second_shift,
):
    length = segments.shape[1]
    head_width = w_qkv.shape[2]
    gains = (norm_gain[0:1], norm_gain[1:2])
    shifts = (norm_bias[0:1], norm_bias[1:2])
    place = positions(segments)[0]
    start = jnp.arange(length, dtype=jnp.int32) - place
    low_blocks = start[::BLK] // BLK
    start = start[None, :]
    tables = rotary_tables(place, min(head_width, 128))

    normed_one_all, qkv_all, out_all, gate_all, *qkv = gather_project(
        groups,
        chips,
        inputs,
        gains[0],
        shifts[0],
        (w_qkv, w_out, w_gate_up[0]),
        qkv_bias,
        tables,
    )
    middle, context_flat, lse, mlp_grad, up_all, down_all = scatter_heads(
        groups, chips, qkv, start, out_all, inputs, out_grad, (w_gate_up[1], w_down)
    )
    normed_two_all, hidden_low, *factors = gather_hidden(
        groups, chips, middle, gains[1], shifts[1], gate_all, up_all
    )
    gate_grad, up_grad, normed_two_grad, parts_down = scatter_hidden(
        groups, chips, mlp_grad, hidden_low, factors, down_all, gate_all, up_all
    )
    attn_grad_all, context_grad, middle_grad, sums_two, outputs, parts_gate, parts_up = (
        gather_context(
            groups,
            chips,
            middle,
            normed_two_grad,
            out_grad,
            gains[1],
            shifts[1],
            out_all,
            hidden_low,
            down_all,
            normed_two_all,
            (gate_grad, up_grad),
        )
    )
    *triple, bias_sums = attention_backward(
        low_blocks, *qkv, start, lse, context_flat, context_grad, tables
    )
    input_grad, small, parts_qkv, parts_out = scatter_triple(
        groups,
        chips,
        triple,
        qkv_all,
        inputs,
        gains[0],
        shifts[0],
        middle_grad,
        sums_two,
        bias_sums,
        normed_one_all,
        context_flat,
        attn_grad_all,
    )

    def add_parts(parts):
        total = parts[0].astype(jnp.float32)
        for offset in range(1, groups):
            total = total + parts[offset].astype(jnp.float32)
        return total

    grad_qkv, grad_out, grad_down = add_parts(parts_qkv), add_parts(parts_out), add_parts(parts_down)
    grad_gate_up = jnp.stack([add_parts(parts_gate), add_parts(parts_up)])
    grad_bias = small[4:7, :head_width]
    grad_gain, grad_shift = small[0:2], small[2:4]
    correct_one = 1.0 - 0.9**STEP
    correct_two = 1.0 - 0.999**STEP
    rates = (0.02, 0.3, 0.02, 0.02, 0.3, 0.3, 0.3)
    masters = (w_qkv, w_out, w_gate_up, w_down, qkv_bias, norm_gain, norm_bias)
    gradients = (grad_qkv, grad_out, grad_gate_up, grad_down, grad_bias, grad_gain, grad_shift)
    firsts = (first_qkv, first_out, first_gate_up, first_down, first_bias, first_gain, first_shift)
    seconds = (
        second_qkv,
        second_out,
        second_gate_up,
        second_down,
        second_bias,
        second_gain,
        second_shift,
    )
    updated = [
        adam_update(
            masters[number],
            gradients[number],
            firsts[number],
            seconds[number],
            correct_one,
            correct_two,
            rates[number],
        )
        for number in range(7)
    ]
    return (
        outputs,
        input_grad,
        grad_qkv,
        grad_out,
        grad_gate_up,
        grad_down,
        grad_bias,
        grad_gain,
        grad_shift,
        updated[0][0],
        updated[1][0],
        updated[2][0],
        updated[3][0],
        updated[4][0],
        updated[5][0],
        updated[6][0],
        updated[0][1],
        updated[1][1],
        updated[2][1],
        updated[3][1],
        updated[4][1],
        updated[5][1],
        updated[6][1],
        updated[0][2],
        updated[1][2],
        updated[2][2],
        updated[3][2],
        updated[4][2],
        updated[5][2],
        updated[6][2],
    )


def solution(mesh):
    in_specs = (
        P(("dp", "tensor"), None),
        P(("dp", "tensor"), None),
        P("dp", None),
        P(None, "dp", "tensor"),
        P("tensor", "dp"),
        P(None, "dp", "tensor"),
        P("tensor", "dp"),
        P(None, "tensor"),
        P(),
        P(),
        P(None, "dp", "tensor"),
        P("tensor", "dp"),
        P(None, "dp", "tensor"),
        P("tensor", "dp"),
        P(None, "tensor"),
        P(),
        P(),
        P(None, "dp", "tensor"),
        P("tensor", "dp"),
        P(None, "dp", "tensor"),
        P("tensor", "dp"),
        P(None, "tensor"),
        P(),
        P(),
    )
    out_specs = (
        P(("dp", "tensor"), None),
        P(("dp", "tensor"), None),
        P(None, "dp", "tensor"),
        P("tensor", "dp"),
        P(None, "dp", "tensor"),
        P("tensor", "dp"),
        P(None, "tensor"),
        P(),
        P(),
        P(None, "dp", "tensor"),
        P("tensor", "dp"),
        P(None, "dp", "tensor"),
        P("tensor", "dp"),
        P(None, "tensor"),
        P(),
        P(),
        P(None, "dp", "tensor"),
        P("tensor", "dp"),
        P(None, "dp", "tensor"),
        P("tensor", "dp"),
        P(None, "tensor"),
        P(),
        P(),
        P(None, "dp", "tensor"),
        P("tensor", "dp"),
        P(None, "dp", "tensor"),
        P("tensor", "dp"),
        P(None, "tensor"),
        P(),
        P(),
    )
    return jax.shard_map(
        functools.partial(per_device, mesh.shape["dp"], mesh.shape["tensor"] // 2),
        mesh=mesh, in_specs=in_specs, out_specs=out_specs, check_vma=False
    )
```

```python
import functools

import jax
import jax.numpy as jnp
from jax import lax
from jax.experimental import pallas as pl
from jax.experimental.pallas import tpu as pltpu
from jax.sharding import PartitionSpec as P

HD = 64
ROT = 16
STEP = 10


def layer_norm_parts(values, gain_row, shift_row):
    average = jnp.mean(values, axis=-1, keepdims=True)
    centred = values - average
    inverse = lax.rsqrt(jnp.mean(centred * centred, axis=-1, keepdims=True) + 1e-05)
    normed = centred * inverse
    return (normed * gain_row + shift_row, normed, inverse)


def layer_norm_back(incoming, normed, inverse, gain_row):
    scaled = incoming * gain_row
    inner = (
        scaled
        - jnp.mean(scaled, axis=-1, keepdims=True)
        - normed * jnp.mean(scaled * normed, axis=-1, keepdims=True)
    )
    return (inner * inverse, jnp.sum(incoming * normed, axis=0), jnp.sum(incoming, axis=0))


def positions(segment_ids):
    length = segment_ids.shape[-1]
    indices = jnp.broadcast_to(jnp.arange(length, dtype=jnp.int32), segment_ids.shape)
    before = jnp.concatenate(
        [jnp.full(segment_ids.shape[:-1] + (1,), -1, jnp.int32), segment_ids[..., :-1]], axis=-1
    )
    starts = lax.cummax(jnp.where(segment_ids != before, indices, 0), axis=segment_ids.ndim - 1)
    return indices - starts


def rotary_tables(position_ids, width):
    half_rot = ROT // 2
    frequency = 10000.0 ** (-(2.0 * jnp.arange(half_rot, dtype=jnp.float32)) / ROT)
    angles = position_ids.astype(jnp.float32)[:, None] * frequency
    cosine, sine = jnp.cos(angles), jnp.sin(angles)
    zeros = jnp.zeros((angles.shape[0], HD - ROT), jnp.float32)
    blank = jnp.zeros_like(sine)
    copies = width // HD
    return tuple(
        jnp.tile(jnp.concatenate(parts, axis=1), (1, copies))
        for parts in (
            (cosine, cosine, zeros + 1.0),
            (-sine, blank, zeros),
            (blank, sine, zeros),
        )
    )


NEG = -1e30
BLK = 256
NT = (((1,), (1,)), ((), ()))
NN = (((1,), (0,)), ((), ()))


def dot(left, right, dims=NN, precision=None):
    return lax.dot_general(
        left, right, dims, preferred_element_type=jnp.float32, precision=precision
    )


def head_masks(width, dtype):
    lane = lax.broadcasted_iota(jnp.int32, (1, width), 1)
    return [(lane // HD == h).astype(dtype) for h in range(width // HD)]


def rope_tile(tile, cosine, sine_low, sine_high, sign):
    width = tile.shape[-1]
    ahead = pltpu.roll(tile, width - ROT // 2, 1)
    behind = pltpu.roll(tile, ROT // 2, 1)
    return tile * cosine + sign * (ahead * sine_low + behind * sine_high)


def attend(number, size, k_ref, v_turned, masked, starts, query_ids, acc, stats):
    base = pl.multiple_of(number * size, size)
    keys = k_ref[pl.ds(base, size), :]
    key_ids = base + lax.broadcasted_iota(jnp.int32, (size, size), 0)
    visible = (key_ids >= starts) & (key_ids <= query_ids)
    for h, queries in enumerate(masked):
        scores = jnp.where(visible, dot(keys, queries, NT), NEG)
        peak_old = stats[h : h + 1, :]
        peak = jnp.maximum(peak_old, jnp.max(scores, axis=0, keepdims=True))
        fade = jnp.exp(peak_old - peak)
        prob = jnp.exp(scores - peak)
        stats[h : h + 1, :] = peak
        stats[8 + h : 9 + h, :] = stats[8 + h : 9 + h, :] * fade + jnp.sum(
            prob, axis=0, keepdims=True
        )
        band = slice(h * HD, (h + 1) * HD)
        acc[band, :] = acc[band, :] * fade + dot(
            v_turned[band, pl.ds(base, size)], prob.astype(jnp.bfloat16)
        )


def backward_kernel(
    low_ref,
    q_ref,
    k_ref,
    v_ref,
    start_ref,
    lse_ref,
    ctx_ref,
    grad_ref,
    cos_ref,
    sin_low_ref,
    sin_high_ref,
    dq_ref,
    dk_ref,
    dv_ref,
    bias_ref,
    k_turned,
    dq_acc,
    dk_acc,
    dv_acc,
):
    block = pl.program_id(0)
    last = pl.num_programs(0) - 1
    length, width = k_ref.shape
    heads = width // HD
    tile = min(width, 128)

    @pl.when(block == 0)
    def _():
        for part in range(length // BLK):
            rows = slice(part * BLK, (part + 1) * BLK)
            k_turned[:, rows] = k_ref[rows, :].T
        dk_acc[...] = jnp.zeros_like(dk_acc)
        dv_acc[...] = jnp.zeros_like(dv_acc)
        bias_ref[...] = jnp.zeros_like(bias_ref)

    here = pl.ds(pl.multiple_of(block * BLK, BLK), BLK)
    masks = head_masks(width, jnp.bfloat16)
    queries = (q_ref[here, :] * 0.125).astype(jnp.bfloat16)
    masked = [queries * m for m in masks]
    grads = grad_ref[...]
    grads_masked = [grads * m for m in masks]
    product = grads.astype(jnp.float32) * ctx_ref[...].astype(jnp.float32)
    select = (
        lax.broadcasted_iota(jnp.int32, (8, width), 1) // HD
        == lax.broadcasted_iota(jnp.int32, (8, width), 0)
    ).astype(jnp.float32)
    delta = dot(select, product, NT, lax.Precision.HIGHEST)
    start = start_ref[...]
    query_ids = block * BLK + lax.broadcasted_iota(jnp.int32, (1, BLK), 1)
    dq_acc[...] = jnp.zeros_like(dq_acc)

    def step(number, _):
        base = pl.multiple_of(number * BLK, BLK)
        rows_k = pl.ds(base, BLK)
        keys = k_ref[rows_k, :]
        vals = v_ref[rows_k, :]
        key_ids = base + lax.broadcasted_iota(jnp.int32, (BLK, BLK), 0)
        visible = (key_ids >= start) & (key_ids <= query_ids)
        dk = dk_acc[rows_k, :]
        dv = dv_acc[rows_k, :]
        for h in range(heads):
            scores = dot(keys, masked[h], NT)
            prob = jnp.where(visible, jnp.exp(scores - lse_ref[h : h + 1, :]), 0.0)
            dprob = dot(vals, grads_masked[h], NT)
            dscore = (prob * (dprob - delta[h : h + 1, :])).astype(jnp.bfloat16)
            dv = dv + dot(prob.astype(jnp.bfloat16), grads_masked[h])
            dk = dk + dot(dscore, masked[h])
            rows = slice(h * HD, (h + 1) * HD)
            dq_acc[rows, :] += dot(k_turned[rows, rows_k], dscore)
        dk_acc[rows_k, :] = dk
        dv_acc[rows_k, :] = dv
        return 0

    lax.fori_loop(low_ref[block], block + 1, step, 0)

    def turn_back(values, rows):
        parts = []
        for t in range(width // tile):
            parts.append(
                rope_tile(
                    values[:, t * tile : (t + 1) * tile],
                    cos_ref[rows, :],
                    sin_low_ref[rows, :],
                    sin_high_ref[rows, :],
                    -1.0,
                )
            )
        return jnp.concatenate(parts, axis=1) if len(parts) > 1 else parts[0]

    dq = turn_back(dq_acc[...].T * 0.125, here).astype(jnp.bfloat16)
    dq_ref[...] = dq
    bias_ref[0:1, :] += jnp.sum(dq.astype(jnp.float32), axis=0, keepdims=True)

    @pl.when(block == last)
    def _():
        def finish(part, _):
            rows = pl.ds(pl.multiple_of(part * BLK, BLK), BLK)
            dk = turn_back(dk_acc[rows, :], rows).astype(jnp.bfloat16)
            dv = dv_acc[rows, :].astype(jnp.bfloat16)
            dk_ref[rows, :] = dk
            dv_ref[rows, :] = dv
            bias_ref[1:2, :] += jnp.sum(dk.astype(jnp.float32), axis=0, keepdims=True)
            bias_ref[2:3, :] += jnp.sum(dv.astype(jnp.float32), axis=0, keepdims=True)
            return 0

        lax.fori_loop(0, length // BLK, finish, 0)


def attention_backward(low_blocks, queries, keys, values, start, lse, context, grads, tables):
    length, width = queries.shape
    whole = pl.BlockSpec((length, width), lambda i, low: (0, 0))
    rows = pl.BlockSpec((BLK, width), lambda i, low: (i, 0))
    table = pl.BlockSpec(tables[0].shape, lambda i, low: (0, 0))
    return pl.pallas_call(
        backward_kernel,
        grid_spec=pltpu.PrefetchScalarGridSpec(
            num_scalar_prefetch=1,
            grid=(length // BLK,),
            in_specs=[
                whole,
                whole,
                whole,
                pl.BlockSpec((1, BLK), lambda i, low: (0, i)),
                pl.BlockSpec((8, BLK), lambda i, low: (0, i)),
                rows,
                rows,
                table,
                table,
                table,
            ],
            out_specs=[rows, whole, whole, pl.BlockSpec((8, width), lambda i, low: (0, 0))],
            scratch_shapes=[
                pltpu.VMEM((width, length), jnp.bfloat16),
                pltpu.VMEM((width, BLK), jnp.float32),
                pltpu.VMEM((length, width), jnp.float32),
                pltpu.VMEM((length, width), jnp.float32),
            ],
        ),
        out_shape=[jax.ShapeDtypeStruct((length, width), jnp.bfloat16)] * 3
        + [jax.ShapeDtypeStruct((8, width), jnp.float32)],
        compiler_params=pltpu.CompilerParams(vmem_limit_bytes=40 << 20),
        name="attention_backward",
    )(low_blocks, queries, keys, values, start, lse, context, grads, *tables)


MESH = pl.DeviceIdType.MESH
VMEM_BYTES = 62 << 20
LONGEST = 1024
TN = (((0,), (0,)), ((), ()))
LOW = jnp.bfloat16


def remote(source, target, send, receive, device):
    return pltpu.make_async_remote_copy(
        src_ref=source,
        dst_ref=target,
        send_sem=send,
        recv_sem=receive,
        device_id=device,
        device_id_type=MESH,
    )


class Place:
    def __init__(self, groups, chips):
        self.groups, self.chips = groups, chips
        self.group = lax.axis_index("dp")
        self.spot = lax.axis_index("tensor")
        self.chip, self.core = self.spot // 2, self.spot % 2

    def at(self, chip, core):
        return (self.group, chip * 2 + core)

    def peer(self, offset):
        return (lax.rem(self.group + offset, self.groups), self.spot)

    def fellow(self, offset):
        return (self.group, lax.rem(self.spot + offset, 2 * self.chips))

    def barrier(self, with_groups=False, with_all_spots=False):
        semaphore = pltpu.get_barrier_semaphore()

        def greet(target):
            pl.semaphore_signal(semaphore, inc=1, device_id=target, device_id_type=MESH)

        if with_all_spots:
            for offset in range(1, 2 * self.chips):
                greet(self.fellow(offset))
            count = 2 * self.chips - 1
        else:
            greet(self.at(self.chip, 1 - self.core))
            pl.when(self.chip > 0)(lambda: greet(self.at(self.chip - 1, self.core)))
            pl.when(self.chip < self.chips - 1)(lambda: greet(self.at(self.chip + 1, self.core)))
            count = 1 + jnp.where(self.chip > 0, 1, 0) + jnp.where(self.chip < self.chips - 1, 1, 0)
        if with_groups:
            for offset in range(1, self.groups):
                greet(self.peer(offset))
            count = count + self.groups - 1
        pl.semaphore_wait(semaphore, count)


def each(count, use):
    def one(index, _):
        use(index)
        return 0

    lax.fori_loop(0, count, one, 0)


def block_of(ref, index, size):
    return ref.at[pl.ds(pl.multiple_of(index * size, size), size)]


def fetch_all(pairs, sems):
    copies = [pltpu.make_async_copy(a, b, sems.at[n]) for n, (a, b) in enumerate(pairs)]
    for copy in copies:
        copy.start()
    return copies


HALVES = 2


class Gather:
    SEMS = 5

    def __init__(self, place, full, sems, kept=None, keep_sem=None):
        self.place, self.full, self.kept, self.keep_sem = place, full, kept, keep_sem
        self.line_in, self.core_in, self.right_out, self.left_out, self.core_out = sems
        self.rows = full.shape[0] // (2 * place.chips)

    @classmethod
    def scratch(cls, chips):
        return [pltpu.SemaphoreType.DMA((chips * HALVES,)) for _ in range(cls.SEMS)]

    def own(self):
        return block_of(self.full, self.place.spot, self.rows)

    def block(self, chip, core, half):
        return block_of(self.full, (chip * 2 + core) * HALVES + half, self.rows // HALVES)

    def right(self, which, half):
        place, part = self.place, self.block(which, self.place.core, half)
        target = place.at(jnp.minimum(place.chip + 1, place.chips - 1), place.core)
        index = which * HALVES + half
        return remote(part, part, self.right_out.at[index], self.line_in.at[index], target)

    def left(self, which, half):
        place, part = self.place, self.block(which, self.place.core, half)
        target = place.at(jnp.maximum(place.chip - 1, 0), place.core)
        index = which * HALVES + half
        return remote(part, part, self.left_out.at[index], self.line_in.at[index], target)

    def across(self, which, core, half):
        place, part = self.place, self.block(which, core, half)
        target = place.at(place.chip, 1 - place.core)
        index = which * HALVES + half
        return remote(part, part, self.core_out.at[index], self.core_in.at[index], target)

    def begin(self):
        chip, chips = self.place.chip, self.place.chips
        for half in range(HALVES):
            pl.when(chip < chips - 1)(lambda: self.right(chip, half).start())
            pl.when(chip > 0)(lambda: self.left(chip, half).start())
        for half in range(HALVES):
            self.across(chip, self.place.core, half).start()

    def pass_on(self, step):
        chip, chips, core = self.place.chip, self.place.chips, self.place.core
        low, high = chip - 1 - step, chip + 1 + step
        for half in range(HALVES):

            @pl.when(low >= 0)
            def _():
                self.right(low, half).wait_recv()
                pl.when(chip < chips - 1)(lambda: self.right(low, half).start())
                self.across(low, core, half).start()

            @pl.when(high < chips)
            def _():
                self.left(high, half).wait_recv()
                pl.when(chip > 0)(lambda: self.left(high, half).start())
                self.across(high, core, half).start()

    def keep(self, which):
        part = block_of(self.full, which, 2 * self.rows)
        return pltpu.make_async_copy(
            part, block_of(self.kept, which, 2 * self.rows), self.keep_sem.at[which]
        )

    def wait_chip(self, which):
        for half in range(HALVES):
            self.across(which, 1 - self.place.core, half).wait_recv()
        if self.kept is not None:
            self.keep(which).start()

    def each_new(self, step, use):
        low, high = self.place.chip - 1 - step, self.place.chip + 1 + step

        @pl.when(low >= 0)
        def _():
            self.wait_chip(low)
            use(low)

        @pl.when(high < self.place.chips)
        def _():
            self.wait_chip(high)
            use(high)

    def drain(self):
        chip, chips, core = self.place.chip, self.place.chips, self.place.core

        def one(which):
            for half in range(HALVES):
                self.across(which, core, half).wait_send()
                pl.when((which <= chip) & (chip < chips - 1))(
                    lambda: self.right(which, half).wait_send()
                )
                pl.when((which >= chip) & (chip > 0))(lambda: self.left(which, half).wait_send())
            if self.kept is not None:
                self.keep(which).wait()

        each(chips, one)


class Scatter:
    def __init__(self, place, work, scratch):
        self.place, self.work = place, work
        self.out, self.side, self.line = scratch[:3]
        self.core_out, self.core_in, self.line_out, self.line_in = scratch[3:]
        self.part = self.out.shape[1] // HALVES
        chip, chips = place.chip, place.chips
        self.near = jnp.minimum(chip, chips - 1 - chip)
        self.alone = chips - 1 - 2 * self.near
        self.flip = jnp.where(chip * 2 < chips, 0, 1)
        self.lag = jnp.where(self.near > 0, 1, 0)

    @staticmethod
    def scratch(chips, rows, width):
        return [
            pltpu.VMEM((chips, rows, width), LOW),
            pltpu.VMEM((chips, rows, width), LOW),
            pltpu.VMEM((chips + 1, rows, width), LOW),
            pltpu.SemaphoreType.DMA((chips,)),
            pltpu.SemaphoreType.DMA((chips,)),
            pltpu.SemaphoreType.DMA((chips * HALVES,)),
            pltpu.SemaphoreType.DMA(((chips + 1) * HALVES,)),
        ]

    SCRATCH = 7

    def order(self, turn):
        chips = self.place.chips
        later = jnp.maximum(turn - self.alone, 0)
        pair = later // 2
        far = jnp.where(turn < self.alone, chips - 1 - turn, chips - 1 - self.alone - pair)
        which = jnp.where((turn >= self.alone) & (later % 2 == 1), pair, far)
        which = jnp.where(turn == chips - 1, self.near, which)
        return jnp.where(self.flip == 1, chips - 1 - which, which)

    def across(self, which):
        place = self.place
        return remote(
            self.out.at[which],
            self.side.at[which],
            self.core_out.at[which],
            self.core_in.at[which],
            place.at(place.chip, 1 - place.core),
        )

    def hop(self, which, slot, half, target):
        rows = slice(half * self.part, (half + 1) * self.part)
        return remote(
            self.out.at[which, rows],
            self.line.at[slot, rows],
            self.line_out.at[which * HALVES + half],
            self.line_in.at[slot * HALVES + half],
            self.place.at(target, self.place.core),
        )

    def right(self, which, half):
        place = self.place
        slot = jnp.where(which == place.chip + 1, place.chips, which)
        return self.hop(which, slot, half, jnp.minimum(place.chip + 1, place.chips - 1))

    def left(self, which, half):
        return self.hop(which, which, half, jnp.maximum(self.place.chip - 1, 0))

    def arrived(self, slot, half):
        place = self.place
        rows = slice(half * self.part, (half + 1) * self.part)
        part = self.line.at[slot, rows]
        other = place.at(place.chip, 1 - place.core)
        remote(
            part, part, self.line_out.at[0], self.line_in.at[slot * HALVES + half], other
        ).wait_recv()
        return self.line[slot, rows].astype(jnp.float32)

    def produce(self, turn):
        which = self.order(turn)
        self.out[which] = self.work(which, 1 - self.place.core).astype(LOW)
        self.across(which).start()

    def chip_sum(self, which):
        mine = self.work(which, self.place.core)
        self.across(which).wait()
        return mine + self.side[which].astype(jnp.float32)

    def send(self, which, upstream, copy):
        total = self.chip_sum(which)

        @pl.when(upstream)
        def _():
            for half in range(HALVES):
                rows = slice(half * self.part, (half + 1) * self.part)
                self.out[which, rows] = (total[rows] + self.arrived(which, half)).astype(LOW)
                copy(which, half).start()

        @pl.when(jnp.logical_not(upstream))
        def _():
            for half in range(HALVES):
                rows = slice(half * self.part, (half + 1) * self.part)
                self.out[which, rows] = total[rows].astype(LOW)
                copy(which, half).start()

    def first(self):
        pl.when(self.lag == 1)(lambda: self.produce(0))

    def slot(self, number):
        chip, chips = self.place.chip, self.place.chips
        self.produce(number + self.lag)
        right = chips - 1 - (number - chip)
        left = number - (chips - 1 - chip)
        pl.when((number >= chip) & (right > chip))(
            lambda: self.send(right, chip > 0, self.right)
        )
        pl.when((left >= 0) & (left < chip))(
            lambda: self.send(left, chip < chips - 1, self.left)
        )

    def last(self):
        pl.when(self.lag == 0)(lambda: self.produce(self.place.chips - 1))

    def own(self, total):
        chip, chips = self.place.chip, self.place.chips
        total[...] = self.chip_sum(chip)
        for half in range(HALVES):
            rows = slice(half * self.part, (half + 1) * self.part)

            @pl.when(chip > 0)
            def _():
                total[rows] += self.arrived(chips, half)

            @pl.when(chip < chips - 1)
            def _():
                total[rows] += self.arrived(chip, half)

    def drain(self):
        chip = self.place.chip

        def one(which):
            for half in range(HALVES):
                pl.when(which > chip)(lambda: self.right(which, half).wait_send())
                pl.when(which < chip)(lambda: self.left(which, half).wait_send())

        each(self.place.chips, one)


class Spread:
    def __init__(self, place, shard, staged, whole, axis, sems):
        self.place, self.staged, self.whole, self.sems = place, staged, whole, sems
        size = shard.shape[axis]
        here = pl.ds(pl.multiple_of(place.group * size, size), size)
        self.mine = whole.at[tuple(here if a == axis else slice(None) for a in range(len(shard.shape)))]
        staged[...] = shard[...].astype(LOW)

    @staticmethod
    def scratch(groups):
        return [pltpu.SemaphoreType.DMA((groups,)), pltpu.SemaphoreType.DMA((groups,))]

    def copy(self, offset):
        return remote(
            self.staged,
            self.mine,
            self.sems[0].at[offset],
            self.sems[1].at[offset],
            self.place.peer(offset),
        )

    def stay(self):
        return pltpu.make_async_copy(self.staged, self.mine, self.sems[0].at[0])

    def start(self):
        for offset in range(1, self.place.groups):
            self.copy(offset).start()
        self.stay().start()

    def wait(self):
        for offset in range(1, self.place.groups):
            self.copy(offset).wait()
        self.stay().wait()


class Exchange:
    def __init__(self, place, staged, landed, sems):
        self.place, self.staged, self.landed = place, staged, landed
        self.send, self.receive = sems

    def copy(self, offset):
        return remote(
            self.staged.at[offset],
            self.landed.at[offset],
            self.send.at[offset],
            self.receive.at[offset],
            self.place.peer(offset),
        )

    def stay(self):
        return pltpu.make_async_copy(self.staged.at[0], self.landed.at[0], self.send.at[0])

    def wait(self):
        def one(offset, _):
            self.copy(offset).wait()
            return 0

        lax.fori_loop(1, self.place.groups, one, 0)
        self.stay().wait()


class SmallSum:
    def __init__(self, slots, me, count, target, sems):
        self.slots, self.me, self.count, self.target = slots, me, count, target
        self.send, self.receive = sems

    def copy(self, offset):
        part = self.slots.at[self.me]
        return remote(
            part, part, self.send.at[offset], self.receive.at[self.me], self.target(offset)
        )

    def begin(self, rows):
        self.slots[self.me] = rows
        for offset in range(1, self.count):
            self.copy(offset).start()

    def result(self):
        for offset in range(1, self.count):
            source = lax.rem(self.me + offset, self.count)
            part = self.slots.at[source]
            remote(
                part, part, self.send.at[offset], self.receive.at[source], self.target(offset)
            ).wait_recv()
        total = self.slots[0]
        for index in range(1, self.count):
            total = total + self.slots[index]
        for offset in range(1, self.count):
            self.copy(offset).wait_send()
        return total


def pieces(number, groups, fill):
    @pl.when(number == 0)
    def _():
        each(groups - 1, lambda index: fill(index + 1))


def line_call(kernel, name, number, operands, out_shape, scratch, flops, in_hbm=(), from_hbm=()):
    whole, hbm = pl.BlockSpec(memory_space=pltpu.VMEM), pl.BlockSpec(memory_space=pl.ANY)
    ins = [hbm if n in from_hbm else whole for n in range(len(operands))]
    outs = [hbm if n in in_hbm else whole for n in range(len(out_shape))]
    return pl.pallas_call(
        kernel,
        out_shape=out_shape,
        in_specs=ins,
        out_specs=outs,
        scratch_shapes=scratch,
        compiler_params=pltpu.CompilerParams(
            collective_id=number, has_side_effects=True, vmem_limit_bytes=VMEM_BYTES
        ),
        cost_estimate=pl.CostEstimate(flops=flops, bytes_accessed=0, transcendentals=0),
        name=name,
    )(*operands)


COST_FLOPS = 80_000_000_000


def shape(dims, kind=LOW):
    return jax.ShapeDtypeStruct(dims, kind)


def split_refs(refs, *counts):
    parts, at = [], 0
    for count in counts:
        parts.append(refs[at : at + count])
        at += count
    return parts


def gather_project(groups, chips, tokens, gain, shift, shards, bias, tables):
    rows, width = tokens.shape
    length = rows * 2 * chips
    qkv_shard, out_shard = shards
    part, out_width = qkv_shard.shape[1:]
    tile = tables[0].shape[1]

    def kernel(
        x_ref, gain_ref, shift_ref, qkv_ref, out_ref, bias_ref, cos_hbm, sin_low_hbm, sin_high_hbm,
        kept, weights_kept, out_whole, q_ref, k_ref, v_ref,
        full, weights, qkv_staged, out_staged, cos_ref, sin_low_ref, sin_high_ref,
        load, keep_sem, *sems
    ):
        place = Place(groups, chips)
        fetches = fetch_all(
            [(cos_hbm, cos_ref), (sin_low_hbm, sin_low_ref), (sin_high_hbm, sin_high_ref)], load
        )
        line, one, two = split_refs(sems, Gather.SEMS, 2, 2)
        gather = Gather(place, full, line, kept, keep_sem)
        normed, _, _ = layer_norm_parts(
            x_ref[...].astype(jnp.float32), gain_ref[...], shift_ref[...]
        )
        gather.own()[...] = normed.astype(LOW)
        spread_qkv = Spread(place, qkv_ref, qkv_staged, weights, 1, one)
        place.barrier(True)
        gather.begin()
        spread_qkv.start()
        spread_out = Spread(place, out_ref, out_staged, out_whole, 1, two)
        spread_out.start()

        def work(chip):
            base = pl.multiple_of(chip * 2 * rows, 2 * rows)
            here = pl.ds(base, 2 * rows)
            values = full[here, :]
            for number, ref in enumerate((q_ref, k_ref, v_ref)):
                result = dot(values, weights[number]) + bias_ref[number : number + 1, :]
                if number < 2:
                    parts = [
                        rope_tile(
                            result[:, t * tile : (t + 1) * tile],
                            cos_ref[here, :],
                            sin_low_ref[here, :],
                            sin_high_ref[here, :],
                            1.0,
                        )
                        for t in range(out_width // tile)
                    ]
                    result = jnp.concatenate(parts, axis=1) if len(parts) > 1 else parts[0]
                ref[here, :] = result.astype(LOW)

        gather.pass_on(0)
        for copy in fetches:
            copy.wait()
        spread_qkv.wait()
        weights_keep = pltpu.make_async_copy(weights, weights_kept, load.at[3])
        weights_keep.start()
        gather.wait_chip(place.chip)
        work(place.chip)

        def step(number):
            pl.when(number > 0)(lambda: gather.pass_on(number))
            gather.each_new(number, work)

        each(chips - 1, step)
        weights_keep.wait()
        spread_out.wait()
        gather.drain()

    head_shape = shape((length, out_width))
    return line_call(
        kernel,
        "gather_project",
        1,
        (tokens, gain, shift, *shards, bias, *tables),
        [
            shape((length, width)),
            shape((3, width, out_width)),
            shape((out_width, width)),
            head_shape,
            head_shape,
            head_shape,
        ],
        [
            pltpu.VMEM((length, width), LOW),
            pltpu.VMEM((3, width, out_width), LOW),
            pltpu.VMEM(qkv_shard.shape, LOW),
            pltpu.VMEM(out_shard.shape, LOW),
            *(pltpu.VMEM((length, tile), jnp.float32) for _ in range(3)),
            pltpu.SemaphoreType.DMA((4,)),
            pltpu.SemaphoreType.DMA((chips,)),
        ]
        + Gather.scratch(chips)
        + Spread.scratch(groups) * 2,
        COST_FLOPS,
        in_hbm=(0, 1, 2),
        from_hbm=(6, 7, 8),
    )


def scatter_heads(groups, chips, qkv, start, weight, tokens, grads, shards):
    rows, width = tokens.shape
    length, head_width = qkv[0].shape
    heads = head_width // HD
    (pair_shard,) = shards

    def kernel(
        q_hbm, k_hbm, v_hbm, w_hbm, x_hbm, og_hbm, start_ref, pair_ref,
        mid_ref, ctx_ref, lse_ref, kept, pair_whole,
        full, q_ref, k_ref, v_ref, w_ref, x_ref, pair_staged,
        load, keep_sem, v_turned, acc, stats, *rest
    ):
        place = Place(groups, chips)
        scratch, line, one = split_refs(rest, Scatter.SCRATCH, Gather.SEMS, 2)
        gather = Gather(place, full, line, kept, keep_sem)
        fetches = fetch_all(
            [
                (og_hbm, gather.own()),
                (k_hbm, k_ref),
                (v_hbm, v_ref),
                (q_hbm, q_ref),
                (w_hbm, w_ref),
                (x_hbm, x_ref),
            ],
            load,
        )
        place.barrier(True)
        fetches[0].wait()
        gather.begin()
        spread_pair = Spread(place, pair_ref, pair_staged, pair_whole, 2, one)
        spread_pair.start()
        for copy in fetches[1:5]:
            copy.wait()
        for part in range(length // BLK):
            here = slice(part * BLK, (part + 1) * BLK)
            v_turned[:, here] = v_ref[here, :].T
        masks = head_masks(head_width, LOW)

        def work(chip, core):
            block = chip * 2 + core
            base = pl.multiple_of(block * rows, rows)
            here = pl.ds(base, rows)
            values = (q_ref[here, :] * 0.125).astype(LOW)
            masked = [values * m for m in masks]
            starts = start_ref[:, here]
            query_ids = base + lax.broadcasted_iota(jnp.int32, (1, rows), 1)
            acc[...] = jnp.zeros_like(acc)
            stats[0:8, :] = jnp.full((8, rows), NEG, jnp.float32)
            stats[8:16, :] = jnp.zeros((8, rows), jnp.float32)

            def step(number, _):
                attend(number, rows, k_ref, v_turned, masked, starts, query_ids, acc, stats)
                return 0

            lax.fori_loop(jnp.maximum(block - LONGEST // rows, 0), block + 1, step, 0)
            for h in range(heads):
                band = slice(h * HD, (h + 1) * HD)
                acc[band, :] = acc[band, :] / stats[8 + h : 9 + h, :]
            context = acc[...].T.astype(LOW)
            ctx_ref[here, :] = context
            total = jnp.where(stats[8:16, :] > 0, stats[8:16, :], 1.0)
            lse_ref[:, here] = stats[0:8, :] + jnp.log(total)
            return dot(context, w_ref[...])

        scatter = Scatter(place, work, scratch)
        scatter.first()

        def seen(chip):
            pass

        def step(number):
            scatter.slot(number)
            gather.pass_on(number)
            pl.when(number > 0)(lambda: gather.each_new(number - 1, seen))

        each(chips - 1, step)
        scatter.last()
        fetches[5].wait()
        gather.wait_chip(place.chip)
        gather.each_new(chips - 2, seen)
        scatter.own(mid_ref)
        mid_ref[...] += x_ref[...].astype(jnp.float32)
        gather.drain()
        scatter.drain()
        spread_pair.wait()

    return line_call(
        kernel,
        "scatter_heads",
        2,
        (*qkv, weight, tokens, grads, start, *shards),
        [
            shape((rows, width), jnp.float32),
            shape((length, head_width)),
            shape((8, length), jnp.float32),
            shape((length, width)),
            shape((2, pair_shard.shape[1], width)),
        ],
        [
            pltpu.VMEM((length, width), LOW),
            *(pltpu.VMEM((length, head_width), LOW) for _ in range(3)),
            pltpu.VMEM((head_width, width), LOW),
            pltpu.VMEM((rows, width), LOW),
            pltpu.VMEM(pair_shard.shape, LOW),
            pltpu.SemaphoreType.DMA((6,)),
            pltpu.SemaphoreType.DMA((chips,)),
            pltpu.VMEM((head_width, length), LOW),
            pltpu.VMEM((head_width, rows), jnp.float32),
            pltpu.VMEM((16, rows), jnp.float32),
        ]
        + Scatter.scratch(chips, rows, width)
        + Gather.scratch(chips)
        + Spread.scratch(groups),
        COST_FLOPS,
        in_hbm=(3, 4),
        from_hbm=(0, 1, 2, 3, 4, 5),
    )


def gather_hidden(groups, chips, middle, gain, shift, pair_weight, down_shard):
    rows, width = middle.shape
    length = rows * 2 * chips
    hidden = pair_weight.shape[1]

    def kernel(
        mid_ref, gain_ref, shift_ref, pair_hbm, down_ref,
        kept, hid_kept, one_kept, two_kept, down_whole,
        full, hid_ref, one_ref, two_ref, pair_ref, down_staged, load, keep_sem, *rest
    ):
        place = Place(groups, chips)
        fetches = fetch_all([(pair_hbm, pair_ref)], load)
        line, keeps, sems = split_refs(rest, Gather.SEMS, 3, 2)
        gather = Gather(place, full, line, kept, keep_sem)
        normed, _, _ = layer_norm_parts(mid_ref[...], gain_ref[...], shift_ref[...])
        gather.own()[...] = normed.astype(LOW)
        place.barrier(True)
        gather.begin()
        spread_down = Spread(place, down_ref, down_staged, down_whole, 1, sems)
        spread_down.start()
        results = list(zip((hid_ref, one_ref, two_ref), (hid_kept, one_kept, two_kept), keeps))

        def store(chip):
            return [
                pltpu.make_async_copy(
                    block_of(a, chip, 2 * rows), block_of(b, chip, 2 * rows), sem.at[chip]
                )
                for a, b, sem in results
            ]

        def work(chip):
            for half in range(2):
                here = pl.ds(pl.multiple_of((chip * 2 + half) * rows, rows), rows)
                values = full[here, :]
                gate = dot(values, pair_ref[0], NT)
                up = dot(values, pair_ref[1], NT)
                sigmoid = 1.0 / (1.0 + jnp.exp(-gate))
                activated = gate * sigmoid
                hid_ref[here, :] = (activated * up).astype(LOW)
                slope = sigmoid * (1.0 + gate * (1.0 - sigmoid))
                one_ref[here, :] = (up * slope).astype(LOW)
                two_ref[here, :] = activated.astype(LOW)
            for copy in store(chip):
                copy.start()

        for copy in fetches:
            copy.wait()
        gather.wait_chip(place.chip)
        work(place.chip)

        def step(number):
            gather.pass_on(number)
            gather.each_new(number, work)

        each(chips - 1, step)
        gather.drain()

        def stored(chip):
            for copy in store(chip):
                copy.wait()

        each(chips, stored)
        spread_down.wait()

    hidden_shape = shape((length, hidden))
    return line_call(
        kernel,
        "gather_hidden",
        3,
        (middle, gain, shift, pair_weight, down_shard),
        [
            shape((length, width)),
            hidden_shape,
            hidden_shape,
            hidden_shape,
            shape((down_shard.shape[0], width)),
        ],
        [
            pltpu.VMEM((length, width), LOW),
            *(pltpu.VMEM((length, hidden), LOW) for _ in range(3)),
            pltpu.VMEM(pair_weight.shape, LOW),
            pltpu.VMEM(down_shard.shape, LOW),
            pltpu.SemaphoreType.DMA((1,)),
            pltpu.SemaphoreType.DMA((chips,)),
        ]
        + Gather.scratch(chips)
        + [pltpu.SemaphoreType.DMA((chips,)) for _ in range(3)]
        + Spread.scratch(groups),
        COST_FLOPS,
        in_hbm=(0, 1, 2, 3, 4),
        from_hbm=(3,),
    )


def scatter_hidden(groups, chips, grads, hidden_low, factors, down, pair_weight):
    length, width = grads.shape
    rows = length // (2 * chips)
    hidden = down.shape[0]
    part = width // groups

    def kernel(
        og_hbm, hid_hbm, one_hbm, two_hbm, down_hbm, pair_hbm,
        gg_kept, ug_kept, sum_ref, landed,
        og_ref, hid_ref, one_ref, two_ref, down_ref, pair_ref, gg_ref, ug_ref, staged,
        load, load_og, load_one, load_two, keep_gg, keep_ug, *rest
    ):
        place = Place(groups, chips)
        scratch, sems = split_refs(rest, Scatter.SCRATCH, 2)
        chunked = ((og_hbm, og_ref, load_og), (one_hbm, one_ref, load_one), (two_hbm, two_ref, load_two))

        def bring(chip):
            return [
                pltpu.make_async_copy(
                    block_of(a, chip, 2 * rows), block_of(b, chip, 2 * rows), sem.at[chip]
                )
                for a, b, sem in chunked
            ]

        def store(block):
            return [
                pltpu.make_async_copy(block_of(a, block, rows), block_of(b, block, rows), sem.at[block])
                for a, b, sem in ((gg_ref, gg_kept, keep_gg), (ug_ref, ug_kept, keep_ug))
            ]

        def work(chip, core):
            block = chip * 2 + core
            here = pl.ds(pl.multiple_of(block * rows, rows), rows)
            hidden_grad = dot(og_ref[here, :], down_ref[...], NT)
            gate_grad = (hidden_grad * one_ref[here, :].astype(jnp.float32)).astype(LOW)
            up_grad = (hidden_grad * two_ref[here, :].astype(jnp.float32)).astype(LOW)
            gg_ref[here, :] = gate_grad
            ug_ref[here, :] = up_grad
            for copy in store(block):
                copy.start()
            return dot(gate_grad, pair_ref[0]) + dot(up_grad, pair_ref[1])

        exchange = Exchange(place, staged, landed, sems)
        scatter = Scatter(place, work, scratch)
        fetches = fetch_all([(down_hbm, down_ref), (pair_hbm, pair_ref)], load)

        def begin(turn):
            for copy in bring(scatter.order(turn)):
                copy.start()

        each(chips, begin)
        late = pltpu.make_async_copy(hid_hbm, hid_ref, load.at[2])
        late.start()
        place.barrier(True)

        def fill(offset):
            block = lax.rem(place.group + offset, groups)
            columns = pl.ds(pl.multiple_of(block * part, part), part)
            staged[offset] = dot(hid_ref[...], og_ref[:, columns], TN).astype(LOW)

        def fill_send(offset):
            fill(offset)
            exchange.copy(offset).start()

        def brought(turn, _=0):
            for copy in bring(scatter.order(turn)):
                copy.wait()
            return 0

        def brought_once(turn):
            brought(turn)

        for copy in fetches:
            copy.wait()
        brought_once(0)
        scatter.first()
        pl.when(scatter.lag == 1)(functools.partial(brought_once, 1))

        def step(number):
            scatter.slot(number)

            @pl.when(number == 0)
            def _():
                lax.fori_loop(1 + scatter.lag, chips, brought, 0)
                late.wait()

            pieces(number, groups, fill_send)

        each(chips - 1, step)
        scatter.last()
        fill(0)
        exchange.stay().start()
        scatter.own(sum_ref)
        scatter.drain()
        exchange.wait()

        def stored(block):
            for copy in store(block):
                copy.wait()

        each(2 * chips, stored)

    hidden_shape = shape((length, hidden))
    return line_call(
        kernel,
        "scatter_hidden",
        4,
        (grads, hidden_low, *factors, down, pair_weight),
        [
            hidden_shape,
            hidden_shape,
            shape((rows, width), jnp.float32),
            shape((groups, hidden, part)),
        ],
        [
            pltpu.VMEM((length, width), LOW),
            *(pltpu.VMEM((length, hidden), LOW) for _ in range(3)),
            pltpu.VMEM(down.shape, LOW),
            pltpu.VMEM(pair_weight.shape, LOW),
            *(pltpu.VMEM((length, hidden), LOW) for _ in range(2)),
            pltpu.VMEM((groups, hidden, part), LOW),
            pltpu.SemaphoreType.DMA((3,)),
            *(pltpu.SemaphoreType.DMA((chips,)) for _ in range(3)),
            *(pltpu.SemaphoreType.DMA((2 * chips,)) for _ in range(2)),
        ]
        + Scatter.scratch(chips, rows, width)
        + Spread.scratch(groups),
        COST_FLOPS,
        in_hbm=(0, 1, 3),
        from_hbm=(0, 1, 2, 3, 4, 5),
    )


def gather_context(
    groups, chips, middle, normed_grad, out_grad, gain, shift, weight, hidden_low, down, normed, pair
):
    rows, width = middle.shape
    length = rows * 2 * chips
    out_width = weight.shape[0]
    hidden = down.shape[0]
    part = width // groups

    def kernel(
        mid_ref, ng_hbm, og_ref, gain_ref, shift_ref, w_hbm, hid_hbm, down_hbm, a_ref, gg_hbm, ug_hbm,
        kept, cg_ref, mg_ref, sums_ref, out_ref, landed,
        full, total, w_ref, hid_ref, down_ref, gg_ref, ug_ref, staged, columns_in, load, keep_sem, *rest
    ):
        place = Place(groups, chips)
        scratch, line, sems = split_refs(rest, Scatter.SCRATCH, Gather.SEMS, 2)

        def fetch(offset):
            block = lax.rem(place.group + offset, groups)
            columns = pl.ds(pl.multiple_of(block * part, part), part)
            slot = lax.rem(offset, 2)
            return pltpu.make_async_copy(a_ref.at[:, columns], columns_in.at[slot], load.at[slot])

        arrive = pltpu.make_async_copy(ng_hbm, total, load.at[3])
        arrive.start()
        late = [
            pltpu.make_async_copy(a, b, load.at[4 + n])
            for n, (a, b) in enumerate(
                (
                    (down_hbm, down_ref),
                    (hid_hbm, hid_ref),
                    (w_hbm, w_ref),
                    (gg_hbm, gg_ref),
                    (ug_hbm, ug_ref),
                )
            )
        ]
        for copy in late:
            copy.start()
        fetch(1).start()
        gather = Gather(place, full, line, kept, keep_sem)
        _, plain, inverse = layer_norm_parts(mid_ref[...], gain_ref[...], shift_ref[...])
        arrive.wait()
        back, gain_grad, shift_grad = layer_norm_back(total[...], plain, inverse, gain_ref[...])
        mid_grad = og_ref[...].astype(jnp.float32) + back
        total[...] = mid_grad
        keep = pltpu.make_async_copy(total, mg_ref, load.at[2])
        keep.start()
        gather.own()[...] = mid_grad.astype(LOW)
        place.barrier(True)
        gather.begin()
        sums_ref[0:1, :] = gain_grad[None, :]
        sums_ref[1:2, :] = shift_grad[None, :]

        def back_work(chip):
            here = pl.ds(pl.multiple_of(chip * 2 * rows, 2 * rows), 2 * rows)
            cg_ref[here, :] = dot(full[here, :], w_ref[...], NT).astype(LOW)

        def out_work(chip, core):
            here = pl.ds(pl.multiple_of((chip * 2 + core) * rows, rows), rows)
            return dot(hid_ref[here, :], down_ref[...])

        exchange = Exchange(place, staged, landed, sems)

        def fill(offset):
            fetch(offset).wait()
            pl.when(offset > 0)(lambda: fetch(lax.rem(offset + 1, groups)).start())
            values = columns_in[lax.rem(offset, 2)]
            staged[offset, 0] = dot(gg_ref[...], values, TN).astype(LOW)
            staged[offset, 1] = dot(ug_ref[...], values, TN).astype(LOW)

        def fill_send(offset):
            fill(offset)
            exchange.copy(offset).start()

        scatter = Scatter(place, out_work, scratch)
        late[0].wait()
        late[1].wait()
        scatter.first()
        for copy in late[2:]:
            copy.wait()

        def step(number):
            scatter.slot(number)
            pieces(number, groups, fill_send)
            gather.pass_on(number)

            @pl.when(number == 0)
            def _():
                gather.wait_chip(place.chip)
                back_work(place.chip)

            gather.each_new(number, back_work)

        each(chips - 1, step)
        scatter.last()
        fill(jnp.int32(0))
        exchange.stay().start()
        keep.wait()
        scatter.own(total)
        out_ref[...] = (mid_ref[...] + total[...]).astype(LOW)
        gather.drain()
        scatter.drain()
        exchange.wait()

    return line_call(
        kernel,
        "gather_context",
        5,
        (middle, normed_grad, out_grad, gain, shift, weight, hidden_low, down, normed, *pair),
        [
            shape((length, width)),
            shape((length, out_width)),
            shape((rows, width), jnp.float32),
            shape((2, width), jnp.float32),
            shape((rows, width)),
            shape((groups, 2, hidden, part)),
        ],
        [
            pltpu.VMEM((length, width), LOW),
            pltpu.VMEM((rows, width), jnp.float32),
            pltpu.VMEM(weight.shape, LOW),
            pltpu.VMEM((length, hidden), LOW),
            pltpu.VMEM(down.shape, LOW),
            pltpu.VMEM((length, hidden), LOW),
            pltpu.VMEM((length, hidden), LOW),
            pltpu.VMEM((groups, 2, hidden, part), LOW),
            pltpu.VMEM((2, length, part), LOW),
            pltpu.SemaphoreType.DMA((9,)),
            pltpu.SemaphoreType.DMA((chips,)),
        ]
        + Scatter.scratch(chips, rows, width)
        + Gather.scratch(chips)
        + Spread.scratch(groups),
        COST_FLOPS,
        in_hbm=(0, 2, 5),
        from_hbm=(1, 5, 6, 7, 8, 9, 10),
    )


def scatter_triple(
    groups, chips, triple, weights, tokens, gain, shift, mid_grad, sums, bias_sums, normed, context, grads
):
    length, in_width = triple[0].shape
    rows = length // (2 * chips)
    width = weights.shape[1]
    part = width // groups

    def kernel(
        q_ref, k_ref, v_ref, w_ref, gain_ref, shift_ref, sums_ref, bias_ref,
        x_hbm, mg_hbm, a_hbm, ctx_hbm, full_hbm,
        in_ref, small_ref, landed_qkv, landed_out,
        x_ref, mg_ref, a_ref, ctx_ref, full_ref, load,
        total, staged_qkv, staged_out, early_spots, early_groups, late_spots, late_groups, *rest
    ):
        place = Place(groups, chips)
        scratch, one, two, sums_sems = split_refs(rest, Scatter.SCRATCH, 2, 2, 8)
        fetches = fetch_all(
            [
                (a_hbm, a_ref),
                (ctx_hbm, ctx_ref),
                (full_hbm, full_ref),
                (x_hbm, x_ref),
                (mg_hbm, mg_ref),
            ],
            load,
        )
        place.barrier(True, True)
        spots, count = place.spot, 2 * chips
        early_a = SmallSum(early_spots, spots, count, place.fellow, sums_sems[0:2])
        early_b = SmallSum(early_groups, place.group, groups, place.peer, sums_sems[2:4])
        late_a = SmallSum(late_spots, spots, count, place.fellow, sums_sems[4:6])
        late_b = SmallSum(late_groups, place.group, groups, place.peer, sums_sems[6:8])

        def work(chip, core):
            here = pl.ds(pl.multiple_of((chip * 2 + core) * rows, rows), rows)
            term = dot(q_ref[here, :], w_ref[0], NT)
            term = term + dot(k_ref[here, :], w_ref[1], NT)
            return term + dot(v_ref[here, :], w_ref[2], NT)

        exchange_qkv = Exchange(place, staged_qkv, landed_qkv, one)
        exchange_out = Exchange(place, staged_out, landed_out, two)

        def fill(offset):
            block = lax.rem(place.group + offset, groups)
            columns = pl.ds(pl.multiple_of(block * part, part), part)
            values = a_ref[:, columns]
            for number, ref in enumerate((q_ref, k_ref, v_ref)):
                staged_qkv[offset, number] = dot(values, ref[...], TN).astype(LOW)
            staged_out[offset] = dot(ctx_ref[...], full_ref[:, columns], TN).astype(LOW)

        def fill_send(offset):
            fill(offset)
            exchange_qkv.copy(offset).start()
            exchange_out.copy(offset).start()

        scatter = Scatter(place, work, scratch)
        scatter.first()

        def step(number):
            scatter.slot(number)

            @pl.when(number == 0)
            def _():
                early_a.begin(sums_ref[...])
                for copy in fetches:
                    copy.wait()

            pieces(number, groups, fill_send)

            @pl.when(number == chips - 2)
            def _():
                early_groups[place.group] = jnp.zeros(early_groups.shape[1:], jnp.float32)
                early_groups[place.group, 4:7, 0:in_width] = bias_ref[0:3, :]
                early_groups[place.group, 0:2, :] = early_a.result()
                early_b.begin(early_groups[place.group])

        each(chips - 1, step)
        scatter.last()
        fill(0)
        exchange_qkv.stay().start()
        exchange_out.stay().start()
        _, plain, inverse = layer_norm_parts(
            x_ref[...].astype(jnp.float32), gain_ref[...], shift_ref[...]
        )
        scatter.own(total)
        back, gain_grad, shift_grad = layer_norm_back(total[...], plain, inverse, gain_ref[...])
        late_a.begin(jnp.concatenate([gain_grad[None, :], shift_grad[None, :]], axis=0))
        in_ref[...] = (mg_ref[...] + back).astype(LOW)
        scatter.drain()
        exchange_qkv.wait()
        exchange_out.wait()
        late_b.begin(late_a.result())
        first = early_b.result()
        last = late_b.result()
        small_ref[...] = first
        small_ref[1:2, :] = first[0:1, :]
        small_ref[3:4, :] = first[1:2, :]
        small_ref[0:1, :] = last[0:1, :]
        small_ref[2:3, :] = last[1:2, :]

    devices = 2 * chips
    return line_call(
        kernel,
        "scatter_triple",
        6,
        (*triple, weights, gain, shift, sums, bias_sums, tokens, mid_grad, normed, context, grads),
        [
            shape((rows, width)),
            shape((8, width), jnp.float32),
            shape((groups, 3, part, in_width)),
            shape((groups, in_width, part)),
        ],
        [
            pltpu.VMEM((rows, width), LOW),
            pltpu.VMEM((rows, width), jnp.float32),
            pltpu.VMEM((length, width), LOW),
            pltpu.VMEM((length, in_width), LOW),
            pltpu.VMEM((length, width), LOW),
            pltpu.SemaphoreType.DMA((5,)),
            pltpu.VMEM((rows, width), jnp.float32),
            pltpu.VMEM((groups, 3, part, in_width), LOW),
            pltpu.VMEM((groups, in_width, part), LOW),
            pltpu.VMEM((devices, 2, width), jnp.float32),
            pltpu.VMEM((groups, 8, width), jnp.float32),
            pltpu.VMEM((devices, 2, width), jnp.float32),
            pltpu.VMEM((groups, 2, width), jnp.float32),
        ]
        + Scatter.scratch(chips, rows, width)
        + Spread.scratch(groups) * 2
        + [pltpu.SemaphoreType.DMA((n,)) for n in (devices, devices, groups, groups) * 2],
        COST_FLOPS,
        in_hbm=(2, 3),
        from_hbm=(8, 9, 10, 11, 12),
    )


def adam_update(master, gradient, moment_one, moment_two, correct_one, correct_two, rate):
    one_new = 0.9 * moment_one + 0.1 * gradient
    two_new = 0.999 * moment_two + 0.001 * gradient * gradient
    change = one_new / correct_one / (jnp.sqrt(two_new / correct_two) + 1e-08) + 0.1 * master
    return (master - rate * change, one_new, two_new)


def per_device(
    groups,
    chips,
    inputs,
    out_grad,
    segments,
    w_qkv,
    w_out,
    w_gate_up,
    w_down,
    qkv_bias,
    norm_gain,
    norm_bias,
    first_qkv,
    first_out,
    first_gate_up,
    first_down,
    first_bias,
    first_gain,
    first_shift,
    second_qkv,
    second_out,
    second_gate_up,
    second_down,
    second_bias,
    second_gain,
    second_shift,
):
    length = segments.shape[1]
    head_width = w_qkv.shape[2]
    gains = (norm_gain[0:1], norm_gain[1:2])
    shifts = (norm_bias[0:1], norm_bias[1:2])
    place = positions(segments)[0]
    start = jnp.arange(length, dtype=jnp.int32) - place
    low_blocks = start[::BLK] // BLK
    start = start[None, :]
    tables = rotary_tables(place, min(head_width, 128))

    gate_up_turned = jnp.swapaxes(w_gate_up, 1, 2)
    normed_one_all, qkv_all, out_all, *qkv = gather_project(
        groups,
        chips,
        inputs,
        gains[0],
        shifts[0],
        (w_qkv, w_out),
        qkv_bias,
        tables,
    )
    middle, context_flat, lse, mlp_grad, pair_all = scatter_heads(
        groups, chips, qkv, start, out_all, inputs, out_grad, (gate_up_turned,)
    )
    normed_two_all, hidden_low, *factors, down_all = gather_hidden(
        groups, chips, middle, gains[1], shifts[1], pair_all, w_down
    )
    gate_grad, up_grad, normed_two_grad, parts_down = scatter_hidden(
        groups, chips, mlp_grad, hidden_low, factors, down_all, pair_all
    )
    attn_grad_all, context_grad, middle_grad, sums_two, outputs, parts_pair = (
        gather_context(
            groups,
            chips,
            middle,
            normed_two_grad,
            out_grad,
            gains[1],
            shifts[1],
            out_all,
            hidden_low,
            down_all,
            normed_two_all,
            (gate_grad, up_grad),
        )
    )
    *triple, bias_sums = attention_backward(
        low_blocks, *qkv, start, lse, context_flat, context_grad, tables
    )
    input_grad, small, parts_qkv, parts_out = scatter_triple(
        groups,
        chips,
        triple,
        qkv_all,
        inputs,
        gains[0],
        shifts[0],
        middle_grad,
        sums_two,
        bias_sums,
        normed_one_all,
        context_flat,
        attn_grad_all,
    )

    def add_parts(parts):
        total = parts[0].astype(jnp.float32)
        for offset in range(1, groups):
            total = total + parts[offset].astype(jnp.float32)
        return total

    grad_qkv, grad_out, grad_down = add_parts(parts_qkv), add_parts(parts_out), add_parts(parts_down)
    grad_gate_up = jnp.swapaxes(add_parts(parts_pair), 1, 2)
    grad_bias = small[4:7, :head_width]
    grad_gain, grad_shift = small[0:2], small[2:4]
    correct_one = 1.0 - 0.9**STEP
    correct_two = 1.0 - 0.999**STEP
    rates = (0.02, 0.3, 0.02, 0.02, 0.3, 0.3, 0.3)
    masters = (w_qkv, w_out, w_gate_up, w_down, qkv_bias, norm_gain, norm_bias)
    gradients = (grad_qkv, grad_out, grad_gate_up, grad_down, grad_bias, grad_gain, grad_shift)
    firsts = (first_qkv, first_out, first_gate_up, first_down, first_bias, first_gain, first_shift)
    seconds = (
        second_qkv,
        second_out,
        second_gate_up,
        second_down,
        second_bias,
        second_gain,
        second_shift,
    )
    updated = [
        adam_update(
            masters[number],
            gradients[number],
            firsts[number],
            seconds[number],
            correct_one,
            correct_two,
            rates[number],
        )
        for number in range(7)
    ]
    return (
        outputs,
        input_grad,
        grad_qkv,
        grad_out,
        grad_gate_up,
        grad_down,
        grad_bias,
        grad_gain,
        grad_shift,
        updated[0][0],
        updated[1][0],
        updated[2][0],
        updated[3][0],
        updated[4][0],
        updated[5][0],
        updated[6][0],
        updated[0][1],
        updated[1][1],
        updated[2][1],
        updated[3][1],
        updated[4][1],
        updated[5][1],
        updated[6][1],
        updated[0][2],
        updated[1][2],
        updated[2][2],
        updated[3][2],
        updated[4][2],
        updated[5][2],
        updated[6][2],
    )


def solution(mesh):
    in_specs = (
        P(("dp", "tensor"), None),
        P(("dp", "tensor"), None),
        P("dp", None),
        P(None, "dp", "tensor"),
        P("tensor", "dp"),
        P(None, "dp", "tensor"),
        P("tensor", "dp"),
        P(None, "tensor"),
        P(),
        P(),
        P(None, "dp", "tensor"),
        P("tensor", "dp"),
        P(None, "dp", "tensor"),
        P("tensor", "dp"),
        P(None, "tensor"),
        P(),
        P(),
        P(None, "dp", "tensor"),
        P("tensor", "dp"),
        P(None, "dp", "tensor"),
        P("tensor", "dp"),
        P(None, "tensor"),
        P(),
        P(),
    )
    out_specs = (
        P(("dp", "tensor"), None),
        P(("dp", "tensor"), None),
        P(None, "dp", "tensor"),
        P("tensor", "dp"),
        P(None, "dp", "tensor"),
        P("tensor", "dp"),
        P(None, "tensor"),
        P(),
        P(),
        P(None, "dp", "tensor"),
        P("tensor", "dp"),
        P(None, "dp", "tensor"),
        P("tensor", "dp"),
        P(None, "tensor"),
        P(),
        P(),
        P(None, "dp", "tensor"),
        P("tensor", "dp"),
        P(None, "dp", "tensor"),
        P("tensor", "dp"),
        P(None, "tensor"),
        P(),
        P(),
        P(None, "dp", "tensor"),
        P("tensor", "dp"),
        P(None, "dp", "tensor"),
        P("tensor", "dp"),
        P(None, "tensor"),
        P(),
        P(),
    )
    return jax.shard_map(
        functools.partial(per_device, mesh.shape["dp"], mesh.shape["tensor"] // 2),
        mesh=mesh, in_specs=in_specs, out_specs=out_specs, check_vma=False
    )
```

```python
import functools

import jax
import jax.numpy as jnp
from jax import lax
from jax.experimental import pallas as pl
from jax.experimental.pallas import tpu as pltpu
from jax.sharding import PartitionSpec as P

HD = 64
ROT = 16
STEP = 10


def layer_norm_parts(values, gain_row, shift_row):
    average = jnp.mean(values, axis=-1, keepdims=True)
    centred = values - average
    inverse = lax.rsqrt(jnp.mean(centred * centred, axis=-1, keepdims=True) + 1e-05)
    normed = centred * inverse
    return (normed * gain_row + shift_row, normed, inverse)


def layer_norm_back(incoming, normed, inverse, gain_row):
    scaled = incoming * gain_row
    inner = (
        scaled
        - jnp.mean(scaled, axis=-1, keepdims=True)
        - normed * jnp.mean(scaled * normed, axis=-1, keepdims=True)
    )
    return (inner * inverse, jnp.sum(incoming * normed, axis=0), jnp.sum(incoming, axis=0))


def positions(segment_ids):
    length = segment_ids.shape[-1]
    indices = jnp.broadcast_to(jnp.arange(length, dtype=jnp.int32), segment_ids.shape)
    before = jnp.concatenate(
        [jnp.full(segment_ids.shape[:-1] + (1,), -1, jnp.int32), segment_ids[..., :-1]], axis=-1
    )
    starts = lax.cummax(jnp.where(segment_ids != before, indices, 0), axis=segment_ids.ndim - 1)
    return indices - starts


def rotary_tables(position_ids, width):
    half_rot = ROT // 2
    frequency = 10000.0 ** (-(2.0 * jnp.arange(half_rot, dtype=jnp.float32)) / ROT)
    angles = position_ids.astype(jnp.float32)[:, None] * frequency
    cosine, sine = jnp.cos(angles), jnp.sin(angles)
    zeros = jnp.zeros((angles.shape[0], HD - ROT), jnp.float32)
    blank = jnp.zeros_like(sine)
    copies = width // HD
    return tuple(
        jnp.tile(jnp.concatenate(parts, axis=1), (1, copies))
        for parts in (
            (cosine, cosine, zeros + 1.0),
            (-sine, blank, zeros),
            (blank, sine, zeros),
        )
    )


NEG = -1e30
BLK = 256
NT = (((1,), (1,)), ((), ()))
NN = (((1,), (0,)), ((), ()))


def dot(left, right, dims=NN, precision=None):
    return lax.dot_general(
        left, right, dims, preferred_element_type=jnp.float32, precision=precision
    )


def head_masks(width, dtype):
    lane = lax.broadcasted_iota(jnp.int32, (1, width), 1)
    return [(lane // HD == h).astype(dtype) for h in range(width // HD)]


def rope_tile(tile, cosine, sine_low, sine_high, sign):
    width = tile.shape[-1]
    ahead = pltpu.roll(tile, width - ROT // 2, 1)
    behind = pltpu.roll(tile, ROT // 2, 1)
    return tile * cosine + sign * (ahead * sine_low + behind * sine_high)


def attend(number, size, k_ref, v_turned, masked, starts, query_ids, acc, stats):
    base = pl.multiple_of(number * size, size)
    keys = k_ref[pl.ds(base, size), :]
    key_ids = base + lax.broadcasted_iota(jnp.int32, (size, size), 0)
    visible = (key_ids >= starts) & (key_ids <= query_ids)
    for h, queries in enumerate(masked):
        scores = jnp.where(visible, dot(keys, queries, NT), NEG)
        peak_old = stats[h : h + 1, :]
        peak = jnp.maximum(peak_old, jnp.max(scores, axis=0, keepdims=True))
        fade = jnp.exp(peak_old - peak)
        prob = jnp.exp(scores - peak)
        stats[h : h + 1, :] = peak
        stats[8 + h : 9 + h, :] = stats[8 + h : 9 + h, :] * fade + jnp.sum(
            prob, axis=0, keepdims=True
        )
        band = slice(h * HD, (h + 1) * HD)
        acc[band, :] = acc[band, :] * fade + dot(
            v_turned[band, pl.ds(base, size)], prob.astype(jnp.bfloat16)
        )


def backward_kernel(
    low_ref,
    q_ref,
    k_ref,
    v_ref,
    start_ref,
    lse_ref,
    ctx_ref,
    grad_ref,
    cos_ref,
    sin_low_ref,
    sin_high_ref,
    dq_ref,
    dk_ref,
    dv_ref,
    bias_ref,
    k_turned,
    dq_acc,
    dk_acc,
    dv_acc,
):
    block = pl.program_id(0)
    last = pl.num_programs(0) - 1
    length, width = k_ref.shape
    heads = width // HD
    tile = min(width, 128)

    @pl.when(block == 0)
    def _():
        for part in range(length // BLK):
            rows = slice(part * BLK, (part + 1) * BLK)
            k_turned[:, rows] = k_ref[rows, :].T
        dk_acc[...] = jnp.zeros_like(dk_acc)
        dv_acc[...] = jnp.zeros_like(dv_acc)
        bias_ref[...] = jnp.zeros_like(bias_ref)

    here = pl.ds(pl.multiple_of(block * BLK, BLK), BLK)
    masks = head_masks(width, jnp.bfloat16)
    queries = (q_ref[here, :] * 0.125).astype(jnp.bfloat16)
    masked = [queries * m for m in masks]
    grads = grad_ref[...]
    grads_masked = [grads * m for m in masks]
    product = grads.astype(jnp.float32) * ctx_ref[...].astype(jnp.float32)
    select = (
        lax.broadcasted_iota(jnp.int32, (8, width), 1) // HD
        == lax.broadcasted_iota(jnp.int32, (8, width), 0)
    ).astype(jnp.float32)
    delta = dot(select, product, NT, lax.Precision.HIGHEST)
    start = start_ref[...]
    query_ids = block * BLK + lax.broadcasted_iota(jnp.int32, (1, BLK), 1)
    dq_acc[...] = jnp.zeros_like(dq_acc)

    def step(number, _):
        base = pl.multiple_of(number * BLK, BLK)
        rows_k = pl.ds(base, BLK)
        keys = k_ref[rows_k, :]
        vals = v_ref[rows_k, :]
        key_ids = base + lax.broadcasted_iota(jnp.int32, (BLK, BLK), 0)
        visible = (key_ids >= start) & (key_ids <= query_ids)
        dk = dk_acc[rows_k, :]
        dv = dv_acc[rows_k, :]
        for h in range(heads):
            scores = dot(keys, masked[h], NT)
            prob = jnp.where(visible, jnp.exp(scores - lse_ref[h : h + 1, :]), 0.0)
            dprob = dot(vals, grads_masked[h], NT)
            dscore = (prob * (dprob - delta[h : h + 1, :])).astype(jnp.bfloat16)
            dv = dv + dot(prob.astype(jnp.bfloat16), grads_masked[h])
            dk = dk + dot(dscore, masked[h])
            rows = slice(h * HD, (h + 1) * HD)
            dq_acc[rows, :] += dot(k_turned[rows, rows_k], dscore)
        dk_acc[rows_k, :] = dk
        dv_acc[rows_k, :] = dv
        return 0

    lax.fori_loop(low_ref[block], block + 1, step, 0)

    def turn_back(values, rows):
        parts = []
        for t in range(width // tile):
            parts.append(
                rope_tile(
                    values[:, t * tile : (t + 1) * tile],
                    cos_ref[rows, :],
                    sin_low_ref[rows, :],
                    sin_high_ref[rows, :],
                    -1.0,
                )
            )
        return jnp.concatenate(parts, axis=1) if len(parts) > 1 else parts[0]

    dq = turn_back(dq_acc[...].T * 0.125, here).astype(jnp.bfloat16)
    dq_ref[...] = dq
    bias_ref[0:1, :] += jnp.sum(dq.astype(jnp.float32), axis=0, keepdims=True)

    @pl.when(block == last)
    def _():
        def finish(part, _):
            rows = pl.ds(pl.multiple_of(part * BLK, BLK), BLK)
            dk = turn_back(dk_acc[rows, :], rows).astype(jnp.bfloat16)
            dv = dv_acc[rows, :].astype(jnp.bfloat16)
            dk_ref[rows, :] = dk
            dv_ref[rows, :] = dv
            bias_ref[1:2, :] += jnp.sum(dk.astype(jnp.float32), axis=0, keepdims=True)
            bias_ref[2:3, :] += jnp.sum(dv.astype(jnp.float32), axis=0, keepdims=True)
            return 0

        lax.fori_loop(0, length // BLK, finish, 0)


def attention_backward(low_blocks, queries, keys, values, start, lse, context, grads, tables):
    length, width = queries.shape
    whole = pl.BlockSpec((length, width), lambda i, low: (0, 0))
    rows = pl.BlockSpec((BLK, width), lambda i, low: (i, 0))
    table = pl.BlockSpec(tables[0].shape, lambda i, low: (0, 0))
    return pl.pallas_call(
        backward_kernel,
        grid_spec=pltpu.PrefetchScalarGridSpec(
            num_scalar_prefetch=1,
            grid=(length // BLK,),
            in_specs=[
                whole,
                whole,
                whole,
                pl.BlockSpec((1, BLK), lambda i, low: (0, i)),
                pl.BlockSpec((8, BLK), lambda i, low: (0, i)),
                rows,
                rows,
                table,
                table,
                table,
            ],
            out_specs=[rows, whole, whole, pl.BlockSpec((8, width), lambda i, low: (0, 0))],
            scratch_shapes=[
                pltpu.VMEM((width, length), jnp.bfloat16),
                pltpu.VMEM((width, BLK), jnp.float32),
                pltpu.VMEM((length, width), jnp.float32),
                pltpu.VMEM((length, width), jnp.float32),
            ],
        ),
        out_shape=[jax.ShapeDtypeStruct((length, width), jnp.bfloat16)] * 3
        + [jax.ShapeDtypeStruct((8, width), jnp.float32)],
        compiler_params=pltpu.CompilerParams(vmem_limit_bytes=40 << 20),
        name="attention_backward",
    )(low_blocks, queries, keys, values, start, lse, context, grads, *tables)


MESH = pl.DeviceIdType.MESH
VMEM_BYTES = 62 << 20
LONGEST = 1024
TN = (((0,), (0,)), ((), ()))
LOW = jnp.bfloat16


def remote(source, target, send, receive, device):
    return pltpu.make_async_remote_copy(
        src_ref=source,
        dst_ref=target,
        send_sem=send,
        recv_sem=receive,
        device_id=device,
        device_id_type=MESH,
    )


class Place:
    def __init__(self, groups, chips):
        self.groups, self.chips = groups, chips
        self.group = lax.axis_index("dp")
        self.spot = lax.axis_index("tensor")
        self.chip, self.core = self.spot // 2, self.spot % 2

    def at(self, chip, core):
        return (self.group, chip * 2 + core)

    def peer(self, offset):
        return (lax.rem(self.group + offset, self.groups), self.spot)

    def fellow(self, offset):
        return (self.group, lax.rem(self.spot + offset, 2 * self.chips))

    def barrier(self, with_groups=False, with_all_spots=False):
        semaphore = pltpu.get_barrier_semaphore()

        def greet(target):
            pl.semaphore_signal(semaphore, inc=1, device_id=target, device_id_type=MESH)

        if with_all_spots:
            for offset in range(1, 2 * self.chips):
                greet(self.fellow(offset))
            count = 2 * self.chips - 1
        else:
            greet(self.at(self.chip, 1 - self.core))
            pl.when(self.chip > 0)(lambda: greet(self.at(self.chip - 1, self.core)))
            pl.when(self.chip < self.chips - 1)(lambda: greet(self.at(self.chip + 1, self.core)))
            count = 1 + jnp.where(self.chip > 0, 1, 0) + jnp.where(self.chip < self.chips - 1, 1, 0)
        if with_groups:
            for offset in range(1, self.groups):
                greet(self.peer(offset))
            count = count + self.groups - 1
        pl.semaphore_wait(semaphore, count)


def each(count, use):
    def one(index, _):
        use(index)
        return 0

    lax.fori_loop(0, count, one, 0)


def block_of(ref, index, size):
    return ref.at[pl.ds(pl.multiple_of(index * size, size), size)]


def fetch_all(pairs, sems):
    copies = [pltpu.make_async_copy(a, b, sems.at[n]) for n, (a, b) in enumerate(pairs)]
    for copy in copies:
        copy.start()
    return copies


HALVES = 2


class Gather:
    SEMS = 5

    def __init__(self, place, full, sems, kept=None, keep_sem=None):
        self.place, self.full, self.kept, self.keep_sem = place, full, kept, keep_sem
        self.line_in, self.core_in, self.right_out, self.left_out, self.core_out = sems
        self.rows = full.shape[0] // (2 * place.chips)

    @classmethod
    def scratch(cls, chips):
        return [pltpu.SemaphoreType.DMA((chips * HALVES,)) for _ in range(cls.SEMS)]

    def own(self):
        return block_of(self.full, self.place.spot, self.rows)

    def block(self, chip, core, half):
        return block_of(self.full, (chip * 2 + core) * HALVES + half, self.rows // HALVES)

    def right(self, which, half):
        place, part = self.place, self.block(which, self.place.core, half)
        target = place.at(jnp.minimum(place.chip + 1, place.chips - 1), place.core)
        index = which * HALVES + half
        return remote(part, part, self.right_out.at[index], self.line_in.at[index], target)

    def left(self, which, half):
        place, part = self.place, self.block(which, self.place.core, half)
        target = place.at(jnp.maximum(place.chip - 1, 0), place.core)
        index = which * HALVES + half
        return remote(part, part, self.left_out.at[index], self.line_in.at[index], target)

    def across(self, which, core, half):
        place, part = self.place, self.block(which, core, half)
        target = place.at(place.chip, 1 - place.core)
        index = which * HALVES + half
        return remote(part, part, self.core_out.at[index], self.core_in.at[index], target)

    def begin(self, halves=range(HALVES)):
        chip, chips = self.place.chip, self.place.chips
        for half in halves:
            pl.when(chip < chips - 1)(lambda: self.right(chip, half).start())
            pl.when(chip > 0)(lambda: self.left(chip, half).start())
        for half in halves:
            self.across(chip, self.place.core, half).start()

    def pass_on(self, step, halves=range(HALVES)):
        chip, chips, core = self.place.chip, self.place.chips, self.place.core
        low, high = chip - 1 - step, chip + 1 + step
        for half in halves:

            @pl.when(low >= 0)
            def _():
                self.right(low, half).wait_recv()
                pl.when(chip < chips - 1)(lambda: self.right(low, half).start())
                self.across(low, core, half).start()

            @pl.when(high < chips)
            def _():
                self.left(high, half).wait_recv()
                pl.when(chip > 0)(lambda: self.left(high, half).start())
                self.across(high, core, half).start()

    def keep(self, which):
        part = block_of(self.full, which, 2 * self.rows)
        return pltpu.make_async_copy(
            part, block_of(self.kept, which, 2 * self.rows), self.keep_sem.at[which]
        )

    def wait_chip(self, which, halves=range(HALVES)):
        for half in halves:
            self.across(which, 1 - self.place.core, half).wait_recv()
        if self.kept is not None and HALVES - 1 in halves:
            self.keep(which).start()

    def each_new(self, step, use, halves=range(HALVES)):
        low, high = self.place.chip - 1 - step, self.place.chip + 1 + step

        @pl.when(low >= 0)
        def _():
            self.wait_chip(low, halves)
            use(low)

        @pl.when(high < self.place.chips)
        def _():
            self.wait_chip(high, halves)
            use(high)

    def drain(self):
        chip, chips, core = self.place.chip, self.place.chips, self.place.core

        def one(which):
            for half in range(HALVES):
                self.across(which, core, half).wait_send()
                pl.when((which <= chip) & (chip < chips - 1))(
                    lambda: self.right(which, half).wait_send()
                )
                pl.when((which >= chip) & (chip > 0))(lambda: self.left(which, half).wait_send())
            if self.kept is not None:
                self.keep(which).wait()

        each(chips, one)


class Scatter:
    def __init__(self, place, work, scratch, halves=HALVES):
        self.place, self.work, self.halves = place, work, halves
        self.out, self.side, self.line = scratch[:3]
        self.core_out, self.core_in, self.line_out, self.line_in = scratch[3:]
        self.part = self.out.shape[1] // halves
        chip, chips = place.chip, place.chips
        self.near = jnp.minimum(chip, chips - 1 - chip)
        self.alone = chips - 1 - 2 * self.near
        self.flip = jnp.where(chip * 2 < chips, 0, 1)
        self.lag = jnp.where(self.near > 0, 1, 0)

    @staticmethod
    def scratch(chips, rows, width):
        return [
            pltpu.VMEM((chips, rows, width), LOW),
            pltpu.VMEM((chips, rows, width), LOW),
            pltpu.VMEM((chips + 1, rows, width), LOW),
            pltpu.SemaphoreType.DMA((chips,)),
            pltpu.SemaphoreType.DMA((chips,)),
            pltpu.SemaphoreType.DMA((chips * HALVES,)),
            pltpu.SemaphoreType.DMA(((chips + 1) * HALVES,)),
        ]

    SCRATCH = 7

    def order(self, turn):
        chips = self.place.chips
        later = jnp.maximum(turn - self.alone, 0)
        pair = later // 2
        far = jnp.where(turn < self.alone, chips - 1 - turn, chips - 1 - self.alone - pair)
        which = jnp.where((turn >= self.alone) & (later % 2 == 1), pair, far)
        which = jnp.where(turn == chips - 1, self.near, which)
        return jnp.where(self.flip == 1, chips - 1 - which, which)

    def across(self, which):
        place = self.place
        return remote(
            self.out.at[which],
            self.side.at[which],
            self.core_out.at[which],
            self.core_in.at[which],
            place.at(place.chip, 1 - place.core),
        )

    def hop(self, which, slot, half, target):
        rows = slice(half * self.part, (half + 1) * self.part)
        return remote(
            self.out.at[which, rows],
            self.line.at[slot, rows],
            self.line_out.at[which * self.halves + half],
            self.line_in.at[slot * self.halves + half],
            self.place.at(target, self.place.core),
        )

    def right(self, which, half):
        place = self.place
        slot = jnp.where(which == place.chip + 1, place.chips, which)
        return self.hop(which, slot, half, jnp.minimum(place.chip + 1, place.chips - 1))

    def left(self, which, half):
        return self.hop(which, which, half, jnp.maximum(self.place.chip - 1, 0))

    def arrived(self, slot, half):
        place = self.place
        rows = slice(half * self.part, (half + 1) * self.part)
        part = self.line.at[slot, rows]
        other = place.at(place.chip, 1 - place.core)
        remote(
            part, part, self.line_out.at[0], self.line_in.at[slot * self.halves + half], other
        ).wait_recv()
        return self.line[slot, rows].astype(jnp.float32)

    def produce(self, turn):
        which = self.order(turn)
        self.out[which] = self.work(which, 1 - self.place.core).astype(LOW)
        self.across(which).start()

    def chip_sum(self, which):
        mine = self.work(which, self.place.core)
        self.across(which).wait()
        return mine + self.side[which].astype(jnp.float32)

    def send(self, which, upstream, copy):
        total = self.chip_sum(which)

        @pl.when(upstream)
        def _():
            for half in range(self.halves):
                rows = slice(half * self.part, (half + 1) * self.part)
                self.out[which, rows] = (total[rows] + self.arrived(which, half)).astype(LOW)
                copy(which, half).start()

        @pl.when(jnp.logical_not(upstream))
        def _():
            for half in range(self.halves):
                rows = slice(half * self.part, (half + 1) * self.part)
                self.out[which, rows] = total[rows].astype(LOW)
                copy(which, half).start()

    def first(self):
        pl.when(self.lag == 1)(lambda: self.produce(0))

    def slot(self, number):
        chip, chips = self.place.chip, self.place.chips
        self.produce(number + self.lag)
        right = chips - 1 - (number - chip)
        left = number - (chips - 1 - chip)
        pl.when((number >= chip) & (right > chip))(
            lambda: self.send(right, chip > 0, self.right)
        )
        pl.when((left >= 0) & (left < chip))(
            lambda: self.send(left, chip < chips - 1, self.left)
        )

    def last(self):
        pl.when(self.lag == 0)(lambda: self.produce(self.place.chips - 1))

    def own(self, total):
        chip, chips = self.place.chip, self.place.chips
        total[...] = self.chip_sum(chip)
        for half in range(self.halves):
            rows = slice(half * self.part, (half + 1) * self.part)

            @pl.when(chip > 0)
            def _():
                total[rows] += self.arrived(chips, half)

            @pl.when(chip < chips - 1)
            def _():
                total[rows] += self.arrived(chip, half)

    def drain(self):
        chip = self.place.chip

        def one(which):
            for half in range(self.halves):
                pl.when(which > chip)(lambda: self.right(which, half).wait_send())
                pl.when(which < chip)(lambda: self.left(which, half).wait_send())

        each(self.place.chips, one)


class StoredScatter(Scatter):
    def __init__(self, place, scratch, mine):
        super().__init__(place, None, scratch, 1)
        self.mine = mine

    def put(self, which, other, own):
        self.out[which] = other.astype(LOW)
        self.across(which).start()
        self.mine[which] = own.astype(LOW)

    def produce(self, turn):
        pass

    def chip_sum(self, which):
        self.across(which).wait()
        return self.mine[which].astype(jnp.float32) + self.side[which].astype(jnp.float32)


class Spread:
    def __init__(self, place, shard, staged, whole, axis, sems):
        self.place, self.staged, self.whole, self.sems = place, staged, whole, sems
        size = shard.shape[axis]
        here = pl.ds(pl.multiple_of(place.group * size, size), size)
        self.mine = whole.at[tuple(here if a == axis else slice(None) for a in range(len(shard.shape)))]
        staged[...] = shard[...].astype(LOW)

    @staticmethod
    def scratch(groups):
        return [pltpu.SemaphoreType.DMA((groups,)), pltpu.SemaphoreType.DMA((groups,))]

    def copy(self, offset):
        return remote(
            self.staged,
            self.mine,
            self.sems[0].at[offset],
            self.sems[1].at[offset],
            self.place.peer(offset),
        )

    def stay(self):
        return pltpu.make_async_copy(self.staged, self.mine, self.sems[0].at[0])

    def start(self):
        for offset in range(1, self.place.groups):
            self.copy(offset).start()
        self.stay().start()

    def wait(self):
        for offset in range(1, self.place.groups):
            self.copy(offset).wait()
        self.stay().wait()


class Exchange:
    def __init__(self, place, staged, landed, sems):
        self.place, self.staged, self.landed = place, staged, landed
        self.send, self.receive = sems

    def copy(self, offset):
        return remote(
            self.staged.at[offset],
            self.landed.at[offset],
            self.send.at[offset],
            self.receive.at[offset],
            self.place.peer(offset),
        )

    def stay(self):
        return pltpu.make_async_copy(self.staged.at[0], self.landed.at[0], self.send.at[0])

    def wait(self):
        def one(offset, _):
            self.copy(offset).wait()
            return 0

        lax.fori_loop(1, self.place.groups, one, 0)
        self.stay().wait()


class SmallSum:
    def __init__(self, slots, me, count, target, sems):
        self.slots, self.me, self.count, self.target = slots, me, count, target
        self.send, self.receive = sems

    def copy(self, offset):
        part = self.slots.at[self.me]
        return remote(
            part, part, self.send.at[offset], self.receive.at[self.me], self.target(offset)
        )

    def begin(self, rows):
        self.slots[self.me] = rows
        for offset in range(1, self.count):
            self.copy(offset).start()

    def result(self):
        for offset in range(1, self.count):
            source = lax.rem(self.me + offset, self.count)
            part = self.slots.at[source]
            remote(
                part, part, self.send.at[offset], self.receive.at[source], self.target(offset)
            ).wait_recv()
        total = self.slots[0]
        for index in range(1, self.count):
            total = total + self.slots[index]
        for offset in range(1, self.count):
            self.copy(offset).wait_send()
        return total


def pieces(number, groups, fill):
    @pl.when(number == 0)
    def _():
        each(groups - 1, lambda index: fill(index + 1))


def line_call(kernel, name, number, operands, out_shape, scratch, flops, in_hbm=(), from_hbm=()):
    whole, hbm = pl.BlockSpec(memory_space=pltpu.VMEM), pl.BlockSpec(memory_space=pl.ANY)
    ins = [hbm if n in from_hbm else whole for n in range(len(operands))]
    outs = [hbm if n in in_hbm else whole for n in range(len(out_shape))]
    return pl.pallas_call(
        kernel,
        out_shape=out_shape,
        in_specs=ins,
        out_specs=outs,
        scratch_shapes=scratch,
        compiler_params=pltpu.CompilerParams(
            collective_id=number, has_side_effects=True, vmem_limit_bytes=VMEM_BYTES
        ),
        cost_estimate=pl.CostEstimate(flops=flops, bytes_accessed=0, transcendentals=0),
        name=name,
    )(*operands)


COST_FLOPS = 80_000_000_000


def shape(dims, kind=LOW):
    return jax.ShapeDtypeStruct(dims, kind)


def split_refs(refs, *counts):
    parts, at = [], 0
    for count in counts:
        parts.append(refs[at : at + count])
        at += count
    return parts


def gather_project(groups, chips, tokens, gain, shift, shards, bias, tables):
    rows, width = tokens.shape
    length = rows * 2 * chips
    qkv_shard, out_shard, down_shard = shards
    part, out_width = qkv_shard.shape[1:]
    upper = down_shard.shape[0] // 2
    tile = tables[0].shape[1]

    def kernel(
        x_ref, gain_ref, shift_ref, qkv_ref, out_ref, down_ref, bias_ref,
        cos_hbm, sin_low_hbm, sin_high_hbm,
        kept, weights_kept, out_whole, down_whole, q_ref, k_ref, v_ref,
        full, weights, qkv_staged, out_staged, down_staged, cos_ref, sin_low_ref, sin_high_ref,
        load, keep_sem, *sems
    ):
        place = Place(groups, chips)
        fetches = fetch_all(
            [(cos_hbm, cos_ref), (sin_low_hbm, sin_low_ref), (sin_high_hbm, sin_high_ref)], load
        )
        line, one, two, three = split_refs(sems, Gather.SEMS, 2, 2, 2)
        gather = Gather(place, full, line, kept, keep_sem)
        normed, _, _ = layer_norm_parts(
            x_ref[...].astype(jnp.float32), gain_ref[...], shift_ref[...]
        )
        gather.own()[...] = normed.astype(LOW)
        spread_qkv = Spread(place, qkv_ref, qkv_staged, weights, 1, one)
        place.barrier(True)
        gather.begin()
        spread_qkv.start()
        spread_out = Spread(place, out_ref, out_staged, out_whole, 1, two)
        spread_out.start()
        spread_down = Spread(place, down_ref.at[0:upper], down_staged, down_whole, 1, three)
        spread_down.start()

        def work(chip):
            base = pl.multiple_of(chip * 2 * rows, 2 * rows)
            here = pl.ds(base, 2 * rows)
            values = full[here, :]
            for number, ref in enumerate((q_ref, k_ref, v_ref)):
                result = dot(values, weights[number]) + bias_ref[number : number + 1, :]
                if number < 2:
                    parts = [
                        rope_tile(
                            result[:, t * tile : (t + 1) * tile],
                            cos_ref[here, :],
                            sin_low_ref[here, :],
                            sin_high_ref[here, :],
                            1.0,
                        )
                        for t in range(out_width // tile)
                    ]
                    result = jnp.concatenate(parts, axis=1) if len(parts) > 1 else parts[0]
                ref[here, :] = result.astype(LOW)

        gather.pass_on(0)
        for copy in fetches:
            copy.wait()
        spread_qkv.wait()
        weights_keep = pltpu.make_async_copy(weights, weights_kept, load.at[3])
        weights_keep.start()
        gather.wait_chip(place.chip)
        work(place.chip)

        def step(number):
            pl.when(number > 0)(lambda: gather.pass_on(number))
            gather.each_new(number, work)

        each(chips - 1, step)
        weights_keep.wait()
        spread_out.wait()
        spread_down.wait()
        gather.drain()

    head_shape = shape((length, out_width))
    return line_call(
        kernel,
        "gather_project",
        1,
        (tokens, gain, shift, *shards, bias, *tables),
        [
            shape((length, width)),
            shape((3, width, out_width)),
            shape((out_width, width)),
            shape((upper, width)),
            head_shape,
            head_shape,
            head_shape,
        ],
        [
            pltpu.VMEM((length, width), LOW),
            pltpu.VMEM((3, width, out_width), LOW),
            pltpu.VMEM(qkv_shard.shape, LOW),
            pltpu.VMEM(out_shard.shape, LOW),
            pltpu.VMEM((upper, down_shard.shape[1]), LOW),
            *(pltpu.VMEM((length, tile), jnp.float32) for _ in range(3)),
            pltpu.SemaphoreType.DMA((4,)),
            pltpu.SemaphoreType.DMA((chips,)),
        ]
        + Gather.scratch(chips)
        + Spread.scratch(groups) * 3,
        COST_FLOPS,
        in_hbm=(0, 1, 2, 3),
        from_hbm=(7, 8, 9),
    )


def scatter_heads(groups, chips, qkv, start, weight, tokens, grads, shards):
    rows, width = tokens.shape
    length, head_width = qkv[0].shape
    heads = head_width // HD
    pair_shard, down_shard = shards
    upper = down_shard.shape[0] // 2

    def kernel(
        q_hbm, k_hbm, v_hbm, w_hbm, x_hbm, og_hbm, start_ref, pair_ref, down_ref,
        mid_ref, ctx_ref, lse_ref, kept, pair_whole, down_whole,
        full, q_ref, k_ref, v_ref, w_ref, x_ref, pair_staged, down_staged,
        load, keep_sem, v_turned, acc, stats, *rest
    ):
        place = Place(groups, chips)
        scratch, line, one, two = split_refs(rest, Scatter.SCRATCH, Gather.SEMS, 2, 2)
        gather = Gather(place, full, line, kept, keep_sem)
        fetches = fetch_all(
            [
                (og_hbm, gather.own()),
                (k_hbm, k_ref),
                (v_hbm, v_ref),
                (q_hbm, q_ref),
                (w_hbm, w_ref),
                (x_hbm, x_ref),
            ],
            load,
        )
        place.barrier(True)
        fetches[0].wait()
        gather.begin()
        spread_pair = Spread(place, pair_ref, pair_staged, pair_whole, 2, one)
        spread_pair.start()
        spread_down = Spread(place, down_ref.at[upper:], down_staged, down_whole, 1, two)
        spread_down.start()
        for copy in fetches[1:5]:
            copy.wait()
        for part in range(length // BLK):
            here = slice(part * BLK, (part + 1) * BLK)
            v_turned[:, here] = v_ref[here, :].T
        masks = head_masks(head_width, LOW)

        def work(chip, core):
            block = chip * 2 + core
            base = pl.multiple_of(block * rows, rows)
            here = pl.ds(base, rows)
            values = (q_ref[here, :] * 0.125).astype(LOW)
            masked = [values * m for m in masks]
            starts = start_ref[:, here]
            query_ids = base + lax.broadcasted_iota(jnp.int32, (1, rows), 1)
            acc[...] = jnp.zeros_like(acc)
            stats[0:8, :] = jnp.full((8, rows), NEG, jnp.float32)
            stats[8:16, :] = jnp.zeros((8, rows), jnp.float32)

            def step(number, _):
                attend(number, rows, k_ref, v_turned, masked, starts, query_ids, acc, stats)
                return 0

            lax.fori_loop(jnp.maximum(block - LONGEST // rows, 0), block + 1, step, 0)
            for h in range(heads):
                band = slice(h * HD, (h + 1) * HD)
                acc[band, :] = acc[band, :] / stats[8 + h : 9 + h, :]
            context = acc[...].T.astype(LOW)
            ctx_ref[here, :] = context
            total = jnp.where(stats[8:16, :] > 0, stats[8:16, :], 1.0)
            lse_ref[:, here] = stats[0:8, :] + jnp.log(total)
            return dot(context, w_ref[...])

        scatter = Scatter(place, work, scratch)
        scatter.first()

        def seen(chip):
            pass

        def step(number):
            scatter.slot(number)
            gather.pass_on(number)
            pl.when(number > 0)(lambda: gather.each_new(number - 1, seen))

        each(chips - 1, step)
        scatter.last()
        fetches[5].wait()
        gather.wait_chip(place.chip)
        gather.each_new(chips - 2, seen)
        scatter.own(mid_ref)
        mid_ref[...] += x_ref[...].astype(jnp.float32)
        gather.drain()
        scatter.drain()
        spread_pair.wait()
        spread_down.wait()

    return line_call(
        kernel,
        "scatter_heads",
        2,
        (*qkv, weight, tokens, grads, start, *shards),
        [
            shape((rows, width), jnp.float32),
            shape((length, head_width)),
            shape((8, length), jnp.float32),
            shape((length, width)),
            shape((2, pair_shard.shape[1], width)),
            shape((down_shard.shape[0] - upper, width)),
        ],
        [
            pltpu.VMEM((length, width), LOW),
            *(pltpu.VMEM((length, head_width), LOW) for _ in range(3)),
            pltpu.VMEM((head_width, width), LOW),
            pltpu.VMEM((rows, width), LOW),
            pltpu.VMEM(pair_shard.shape, LOW),
            pltpu.VMEM((down_shard.shape[0] - upper, down_shard.shape[1]), LOW),
            pltpu.SemaphoreType.DMA((6,)),
            pltpu.SemaphoreType.DMA((chips,)),
            pltpu.VMEM((head_width, length), LOW),
            pltpu.VMEM((head_width, rows), jnp.float32),
            pltpu.VMEM((16, rows), jnp.float32),
        ]
        + Scatter.scratch(chips, rows, width)
        + Gather.scratch(chips)
        + Spread.scratch(groups) * 2,
        COST_FLOPS,
        in_hbm=(3, 4, 5),
        from_hbm=(0, 1, 2, 3, 4, 5),
    )


def hidden_layers(groups, chips, middle, gain, shift, pair_weight, down_parts, grads):
    rows, width = middle.shape
    length = rows * 2 * chips
    hidden = pair_weight.shape[1]
    upper = down_parts[0].shape[0]
    part = width // groups
    size = rows // HALVES

    def kernel(
        gain_ref, shift_ref, mid_hbm, pair_hbm, down_one, down_two, og_hbm,
        kept, hid_kept, gg_kept, ug_kept, sum_ref, landed,
        full, og_ref, pair_ref, down_ref, hid_ref, held, staged, mine, load, keep_sem, store_sem, *rest
    ):
        place = Place(groups, chips)
        first, second, line, sems = split_refs(rest, Scatter.SCRATCH, Scatter.SCRATCH, Gather.SEMS, 2)
        fetches = fetch_all(
            [
                (mid_hbm, sum_ref),
                (pair_hbm, pair_ref),
                (down_one, down_ref.at[0:upper]),
                (down_two, down_ref.at[upper:hidden]),
                (og_hbm, og_ref),
            ],
            load,
        )
        gather = Gather(place, full, line, kept, keep_sem)
        scatters = [
            StoredScatter(place, scratch, mine.at[half])
            for half, scratch in enumerate((first, second))
        ]
        exchange = Exchange(place, staged, landed, sems)
        fetches[0].wait()
        normed, _, _ = layer_norm_parts(sum_ref[...], gain_ref[...], shift_ref[...])
        gather.own()[...] = normed.astype(LOW)
        place.barrier(True)
        at_end = (place.chip == 0) | (place.chip == chips - 1)
        gather.begin((0,))
        pl.when(at_end)(lambda: gather.begin((1,)))
        for copy in fetches[1:]:
            copy.wait()

        def work(chip, half):
            pieces_of = [
                pl.ds(pl.multiple_of((chip * 2 + core) * rows + half * size, size), size)
                for core in range(2)
            ]
            values = jnp.concatenate([full[here, :] for here in pieces_of], axis=0)
            gate = dot(values, pair_ref[0], NT)
            up = dot(values, pair_ref[1], NT)
            sigmoid = 1.0 / (1.0 + jnp.exp(-gate))
            activated = gate * sigmoid
            hidden_low = (activated * up).astype(LOW)
            hidden_grad = dot(
                jnp.concatenate([og_ref[here, :] for here in pieces_of], axis=0), down_ref[...], NT
            )
            slope = sigmoid * (1.0 + gate * (1.0 - sigmoid))
            gate_grad = (hidden_grad * (up * slope)).astype(LOW)
            up_grad = (hidden_grad * activated).astype(LOW)
            held[0] = gate_grad
            held[1] = up_grad
            copies = []
            for core, here in enumerate(pieces_of):
                hid_ref[here, :] = hidden_low[core * size : (core + 1) * size]
                from_held = pl.ds(core * size, size)
                copies += [
                    pltpu.make_async_copy(hid_ref.at[here], hid_kept.at[here], store_sem.at[core]),
                    pltpu.make_async_copy(
                        held.at[0, from_held], gg_kept.at[here], store_sem.at[2 + core]
                    ),
                    pltpu.make_async_copy(
                        held.at[1, from_held], ug_kept.at[here], store_sem.at[4 + core]
                    ),
                ]
            for copy in copies:
                copy.start()
            term = dot(gate_grad, pair_ref[0]) + dot(up_grad, pair_ref[1])
            low, high = term[0:size], term[size : 2 * size]
            scatters[half].put(
                chip,
                jnp.where(place.core == 0, high, low),
                jnp.where(place.core == 0, low, high),
            )
            for copy in copies:
                copy.wait()

        def fill(offset):
            block = lax.rem(place.group + offset, groups)
            columns = pl.ds(pl.multiple_of(block * part, part), part)
            staged[offset] = dot(hid_ref[...], og_ref[:, columns], TN).astype(LOW)

        def fill_send(offset):
            fill(offset)
            exchange.copy(offset).start()

        gather.wait_chip(place.chip, (0,))
        work(place.chip, 0)

        def gather_first(step):
            gather.pass_on(step, (0,))
            gather.each_new(step, lambda chip: work(chip, 0), (0,))

        each(chips - 1, gather_first)
        pl.when(jnp.logical_not(at_end))(lambda: gather.begin((1,)))

        def both(step):
            scatters[0].slot(step)

            @pl.when(step == 0)
            def _():
                gather.wait_chip(place.chip, (1,))
                work(place.chip, 1)

            gather.pass_on(step, (1,))
            gather.each_new(step, lambda chip: work(chip, 1), (1,))

        each(chips - 1, both)

        def scatter_second(step):
            scatters[1].slot(step)
            pieces(step, groups, fill_send)
            pl.when(step == 0)(lambda: scatters[0].own(sum_ref.at[0:size]))

        each(chips - 1, scatter_second)
        fill(0)
        exchange.stay().start()
        scatters[1].own(sum_ref.at[size:rows])
        gather.drain()
        scatters[0].drain()
        scatters[1].drain()
        exchange.wait()

    hidden_shape = shape((length, hidden))
    return line_call(
        kernel,
        "gather_hidden",
        3,
        (gain, shift, middle, pair_weight, *down_parts, grads),
        [
            shape((length, width)),
            hidden_shape,
            hidden_shape,
            hidden_shape,
            shape((rows, width), jnp.float32),
            shape((groups, hidden, part)),
        ],
        [
            pltpu.VMEM((length, width), LOW),
            pltpu.VMEM((length, width), LOW),
            pltpu.VMEM(pair_weight.shape, LOW),
            pltpu.VMEM((hidden, width), LOW),
            pltpu.VMEM((length, hidden), LOW),
            pltpu.VMEM((2, rows, hidden), LOW),
            pltpu.VMEM((groups, hidden, part), LOW),
            pltpu.VMEM((HALVES, chips, size, width), LOW),
            pltpu.SemaphoreType.DMA((5,)),
            pltpu.SemaphoreType.DMA((chips,)),
            pltpu.SemaphoreType.DMA((6,)),
        ]
        + Scatter.scratch(chips, size, width) * 2
        + Gather.scratch(chips)
        + Spread.scratch(groups),
        COST_FLOPS,
        in_hbm=(0, 1, 2, 3, 5),
        from_hbm=(2, 3, 4, 5, 6),
    )


def gather_context(
    groups, chips, middle, normed_grad, out_grad, gain, shift, weight, hidden_low, down_parts, normed, pair
):
    rows, width = middle.shape
    length = rows * 2 * chips
    out_width = weight.shape[0]
    hidden = hidden_low.shape[1]
    upper = down_parts[0].shape[0]
    part = width // groups

    def kernel(
        mid_ref, ng_hbm, og_ref, gain_ref, shift_ref, w_hbm, hid_hbm, down_one, down_two,
        a_ref, gg_hbm, ug_hbm,
        kept, cg_ref, mg_ref, sums_ref, out_ref, landed,
        full, total, w_ref, hid_ref, down_ref, gg_ref, ug_ref, staged, columns_in, load, keep_sem, *rest
    ):
        place = Place(groups, chips)
        scratch, line, sems = split_refs(rest, Scatter.SCRATCH, Gather.SEMS, 2)

        def fetch(offset):
            block = lax.rem(place.group + offset, groups)
            columns = pl.ds(pl.multiple_of(block * part, part), part)
            slot = lax.rem(offset, 2)
            return pltpu.make_async_copy(a_ref.at[:, columns], columns_in.at[slot], load.at[slot])

        arrive = pltpu.make_async_copy(ng_hbm, total, load.at[3])
        arrive.start()
        late = [
            pltpu.make_async_copy(a, b, load.at[4 + n])
            for n, (a, b) in enumerate(
                (
                    (down_one, down_ref.at[0:upper]),
                    (down_two, down_ref.at[upper:hidden]),
                    (hid_hbm, hid_ref),
                    (w_hbm, w_ref),
                    (gg_hbm, gg_ref),
                    (ug_hbm, ug_ref),
                )
            )
        ]
        for copy in late:
            copy.start()
        fetch(1).start()
        gather = Gather(place, full, line, kept, keep_sem)
        _, plain, inverse = layer_norm_parts(mid_ref[...], gain_ref[...], shift_ref[...])
        arrive.wait()
        back, gain_grad, shift_grad = layer_norm_back(total[...], plain, inverse, gain_ref[...])
        mid_grad = og_ref[...].astype(jnp.float32) + back
        total[...] = mid_grad
        keep = pltpu.make_async_copy(total, mg_ref, load.at[2])
        keep.start()
        gather.own()[...] = mid_grad.astype(LOW)
        place.barrier(True)
        gather.begin()
        sums_ref[0:1, :] = gain_grad[None, :]
        sums_ref[1:2, :] = shift_grad[None, :]

        def back_work(chip):
            here = pl.ds(pl.multiple_of(chip * 2 * rows, 2 * rows), 2 * rows)
            cg_ref[here, :] = dot(full[here, :], w_ref[...], NT).astype(LOW)

        def out_work(chip, core):
            here = pl.ds(pl.multiple_of((chip * 2 + core) * rows, rows), rows)
            return dot(hid_ref[here, :], down_ref[...])

        exchange = Exchange(place, staged, landed, sems)

        def fill(offset):
            fetch(offset).wait()
            pl.when(offset > 0)(lambda: fetch(lax.rem(offset + 1, groups)).start())
            values = columns_in[lax.rem(offset, 2)]
            staged[offset, 0] = dot(gg_ref[...], values, TN).astype(LOW)
            staged[offset, 1] = dot(ug_ref[...], values, TN).astype(LOW)

        def fill_send(offset):
            fill(offset)
            exchange.copy(offset).start()

        scatter = Scatter(place, out_work, scratch)
        for copy in late[:3]:
            copy.wait()
        scatter.first()
        for copy in late[3:]:
            copy.wait()

        def step(number):
            scatter.slot(number)
            pieces(number, groups, fill_send)
            gather.pass_on(number)

            @pl.when(number == 0)
            def _():
                gather.wait_chip(place.chip)
                back_work(place.chip)

            gather.each_new(number, back_work)

        each(chips - 1, step)
        scatter.last()
        fill(jnp.int32(0))
        exchange.stay().start()
        keep.wait()
        scatter.own(total)
        out_ref[...] = (mid_ref[...] + total[...]).astype(LOW)
        gather.drain()
        scatter.drain()
        exchange.wait()

    return line_call(
        kernel,
        "gather_context",
        5,
        (middle, normed_grad, out_grad, gain, shift, weight, hidden_low, *down_parts, normed, *pair),
        [
            shape((length, width)),
            shape((length, out_width)),
            shape((rows, width), jnp.float32),
            shape((2, width), jnp.float32),
            shape((rows, width)),
            shape((groups, 2, hidden, part)),
        ],
        [
            pltpu.VMEM((length, width), LOW),
            pltpu.VMEM((rows, width), jnp.float32),
            pltpu.VMEM(weight.shape, LOW),
            pltpu.VMEM((length, hidden), LOW),
            pltpu.VMEM((hidden, width), LOW),
            pltpu.VMEM((length, hidden), LOW),
            pltpu.VMEM((length, hidden), LOW),
            pltpu.VMEM((groups, 2, hidden, part), LOW),
            pltpu.VMEM((2, length, part), LOW),
            pltpu.SemaphoreType.DMA((10,)),
            pltpu.SemaphoreType.DMA((chips,)),
        ]
        + Scatter.scratch(chips, rows, width)
        + Gather.scratch(chips)
        + Spread.scratch(groups),
        COST_FLOPS,
        in_hbm=(0, 2, 5),
        from_hbm=(1, 5, 6, 7, 8, 9, 10, 11),
    )


def scatter_triple(
    groups, chips, triple, weights, tokens, gain, shift, mid_grad, sums, bias_sums, normed, context, grads
):
    length, in_width = triple[0].shape
    rows = length // (2 * chips)
    width = weights.shape[1]
    part = width // groups

    def kernel(
        q_ref, k_ref, v_ref, w_ref, gain_ref, shift_ref, sums_ref, bias_ref,
        x_hbm, mg_hbm, a_hbm, ctx_hbm, full_hbm,
        in_ref, small_ref, landed_qkv, landed_out,
        x_ref, mg_ref, a_ref, ctx_ref, full_ref, load,
        total, staged_qkv, staged_out, early_spots, early_groups, late_spots, late_groups, *rest
    ):
        place = Place(groups, chips)
        scratch, one, two, sums_sems = split_refs(rest, Scatter.SCRATCH, 2, 2, 8)
        fetches = fetch_all(
            [
                (a_hbm, a_ref),
                (ctx_hbm, ctx_ref),
                (full_hbm, full_ref),
                (x_hbm, x_ref),
                (mg_hbm, mg_ref),
            ],
            load,
        )
        place.barrier(True, True)
        spots, count = place.spot, 2 * chips
        early_a = SmallSum(early_spots, spots, count, place.fellow, sums_sems[0:2])
        early_b = SmallSum(early_groups, place.group, groups, place.peer, sums_sems[2:4])
        late_a = SmallSum(late_spots, spots, count, place.fellow, sums_sems[4:6])
        late_b = SmallSum(late_groups, place.group, groups, place.peer, sums_sems[6:8])

        def work(chip, core):
            here = pl.ds(pl.multiple_of((chip * 2 + core) * rows, rows), rows)
            term = dot(q_ref[here, :], w_ref[0], NT)
            term = term + dot(k_ref[here, :], w_ref[1], NT)
            return term + dot(v_ref[here, :], w_ref[2], NT)

        exchange_qkv = Exchange(place, staged_qkv, landed_qkv, one)
        exchange_out = Exchange(place, staged_out, landed_out, two)

        def fill(offset):
            block = lax.rem(place.group + offset, groups)
            columns = pl.ds(pl.multiple_of(block * part, part), part)
            values = a_ref[:, columns]
            for number, ref in enumerate((q_ref, k_ref, v_ref)):
                staged_qkv[offset, number] = dot(values, ref[...], TN).astype(LOW)
            staged_out[offset] = dot(ctx_ref[...], full_ref[:, columns], TN).astype(LOW)

        def fill_send(offset):
            fill(offset)
            exchange_qkv.copy(offset).start()
            exchange_out.copy(offset).start()

        scatter = Scatter(place, work, scratch)
        scatter.first()

        def step(number):
            scatter.slot(number)

            @pl.when(number == 0)
            def _():
                early_a.begin(sums_ref[...])
                for copy in fetches:
                    copy.wait()

            pieces(number, groups, fill_send)

            @pl.when(number == chips - 2)
            def _():
                early_groups[place.group] = jnp.zeros(early_groups.shape[1:], jnp.float32)
                early_groups[place.group, 4:7, 0:in_width] = bias_ref[0:3, :]
                early_groups[place.group, 0:2, :] = early_a.result()
                early_b.begin(early_groups[place.group])

        each(chips - 1, step)
        scatter.last()
        fill(0)
        exchange_qkv.stay().start()
        exchange_out.stay().start()
        _, plain, inverse = layer_norm_parts(
            x_ref[...].astype(jnp.float32), gain_ref[...], shift_ref[...]
        )
        scatter.own(total)
        back, gain_grad, shift_grad = layer_norm_back(total[...], plain, inverse, gain_ref[...])
        late_a.begin(jnp.concatenate([gain_grad[None, :], shift_grad[None, :]], axis=0))
        in_ref[...] = (mg_ref[...] + back).astype(LOW)
        scatter.drain()
        exchange_qkv.wait()
        exchange_out.wait()
        late_b.begin(late_a.result())
        first = early_b.result()
        last = late_b.result()
        small_ref[...] = first
        small_ref[1:2, :] = first[0:1, :]
        small_ref[3:4, :] = first[1:2, :]
        small_ref[0:1, :] = last[0:1, :]
        small_ref[2:3, :] = last[1:2, :]

    devices = 2 * chips
    return line_call(
        kernel,
        "scatter_triple",
        6,
        (*triple, weights, gain, shift, sums, bias_sums, tokens, mid_grad, normed, context, grads),
        [
            shape((rows, width)),
            shape((8, width), jnp.float32),
            shape((groups, 3, part, in_width)),
            shape((groups, in_width, part)),
        ],
        [
            pltpu.VMEM((rows, width), LOW),
            pltpu.VMEM((rows, width), jnp.float32),
            pltpu.VMEM((length, width), LOW),
            pltpu.VMEM((length, in_width), LOW),
            pltpu.VMEM((length, width), LOW),
            pltpu.SemaphoreType.DMA((5,)),
            pltpu.VMEM((rows, width), jnp.float32),
            pltpu.VMEM((groups, 3, part, in_width), LOW),
            pltpu.VMEM((groups, in_width, part), LOW),
            pltpu.VMEM((devices, 2, width), jnp.float32),
            pltpu.VMEM((groups, 8, width), jnp.float32),
            pltpu.VMEM((devices, 2, width), jnp.float32),
            pltpu.VMEM((groups, 2, width), jnp.float32),
        ]
        + Scatter.scratch(chips, rows, width)
        + Spread.scratch(groups) * 2
        + [pltpu.SemaphoreType.DMA((n,)) for n in (devices, devices, groups, groups) * 2],
        COST_FLOPS,
        in_hbm=(2, 3),
        from_hbm=(8, 9, 10, 11, 12),
    )


def adam_update(master, gradient, moment_one, moment_two, correct_one, correct_two, rate):
    one_new = 0.9 * moment_one + 0.1 * gradient
    two_new = 0.999 * moment_two + 0.001 * gradient * gradient
    change = one_new / correct_one / (jnp.sqrt(two_new / correct_two) + 1e-08) + 0.1 * master
    return (master - rate * change, one_new, two_new)


def per_device(
    groups,
    chips,
    inputs,
    out_grad,
    segments,
    w_qkv,
    w_out,
    w_gate_up,
    w_down,
    qkv_bias,
    norm_gain,
    norm_bias,
    first_qkv,
    first_out,
    first_gate_up,
    first_down,
    first_bias,
    first_gain,
    first_shift,
    second_qkv,
    second_out,
    second_gate_up,
    second_down,
    second_bias,
    second_gain,
    second_shift,
):
    length = segments.shape[1]
    head_width = w_qkv.shape[2]
    gains = (norm_gain[0:1], norm_gain[1:2])
    shifts = (norm_bias[0:1], norm_bias[1:2])
    place = positions(segments)[0]
    start = jnp.arange(length, dtype=jnp.int32) - place
    low_blocks = start[::BLK] // BLK
    start = start[None, :]
    tables = rotary_tables(place, min(head_width, 128))

    gate_up_turned = jnp.swapaxes(w_gate_up, 1, 2)
    normed_one_all, qkv_all, out_all, down_one, *qkv = gather_project(
        groups,
        chips,
        inputs,
        gains[0],
        shifts[0],
        (w_qkv, w_out, w_down),
        qkv_bias,
        tables,
    )
    middle, context_flat, lse, mlp_grad, pair_all, down_two = scatter_heads(
        groups, chips, qkv, start, out_all, inputs, out_grad, (gate_up_turned, w_down)
    )
    down_parts = (down_one, down_two)
    normed_two_all, hidden_low, gate_grad, up_grad, normed_two_grad, parts_down = hidden_layers(
        groups, chips, middle, gains[1], shifts[1], pair_all, down_parts, mlp_grad
    )
    attn_grad_all, context_grad, middle_grad, sums_two, outputs, parts_pair = (
        gather_context(
            groups,
            chips,
            middle,
            normed_two_grad,
            out_grad,
            gains[1],
            shifts[1],
            out_all,
            hidden_low,
            down_parts,
            normed_two_all,
            (gate_grad, up_grad),
        )
    )
    *triple, bias_sums = attention_backward(
        low_blocks, *qkv, start, lse, context_flat, context_grad, tables
    )
    input_grad, small, parts_qkv, parts_out = scatter_triple(
        groups,
        chips,
        triple,
        qkv_all,
        inputs,
        gains[0],
        shifts[0],
        middle_grad,
        sums_two,
        bias_sums,
        normed_one_all,
        context_flat,
        attn_grad_all,
    )

    def add_parts(parts):
        total = parts[0].astype(jnp.float32)
        for offset in range(1, groups):
            total = total + parts[offset].astype(jnp.float32)
        return total

    grad_qkv, grad_out, grad_down = add_parts(parts_qkv), add_parts(parts_out), add_parts(parts_down)
    grad_gate_up = jnp.swapaxes(add_parts(parts_pair), 1, 2)
    grad_bias = small[4:7, :head_width]
    grad_gain, grad_shift = small[0:2], small[2:4]
    correct_one = 1.0 - 0.9**STEP
    correct_two = 1.0 - 0.999**STEP
    rates = (0.02, 0.3, 0.02, 0.02, 0.3, 0.3, 0.3)
    masters = (w_qkv, w_out, w_gate_up, w_down, qkv_bias, norm_gain, norm_bias)
    gradients = (grad_qkv, grad_out, grad_gate_up, grad_down, grad_bias, grad_gain, grad_shift)
    firsts = (first_qkv, first_out, first_gate_up, first_down, first_bias, first_gain, first_shift)
    seconds = (
        second_qkv,
        second_out,
        second_gate_up,
        second_down,
        second_bias,
        second_gain,
        second_shift,
    )
    updated = [
        adam_update(
            masters[number],
            gradients[number],
            firsts[number],
            seconds[number],
            correct_one,
            correct_two,
            rates[number],
        )
        for number in range(7)
    ]
    return (
        outputs,
        input_grad,
        grad_qkv,
        grad_out,
        grad_gate_up,
        grad_down,
        grad_bias,
        grad_gain,
        grad_shift,
        updated[0][0],
        updated[1][0],
        updated[2][0],
        updated[3][0],
        updated[4][0],
        updated[5][0],
        updated[6][0],
        updated[0][1],
        updated[1][1],
        updated[2][1],
        updated[3][1],
        updated[4][1],
        updated[5][1],
        updated[6][1],
        updated[0][2],
        updated[1][2],
        updated[2][2],
        updated[3][2],
        updated[4][2],
        updated[5][2],
        updated[6][2],
    )


def solution(mesh):
    in_specs = (
        P(("dp", "tensor"), None),
        P(("dp", "tensor"), None),
        P("dp", None),
        P(None, "dp", "tensor"),
        P("tensor", "dp"),
        P(None, "dp", "tensor"),
        P("tensor", "dp"),
        P(None, "tensor"),
        P(),
        P(),
        P(None, "dp", "tensor"),
        P("tensor", "dp"),
        P(None, "dp", "tensor"),
        P("tensor", "dp"),
        P(None, "tensor"),
        P(),
        P(),
        P(None, "dp", "tensor"),
        P("tensor", "dp"),
        P(None, "dp", "tensor"),
        P("tensor", "dp"),
        P(None, "tensor"),
        P(),
        P(),
    )
    out_specs = (
        P(("dp", "tensor"), None),
        P(("dp", "tensor"), None),
        P(None, "dp", "tensor"),
        P("tensor", "dp"),
        P(None, "dp", "tensor"),
        P("tensor", "dp"),
        P(None, "tensor"),
        P(),
        P(),
        P(None, "dp", "tensor"),
        P("tensor", "dp"),
        P(None, "dp", "tensor"),
        P("tensor", "dp"),
        P(None, "tensor"),
        P(),
        P(),
        P(None, "dp", "tensor"),
        P("tensor", "dp"),
        P(None, "dp", "tensor"),
        P("tensor", "dp"),
        P(None, "tensor"),
        P(),
        P(),
        P(None, "dp", "tensor"),
        P("tensor", "dp"),
        P(None, "dp", "tensor"),
        P("tensor", "dp"),
        P(None, "tensor"),
        P(),
        P(),
    )
    return jax.shard_map(
        functools.partial(per_device, mesh.shape["dp"], mesh.shape["tensor"] // 2),
        mesh=mesh, in_specs=in_specs, out_specs=out_specs, check_vma=False
    )
```

```python
import functools

import jax
import jax.numpy as jnp
from jax import lax
from jax.experimental import pallas as pl
from jax.experimental.pallas import tpu as pltpu
from jax.sharding import PartitionSpec as P

HD = 64
ROT = 16
STEP = 10


def layer_norm_parts(values, gain_row, shift_row):
    average = jnp.mean(values, axis=-1, keepdims=True)
    centred = values - average
    inverse = lax.rsqrt(jnp.mean(centred * centred, axis=-1, keepdims=True) + 1e-05)
    normed = centred * inverse
    return (normed * gain_row + shift_row, normed, inverse)


def layer_norm_back(incoming, normed, inverse, gain_row):
    scaled = incoming * gain_row
    inner = (
        scaled
        - jnp.mean(scaled, axis=-1, keepdims=True)
        - normed * jnp.mean(scaled * normed, axis=-1, keepdims=True)
    )
    return (inner * inverse, jnp.sum(incoming * normed, axis=0), jnp.sum(incoming, axis=0))


def positions(segment_ids):
    length = segment_ids.shape[-1]
    indices = jnp.broadcast_to(jnp.arange(length, dtype=jnp.int32), segment_ids.shape)
    before = jnp.concatenate(
        [jnp.full(segment_ids.shape[:-1] + (1,), -1, jnp.int32), segment_ids[..., :-1]], axis=-1
    )
    starts = lax.cummax(jnp.where(segment_ids != before, indices, 0), axis=segment_ids.ndim - 1)
    return indices - starts


def rotary_tables(position_ids, width):
    half_rot = ROT // 2
    frequency = 10000.0 ** (-(2.0 * jnp.arange(half_rot, dtype=jnp.float32)) / ROT)
    angles = position_ids.astype(jnp.float32)[:, None] * frequency
    cosine, sine = jnp.cos(angles), jnp.sin(angles)
    zeros = jnp.zeros((angles.shape[0], HD - ROT), jnp.float32)
    blank = jnp.zeros_like(sine)
    copies = width // HD
    return tuple(
        jnp.tile(jnp.concatenate(parts, axis=1), (1, copies))
        for parts in (
            (cosine, cosine, zeros + 1.0),
            (-sine, blank, zeros),
            (blank, sine, zeros),
        )
    )


NEG = -1e30
BLK = 256
NT = (((1,), (1,)), ((), ()))
NN = (((1,), (0,)), ((), ()))


def dot(left, right, dims=NN, precision=None):
    return lax.dot_general(
        left, right, dims, preferred_element_type=jnp.float32, precision=precision
    )


def head_masks(width, dtype):
    lane = lax.broadcasted_iota(jnp.int32, (1, width), 1)
    return [(lane // HD == h).astype(dtype) for h in range(width // HD)]


def rope_tile(tile, cosine, sine_low, sine_high, sign):
    width = tile.shape[-1]
    ahead = pltpu.roll(tile, width - ROT // 2, 1)
    behind = pltpu.roll(tile, ROT // 2, 1)
    return tile * cosine + sign * (ahead * sine_low + behind * sine_high)


def attend(number, size, k_ref, v_turned, masked, starts, query_ids, acc, stats):
    base = pl.multiple_of(number * size, size)
    keys = k_ref[pl.ds(base, size), :]
    key_ids = base + lax.broadcasted_iota(jnp.int32, (size, size), 0)
    visible = (key_ids >= starts) & (key_ids <= query_ids)
    for h, queries in enumerate(masked):
        scores = jnp.where(visible, dot(keys, queries, NT), NEG)
        peak_old = stats[h : h + 1, :]
        peak = jnp.maximum(peak_old, jnp.max(scores, axis=0, keepdims=True))
        fade = jnp.exp(peak_old - peak)
        prob = jnp.exp(scores - peak)
        stats[h : h + 1, :] = peak
        stats[8 + h : 9 + h, :] = stats[8 + h : 9 + h, :] * fade + jnp.sum(
            prob, axis=0, keepdims=True
        )
        band = slice(h * HD, (h + 1) * HD)
        acc[band, :] = acc[band, :] * fade + dot(
            v_turned[band, pl.ds(base, size)], prob.astype(jnp.bfloat16)
        )


MESH = pl.DeviceIdType.MESH
VMEM_BYTES = 62 << 20
LONGEST = 1024
TN = (((0,), (0,)), ((), ()))
LOW = jnp.bfloat16


def remote(source, target, send, receive, device):
    return pltpu.make_async_remote_copy(
        src_ref=source,
        dst_ref=target,
        send_sem=send,
        recv_sem=receive,
        device_id=device,
        device_id_type=MESH,
    )


class Place:
    def __init__(self, groups, chips):
        self.groups, self.chips = groups, chips
        self.group = lax.axis_index("dp")
        self.spot = lax.axis_index("tensor")
        self.chip, self.core = self.spot // 2, self.spot % 2

    def at(self, chip, core):
        return (self.group, chip * 2 + core)

    def peer(self, offset):
        return (lax.rem(self.group + offset, self.groups), self.spot)

    def fellow(self, offset):
        return (self.group, lax.rem(self.spot + offset, 2 * self.chips))

    def barrier(self, with_groups=False, with_all_spots=False):
        semaphore = pltpu.get_barrier_semaphore()

        def greet(target):
            pl.semaphore_signal(semaphore, inc=1, device_id=target, device_id_type=MESH)

        if with_all_spots:
            for offset in range(1, 2 * self.chips):
                greet(self.fellow(offset))
            count = 2 * self.chips - 1
        else:
            greet(self.at(self.chip, 1 - self.core))
            pl.when(self.chip > 0)(lambda: greet(self.at(self.chip - 1, self.core)))
            pl.when(self.chip < self.chips - 1)(lambda: greet(self.at(self.chip + 1, self.core)))
            count = 1 + jnp.where(self.chip > 0, 1, 0) + jnp.where(self.chip < self.chips - 1, 1, 0)
        if with_groups:
            for offset in range(1, self.groups):
                greet(self.peer(offset))
            count = count + self.groups - 1
        pl.semaphore_wait(semaphore, count)


def each(count, use):
    def one(index, _):
        use(index)
        return 0

    lax.fori_loop(0, count, one, 0)


def block_of(ref, index, size):
    return ref.at[pl.ds(pl.multiple_of(index * size, size), size)]


def fetch_all(pairs, sems):
    copies = [pltpu.make_async_copy(a, b, sems.at[n]) for n, (a, b) in enumerate(pairs)]
    for copy in copies:
        copy.start()
    return copies


HALVES = 2


class Gather:
    SEMS = 5

    def __init__(self, place, full, sems, kept=None, keep_sem=None):
        self.place, self.full, self.kept, self.keep_sem = place, full, kept, keep_sem
        self.line_in, self.core_in, self.right_out, self.left_out, self.core_out = sems
        self.rows = full.shape[0] // (2 * place.chips)

    @classmethod
    def scratch(cls, chips):
        return [pltpu.SemaphoreType.DMA((chips * HALVES,)) for _ in range(cls.SEMS)]

    def own(self):
        return block_of(self.full, self.place.spot, self.rows)

    def block(self, chip, core, half):
        return block_of(self.full, (chip * 2 + core) * HALVES + half, self.rows // HALVES)

    def right(self, which, half):
        place, part = self.place, self.block(which, self.place.core, half)
        target = place.at(jnp.minimum(place.chip + 1, place.chips - 1), place.core)
        index = which * HALVES + half
        return remote(part, part, self.right_out.at[index], self.line_in.at[index], target)

    def left(self, which, half):
        place, part = self.place, self.block(which, self.place.core, half)
        target = place.at(jnp.maximum(place.chip - 1, 0), place.core)
        index = which * HALVES + half
        return remote(part, part, self.left_out.at[index], self.line_in.at[index], target)

    def across(self, which, core, half):
        place, part = self.place, self.block(which, core, half)
        target = place.at(place.chip, 1 - place.core)
        index = which * HALVES + half
        return remote(part, part, self.core_out.at[index], self.core_in.at[index], target)

    def begin(self, halves=range(HALVES)):
        chip, chips = self.place.chip, self.place.chips
        for half in halves:
            pl.when(chip < chips - 1)(lambda: self.right(chip, half).start())
            pl.when(chip > 0)(lambda: self.left(chip, half).start())
        for half in halves:
            self.across(chip, self.place.core, half).start()

    def pass_on(self, step, halves=range(HALVES)):
        chip, chips, core = self.place.chip, self.place.chips, self.place.core
        low, high = chip - 1 - step, chip + 1 + step
        for half in halves:

            @pl.when(low >= 0)
            def _():
                self.right(low, half).wait_recv()
                pl.when(chip < chips - 1)(lambda: self.right(low, half).start())
                self.across(low, core, half).start()

            @pl.when(high < chips)
            def _():
                self.left(high, half).wait_recv()
                pl.when(chip > 0)(lambda: self.left(high, half).start())
                self.across(high, core, half).start()

    def keep(self, which):
        part = block_of(self.full, which, 2 * self.rows)
        return pltpu.make_async_copy(
            part, block_of(self.kept, which, 2 * self.rows), self.keep_sem.at[which]
        )

    def wait_chip(self, which, halves=range(HALVES)):
        for half in halves:
            self.across(which, 1 - self.place.core, half).wait_recv()
        if self.kept is not None and HALVES - 1 in halves:
            self.keep(which).start()

    def each_new(self, step, use, halves=range(HALVES)):
        low, high = self.place.chip - 1 - step, self.place.chip + 1 + step

        @pl.when(low >= 0)
        def _():
            self.wait_chip(low, halves)
            use(low)

        @pl.when(high < self.place.chips)
        def _():
            self.wait_chip(high, halves)
            use(high)

    def drain(self):
        chip, chips, core = self.place.chip, self.place.chips, self.place.core

        def one(which):
            for half in range(HALVES):
                self.across(which, core, half).wait_send()
                pl.when((which <= chip) & (chip < chips - 1))(
                    lambda: self.right(which, half).wait_send()
                )
                pl.when((which >= chip) & (chip > 0))(lambda: self.left(which, half).wait_send())
            if self.kept is not None:
                self.keep(which).wait()

        each(chips, one)


class Scatter:
    def __init__(self, place, work, scratch, halves=HALVES):
        self.place, self.work, self.halves = place, work, halves
        self.out, self.side, self.line = scratch[:3]
        self.core_out, self.core_in, self.line_out, self.line_in = scratch[3:]
        self.part = self.out.shape[1] // halves
        chip, chips = place.chip, place.chips
        self.near = jnp.minimum(chip, chips - 1 - chip)
        self.alone = chips - 1 - 2 * self.near
        self.flip = jnp.where(chip * 2 < chips, 0, 1)
        self.lag = jnp.where(self.near > 0, 1, 0)

    @staticmethod
    def scratch(chips, rows, width):
        return [
            pltpu.VMEM((chips, rows, width), LOW),
            pltpu.VMEM((chips, rows, width), LOW),
            pltpu.VMEM((chips + 1, rows, width), LOW),
            pltpu.SemaphoreType.DMA((chips,)),
            pltpu.SemaphoreType.DMA((chips,)),
            pltpu.SemaphoreType.DMA((chips * HALVES,)),
            pltpu.SemaphoreType.DMA(((chips + 1) * HALVES,)),
        ]

    SCRATCH = 7

    def order(self, turn):
        chips = self.place.chips
        later = jnp.maximum(turn - self.alone, 0)
        pair = later // 2
        far = jnp.where(turn < self.alone, chips - 1 - turn, chips - 1 - self.alone - pair)
        which = jnp.where((turn >= self.alone) & (later % 2 == 1), pair, far)
        which = jnp.where(turn == chips - 1, self.near, which)
        return jnp.where(self.flip == 1, chips - 1 - which, which)

    def across(self, which):
        place = self.place
        return remote(
            self.out.at[which],
            self.side.at[which],
            self.core_out.at[which],
            self.core_in.at[which],
            place.at(place.chip, 1 - place.core),
        )

    def hop(self, which, slot, half, target):
        rows = slice(half * self.part, (half + 1) * self.part)
        return remote(
            self.out.at[which, rows],
            self.line.at[slot, rows],
            self.line_out.at[which * self.halves + half],
            self.line_in.at[slot * self.halves + half],
            self.place.at(target, self.place.core),
        )

    def right(self, which, half):
        place = self.place
        slot = jnp.where(which == place.chip + 1, place.chips, which)
        return self.hop(which, slot, half, jnp.minimum(place.chip + 1, place.chips - 1))

    def left(self, which, half):
        return self.hop(which, which, half, jnp.maximum(self.place.chip - 1, 0))

    def arrived(self, slot, half):
        place = self.place
        rows = slice(half * self.part, (half + 1) * self.part)
        part = self.line.at[slot, rows]
        other = place.at(place.chip, 1 - place.core)
        remote(
            part, part, self.line_out.at[0], self.line_in.at[slot * self.halves + half], other
        ).wait_recv()
        return self.line[slot, rows].astype(jnp.float32)

    def produce(self, turn):
        which = self.order(turn)
        self.out[which] = self.work(which, 1 - self.place.core).astype(LOW)
        self.across(which).start()

    def chip_sum(self, which):
        mine = self.work(which, self.place.core)
        self.across(which).wait()
        return mine + self.side[which].astype(jnp.float32)

    def send(self, which, upstream, copy):
        total = self.chip_sum(which)

        @pl.when(upstream)
        def _():
            for half in range(self.halves):
                rows = slice(half * self.part, (half + 1) * self.part)
                self.out[which, rows] = (total[rows] + self.arrived(which, half)).astype(LOW)
                copy(which, half).start()

        @pl.when(jnp.logical_not(upstream))
        def _():
            for half in range(self.halves):
                rows = slice(half * self.part, (half + 1) * self.part)
                self.out[which, rows] = total[rows].astype(LOW)
                copy(which, half).start()

    def first(self):
        pl.when(self.lag == 1)(lambda: self.produce(0))

    def slot(self, number):
        chip, chips = self.place.chip, self.place.chips
        self.produce(number + self.lag)
        right = chips - 1 - (number - chip)
        left = number - (chips - 1 - chip)
        pl.when((number >= chip) & (right > chip))(
            lambda: self.send(right, chip > 0, self.right)
        )
        pl.when((left >= 0) & (left < chip))(
            lambda: self.send(left, chip < chips - 1, self.left)
        )

    def last(self):
        pl.when(self.lag == 0)(lambda: self.produce(self.place.chips - 1))

    def own(self, total):
        chip, chips = self.place.chip, self.place.chips
        total[...] = self.chip_sum(chip)
        for half in range(self.halves):
            rows = slice(half * self.part, (half + 1) * self.part)

            @pl.when(chip > 0)
            def _():
                total[rows] += self.arrived(chips, half)

            @pl.when(chip < chips - 1)
            def _():
                total[rows] += self.arrived(chip, half)

    def drain(self):
        chip = self.place.chip

        def one(which):
            for half in range(self.halves):
                pl.when(which > chip)(lambda: self.right(which, half).wait_send())
                pl.when(which < chip)(lambda: self.left(which, half).wait_send())

        each(self.place.chips, one)


class StoredScatter(Scatter):
    def __init__(self, place, scratch, mine):
        super().__init__(place, None, scratch, 1)
        self.mine = mine

    def put(self, which, other, own):
        self.out[which] = other.astype(LOW)
        self.across(which).start()
        self.mine[which] = own.astype(LOW)

    def produce(self, turn):
        pass

    def chip_sum(self, which):
        self.across(which).wait()
        return self.mine[which].astype(jnp.float32) + self.side[which].astype(jnp.float32)


class Spread:
    def __init__(self, place, shard, staged, whole, axis, sems):
        self.place, self.staged, self.whole, self.sems = place, staged, whole, sems
        size = shard.shape[axis]
        here = pl.ds(pl.multiple_of(place.group * size, size), size)
        self.mine = whole.at[tuple(here if a == axis else slice(None) for a in range(len(shard.shape)))]
        staged[...] = shard[...].astype(LOW)

    @staticmethod
    def scratch(groups):
        return [pltpu.SemaphoreType.DMA((groups,)), pltpu.SemaphoreType.DMA((groups,))]

    def copy(self, offset):
        return remote(
            self.staged,
            self.mine,
            self.sems[0].at[offset],
            self.sems[1].at[offset],
            self.place.peer(offset),
        )

    def stay(self):
        return pltpu.make_async_copy(self.staged, self.mine, self.sems[0].at[0])

    def start(self):
        for offset in range(1, self.place.groups):
            self.copy(offset).start()
        self.stay().start()

    def wait(self):
        for offset in range(1, self.place.groups):
            self.copy(offset).wait()
        self.stay().wait()


class Exchange:
    def __init__(self, place, staged, landed, sems):
        self.place, self.staged, self.landed = place, staged, landed
        self.send, self.receive = sems

    def copy(self, offset):
        return remote(
            self.staged.at[offset],
            self.landed.at[offset],
            self.send.at[offset],
            self.receive.at[offset],
            self.place.peer(offset),
        )

    def stay(self):
        return pltpu.make_async_copy(self.staged.at[0], self.landed.at[0], self.send.at[0])

    def wait(self):
        def one(offset, _):
            self.copy(offset).wait()
            return 0

        lax.fori_loop(1, self.place.groups, one, 0)
        self.stay().wait()


class SmallSum:
    def __init__(self, slots, me, count, target, sems):
        self.slots, self.me, self.count, self.target = slots, me, count, target
        self.send, self.receive = sems

    def copy(self, offset):
        part = self.slots.at[self.me]
        return remote(
            part, part, self.send.at[offset], self.receive.at[self.me], self.target(offset)
        )

    def begin(self, rows):
        self.slots[self.me] = rows
        for offset in range(1, self.count):
            self.copy(offset).start()

    def result(self):
        for offset in range(1, self.count):
            source = lax.rem(self.me + offset, self.count)
            part = self.slots.at[source]
            remote(
                part, part, self.send.at[offset], self.receive.at[source], self.target(offset)
            ).wait_recv()
        total = self.slots[0]
        for index in range(1, self.count):
            total = total + self.slots[index]
        for offset in range(1, self.count):
            self.copy(offset).wait_send()
        return total


def pieces(number, groups, fill):
    @pl.when(number == 0)
    def _():
        each(groups - 1, lambda index: fill(index + 1))


def line_call(kernel, name, number, operands, out_shape, scratch, flops, in_hbm=(), from_hbm=()):
    whole, hbm = pl.BlockSpec(memory_space=pltpu.VMEM), pl.BlockSpec(memory_space=pl.ANY)
    ins = [hbm if n in from_hbm else whole for n in range(len(operands))]
    outs = [hbm if n in in_hbm else whole for n in range(len(out_shape))]
    return pl.pallas_call(
        kernel,
        out_shape=out_shape,
        in_specs=ins,
        out_specs=outs,
        scratch_shapes=scratch,
        compiler_params=pltpu.CompilerParams(
            collective_id=number, has_side_effects=True, vmem_limit_bytes=VMEM_BYTES
        ),
        cost_estimate=pl.CostEstimate(flops=flops, bytes_accessed=0, transcendentals=0),
        name=name,
    )(*operands)


COST_FLOPS = 80_000_000_000


def shape(dims, kind=LOW):
    return jax.ShapeDtypeStruct(dims, kind)


def split_refs(refs, *counts):
    parts, at = [], 0
    for count in counts:
        parts.append(refs[at : at + count])
        at += count
    return parts


def gather_project(groups, chips, tokens, gain, shift, shards, bias, tables):
    rows, width = tokens.shape
    length = rows * 2 * chips
    qkv_shard, out_shard, down_shard = shards
    part, out_width = qkv_shard.shape[1:]
    upper = down_shard.shape[0] // 2
    tile = tables[0].shape[1]

    def kernel(
        x_ref, gain_ref, shift_ref, qkv_ref, out_ref, down_ref, bias_ref,
        cos_hbm, sin_low_hbm, sin_high_hbm,
        kept, weights_kept, out_whole, down_whole, q_ref, k_ref, v_ref,
        full, weights, qkv_staged, out_staged, down_staged, cos_ref, sin_low_ref, sin_high_ref,
        load, keep_sem, *sems
    ):
        place = Place(groups, chips)
        fetches = fetch_all(
            [(cos_hbm, cos_ref), (sin_low_hbm, sin_low_ref), (sin_high_hbm, sin_high_ref)], load
        )
        line, one, two, three = split_refs(sems, Gather.SEMS, 2, 2, 2)
        gather = Gather(place, full, line, kept, keep_sem)
        normed, _, _ = layer_norm_parts(
            x_ref[...].astype(jnp.float32), gain_ref[...], shift_ref[...]
        )
        gather.own()[...] = normed.astype(LOW)
        spread_qkv = Spread(place, qkv_ref, qkv_staged, weights, 1, one)
        place.barrier(True)
        gather.begin()
        spread_qkv.start()
        spread_out = Spread(place, out_ref, out_staged, out_whole, 1, two)
        spread_out.start()
        spread_down = Spread(place, down_ref.at[0:upper], down_staged, down_whole, 1, three)
        spread_down.start()

        def work(chip):
            base = pl.multiple_of(chip * 2 * rows, 2 * rows)
            here = pl.ds(base, 2 * rows)
            values = full[here, :]
            for number, ref in enumerate((q_ref, k_ref, v_ref)):
                result = dot(values, weights[number]) + bias_ref[number : number + 1, :]
                if number < 2:
                    parts = [
                        rope_tile(
                            result[:, t * tile : (t + 1) * tile],
                            cos_ref[here, :],
                            sin_low_ref[here, :],
                            sin_high_ref[here, :],
                            1.0,
                        )
                        for t in range(out_width // tile)
                    ]
                    result = jnp.concatenate(parts, axis=1) if len(parts) > 1 else parts[0]
                ref[here, :] = result.astype(LOW)

        gather.pass_on(0)
        for copy in fetches:
            copy.wait()
        spread_qkv.wait()
        weights_keep = pltpu.make_async_copy(weights, weights_kept, load.at[3])
        weights_keep.start()
        gather.wait_chip(place.chip)
        work(place.chip)

        def step(number):
            pl.when(number > 0)(lambda: gather.pass_on(number))
            gather.each_new(number, work)

        each(chips - 1, step)
        weights_keep.wait()
        spread_out.wait()
        spread_down.wait()
        gather.drain()

    head_shape = shape((length, out_width))
    return line_call(
        kernel,
        "gather_project",
        1,
        (tokens, gain, shift, *shards, bias, *tables),
        [
            shape((length, width)),
            shape((3, width, out_width)),
            shape((out_width, width)),
            shape((upper, width)),
            head_shape,
            head_shape,
            head_shape,
        ],
        [
            pltpu.VMEM((length, width), LOW),
            pltpu.VMEM((3, width, out_width), LOW),
            pltpu.VMEM(qkv_shard.shape, LOW),
            pltpu.VMEM(out_shard.shape, LOW),
            pltpu.VMEM((upper, down_shard.shape[1]), LOW),
            *(pltpu.VMEM((length, tile), jnp.float32) for _ in range(3)),
            pltpu.SemaphoreType.DMA((4,)),
            pltpu.SemaphoreType.DMA((chips,)),
        ]
        + Gather.scratch(chips)
        + Spread.scratch(groups) * 3,
        COST_FLOPS,
        in_hbm=(0, 1, 2, 3),
        from_hbm=(7, 8, 9),
    )


def scatter_heads(groups, chips, qkv, start, weight, tokens, grads, shards):
    rows, width = tokens.shape
    length, head_width = qkv[0].shape
    heads = head_width // HD
    pair_shard, down_shard = shards
    upper = down_shard.shape[0] // 2

    def kernel(
        q_hbm, k_hbm, v_hbm, w_hbm, x_hbm, og_hbm, start_ref, pair_ref, down_ref,
        mid_ref, ctx_ref, lse_ref, kept, pair_whole, down_whole,
        full, q_ref, k_ref, v_ref, w_ref, x_ref, pair_staged, down_staged,
        load, keep_sem, v_turned, acc, stats, *rest
    ):
        place = Place(groups, chips)
        scratch, line, one, two = split_refs(rest, Scatter.SCRATCH, Gather.SEMS, 2, 2)
        gather = Gather(place, full, line, kept, keep_sem)
        fetches = fetch_all(
            [
                (og_hbm, gather.own()),
                (k_hbm, k_ref),
                (v_hbm, v_ref),
                (q_hbm, q_ref),
                (w_hbm, w_ref),
                (x_hbm, x_ref),
            ],
            load,
        )
        place.barrier(True)
        fetches[0].wait()
        gather.begin()
        spread_pair = Spread(place, pair_ref, pair_staged, pair_whole, 2, one)
        spread_pair.start()
        spread_down = Spread(place, down_ref.at[upper:], down_staged, down_whole, 1, two)
        spread_down.start()
        for copy in fetches[1:5]:
            copy.wait()
        for part in range(length // BLK):
            here = slice(part * BLK, (part + 1) * BLK)
            v_turned[:, here] = v_ref[here, :].T
        masks = head_masks(head_width, LOW)

        def work(chip, core):
            block = chip * 2 + core
            base = pl.multiple_of(block * rows, rows)
            here = pl.ds(base, rows)
            values = (q_ref[here, :] * 0.125).astype(LOW)
            masked = [values * m for m in masks]
            starts = start_ref[:, here]
            query_ids = base + lax.broadcasted_iota(jnp.int32, (1, rows), 1)
            acc[...] = jnp.zeros_like(acc)
            stats[0:8, :] = jnp.full((8, rows), NEG, jnp.float32)
            stats[8:16, :] = jnp.zeros((8, rows), jnp.float32)

            def step(number, _):
                attend(number, rows, k_ref, v_turned, masked, starts, query_ids, acc, stats)
                return 0

            lax.fori_loop(jnp.maximum(block - LONGEST // rows, 0), block + 1, step, 0)
            for h in range(heads):
                band = slice(h * HD, (h + 1) * HD)
                acc[band, :] = acc[band, :] / stats[8 + h : 9 + h, :]
            context = acc[...].T.astype(LOW)
            ctx_ref[here, :] = context
            total = jnp.where(stats[8:16, :] > 0, stats[8:16, :], 1.0)
            lse_ref[:, here] = stats[0:8, :] + jnp.log(total)
            return dot(context, w_ref[...])

        scatter = Scatter(place, work, scratch)
        scatter.first()

        def seen(chip):
            pass

        def step(number):
            scatter.slot(number)
            gather.pass_on(number)
            pl.when(number > 0)(lambda: gather.each_new(number - 1, seen))

        each(chips - 1, step)
        scatter.last()
        fetches[5].wait()
        gather.wait_chip(place.chip)
        gather.each_new(chips - 2, seen)
        scatter.own(mid_ref)
        mid_ref[...] += x_ref[...].astype(jnp.float32)
        gather.drain()
        scatter.drain()
        spread_pair.wait()
        spread_down.wait()

    return line_call(
        kernel,
        "scatter_heads",
        2,
        (*qkv, weight, tokens, grads, start, *shards),
        [
            shape((rows, width), jnp.float32),
            shape((length, head_width)),
            shape((8, length), jnp.float32),
            shape((length, width)),
            shape((2, pair_shard.shape[1], width)),
            shape((down_shard.shape[0] - upper, width)),
        ],
        [
            pltpu.VMEM((length, width), LOW),
            *(pltpu.VMEM((length, head_width), LOW) for _ in range(3)),
            pltpu.VMEM((head_width, width), LOW),
            pltpu.VMEM((rows, width), LOW),
            pltpu.VMEM(pair_shard.shape, LOW),
            pltpu.VMEM((down_shard.shape[0] - upper, down_shard.shape[1]), LOW),
            pltpu.SemaphoreType.DMA((6,)),
            pltpu.SemaphoreType.DMA((chips,)),
            pltpu.VMEM((head_width, length), LOW),
            pltpu.VMEM((head_width, rows), jnp.float32),
            pltpu.VMEM((16, rows), jnp.float32),
        ]
        + Scatter.scratch(chips, rows, width)
        + Gather.scratch(chips)
        + Spread.scratch(groups) * 2,
        COST_FLOPS,
        in_hbm=(3, 4, 5),
        from_hbm=(0, 1, 2, 3, 4, 5),
    )


def hidden_layers(groups, chips, middle, gain, shift, pair_weight, down_parts, grads):
    rows, width = middle.shape
    length = rows * 2 * chips
    hidden = pair_weight.shape[1]
    upper = down_parts[0].shape[0]
    part = width // groups
    size = rows // HALVES

    def kernel(
        gain_ref, shift_ref, mid_hbm, pair_hbm, down_one, down_two, og_hbm,
        kept, hid_kept, gg_kept, ug_kept, sum_ref, landed,
        full, og_ref, pair_ref, down_ref, hid_ref, held, staged, mine, load, keep_sem, store_sem, *rest
    ):
        place = Place(groups, chips)
        first, second, line, sems = split_refs(rest, Scatter.SCRATCH, Scatter.SCRATCH, Gather.SEMS, 2)
        fetches = fetch_all(
            [
                (mid_hbm, sum_ref),
                (pair_hbm, pair_ref),
                (down_one, down_ref.at[0:upper]),
                (down_two, down_ref.at[upper:hidden]),
                (og_hbm, og_ref),
            ],
            load,
        )
        gather = Gather(place, full, line, kept, keep_sem)
        scatters = [
            StoredScatter(place, scratch, mine.at[half])
            for half, scratch in enumerate((first, second))
        ]
        exchange = Exchange(place, staged, landed, sems)
        fetches[0].wait()
        normed, _, _ = layer_norm_parts(sum_ref[...], gain_ref[...], shift_ref[...])
        gather.own()[...] = normed.astype(LOW)
        place.barrier(True)
        at_end = (place.chip == 0) | (place.chip == chips - 1)
        gather.begin((0,))
        pl.when(at_end)(lambda: gather.begin((1,)))
        for copy in fetches[1:]:
            copy.wait()

        def work(chip, half):
            pieces_of = [
                pl.ds(pl.multiple_of((chip * 2 + core) * rows + half * size, size), size)
                for core in range(2)
            ]
            values = jnp.concatenate([full[here, :] for here in pieces_of], axis=0)
            gate = dot(values, pair_ref[0], NT)
            up = dot(values, pair_ref[1], NT)
            sigmoid = 1.0 / (1.0 + jnp.exp(-gate))
            activated = gate * sigmoid
            hidden_low = (activated * up).astype(LOW)
            hidden_grad = dot(
                jnp.concatenate([og_ref[here, :] for here in pieces_of], axis=0), down_ref[...], NT
            )
            slope = sigmoid * (1.0 + gate * (1.0 - sigmoid))
            gate_grad = (hidden_grad * (up * slope)).astype(LOW)
            up_grad = (hidden_grad * activated).astype(LOW)
            held[0] = gate_grad
            held[1] = up_grad
            copies = []
            for core, here in enumerate(pieces_of):
                hid_ref[here, :] = hidden_low[core * size : (core + 1) * size]
                from_held = pl.ds(core * size, size)
                copies += [
                    pltpu.make_async_copy(hid_ref.at[here], hid_kept.at[here], store_sem.at[core]),
                    pltpu.make_async_copy(
                        held.at[0, from_held], gg_kept.at[here], store_sem.at[2 + core]
                    ),
                    pltpu.make_async_copy(
                        held.at[1, from_held], ug_kept.at[here], store_sem.at[4 + core]
                    ),
                ]
            for copy in copies:
                copy.start()
            term = dot(gate_grad, pair_ref[0]) + dot(up_grad, pair_ref[1])
            low, high = term[0:size], term[size : 2 * size]
            scatters[half].put(
                chip,
                jnp.where(place.core == 0, high, low),
                jnp.where(place.core == 0, low, high),
            )
            for copy in copies:
                copy.wait()

        def fill(offset):
            block = lax.rem(place.group + offset, groups)
            columns = pl.ds(pl.multiple_of(block * part, part), part)
            staged[offset] = dot(hid_ref[...], og_ref[:, columns], TN).astype(LOW)

        def fill_send(offset):
            fill(offset)
            exchange.copy(offset).start()

        gather.wait_chip(place.chip, (0,))
        work(place.chip, 0)

        def gather_first(step):
            gather.pass_on(step, (0,))
            gather.each_new(step, lambda chip: work(chip, 0), (0,))

        each(chips - 1, gather_first)
        pl.when(jnp.logical_not(at_end))(lambda: gather.begin((1,)))

        def both(step):
            scatters[0].slot(step)

            @pl.when(step == 0)
            def _():
                gather.wait_chip(place.chip, (1,))
                work(place.chip, 1)

            gather.pass_on(step, (1,))
            gather.each_new(step, lambda chip: work(chip, 1), (1,))

        each(chips - 1, both)

        def scatter_second(step):
            scatters[1].slot(step)
            pieces(step, groups, fill_send)
            pl.when(step == 0)(lambda: scatters[0].own(sum_ref.at[0:size]))

        each(chips - 1, scatter_second)
        fill(0)
        exchange.stay().start()
        scatters[1].own(sum_ref.at[size:rows])
        gather.drain()
        scatters[0].drain()
        scatters[1].drain()
        exchange.wait()

    hidden_shape = shape((length, hidden))
    return line_call(
        kernel,
        "gather_hidden",
        3,
        (gain, shift, middle, pair_weight, *down_parts, grads),
        [
            shape((length, width)),
            hidden_shape,
            hidden_shape,
            hidden_shape,
            shape((rows, width), jnp.float32),
            shape((groups, hidden, part)),
        ],
        [
            pltpu.VMEM((length, width), LOW),
            pltpu.VMEM((length, width), LOW),
            pltpu.VMEM(pair_weight.shape, LOW),
            pltpu.VMEM((hidden, width), LOW),
            pltpu.VMEM((length, hidden), LOW),
            pltpu.VMEM((2, rows, hidden), LOW),
            pltpu.VMEM((groups, hidden, part), LOW),
            pltpu.VMEM((HALVES, chips, size, width), LOW),
            pltpu.SemaphoreType.DMA((5,)),
            pltpu.SemaphoreType.DMA((chips,)),
            pltpu.SemaphoreType.DMA((6,)),
        ]
        + Scatter.scratch(chips, size, width) * 2
        + Gather.scratch(chips)
        + Spread.scratch(groups),
        COST_FLOPS,
        in_hbm=(0, 1, 2, 3, 5),
        from_hbm=(2, 3, 4, 5, 6),
    )


def gather_context(
    groups, chips, middle, normed_grad, out_grad, gain, shift, weight, hidden_low, down_parts, normed, pair
):
    rows, width = middle.shape
    length = rows * 2 * chips
    out_width = weight.shape[0]
    hidden = hidden_low.shape[1]
    upper = down_parts[0].shape[0]
    part = width // groups

    def kernel(
        mid_ref, ng_hbm, og_ref, gain_ref, shift_ref, w_hbm, hid_hbm, down_one, down_two,
        a_ref, gg_hbm, ug_hbm,
        kept, cg_ref, mg_ref, sums_ref, out_ref, landed,
        full, total, w_ref, hid_ref, down_ref, gg_ref, ug_ref, staged, columns_in, load, keep_sem, *rest
    ):
        place = Place(groups, chips)
        scratch, line, sems = split_refs(rest, Scatter.SCRATCH, Gather.SEMS, 2)

        def fetch(offset):
            block = lax.rem(place.group + offset, groups)
            columns = pl.ds(pl.multiple_of(block * part, part), part)
            slot = lax.rem(offset, 2)
            return pltpu.make_async_copy(a_ref.at[:, columns], columns_in.at[slot], load.at[slot])

        arrive = pltpu.make_async_copy(ng_hbm, total, load.at[3])
        arrive.start()
        late = [
            pltpu.make_async_copy(a, b, load.at[4 + n])
            for n, (a, b) in enumerate(
                (
                    (down_one, down_ref.at[0:upper]),
                    (down_two, down_ref.at[upper:hidden]),
                    (hid_hbm, hid_ref),
                    (w_hbm, w_ref),
                    (gg_hbm, gg_ref),
                    (ug_hbm, ug_ref),
                )
            )
        ]
        for copy in late:
            copy.start()
        fetch(1).start()
        gather = Gather(place, full, line, kept, keep_sem)
        _, plain, inverse = layer_norm_parts(mid_ref[...], gain_ref[...], shift_ref[...])
        arrive.wait()
        back, gain_grad, shift_grad = layer_norm_back(total[...], plain, inverse, gain_ref[...])
        mid_grad = og_ref[...].astype(jnp.float32) + back
        total[...] = mid_grad
        keep = pltpu.make_async_copy(total, mg_ref, load.at[2])
        keep.start()
        gather.own()[...] = mid_grad.astype(LOW)
        place.barrier(True)
        gather.begin()
        sums_ref[0:1, :] = gain_grad[None, :]
        sums_ref[1:2, :] = shift_grad[None, :]

        def back_work(chip):
            here = pl.ds(pl.multiple_of(chip * 2 * rows, 2 * rows), 2 * rows)
            cg_ref[here, :] = dot(full[here, :], w_ref[...], NT).astype(LOW)

        def out_work(chip, core):
            here = pl.ds(pl.multiple_of((chip * 2 + core) * rows, rows), rows)
            return dot(hid_ref[here, :], down_ref[...])

        exchange = Exchange(place, staged, landed, sems)

        def fill(offset):
            fetch(offset).wait()
            pl.when(offset > 0)(lambda: fetch(lax.rem(offset + 1, groups)).start())
            values = columns_in[lax.rem(offset, 2)]
            staged[offset, 0] = dot(gg_ref[...], values, TN).astype(LOW)
            staged[offset, 1] = dot(ug_ref[...], values, TN).astype(LOW)

        def fill_send(offset):
            fill(offset)
            exchange.copy(offset).start()

        scatter = Scatter(place, out_work, scratch)
        for copy in late[:3]:
            copy.wait()
        scatter.first()
        for copy in late[3:]:
            copy.wait()

        def step(number):
            scatter.slot(number)
            pieces(number, groups, fill_send)
            gather.pass_on(number)

            @pl.when(number == 0)
            def _():
                gather.wait_chip(place.chip)
                back_work(place.chip)

            gather.each_new(number, back_work)

        each(chips - 1, step)
        scatter.last()
        fill(jnp.int32(0))
        exchange.stay().start()
        keep.wait()
        scatter.own(total)
        out_ref[...] = (mid_ref[...] + total[...]).astype(LOW)
        gather.drain()
        scatter.drain()
        exchange.wait()

    return line_call(
        kernel,
        "gather_context",
        5,
        (middle, normed_grad, out_grad, gain, shift, weight, hidden_low, *down_parts, normed, *pair),
        [
            shape((length, width)),
            shape((length, out_width)),
            shape((rows, width), jnp.float32),
            shape((2, width), jnp.float32),
            shape((rows, width)),
            shape((groups, 2, hidden, part)),
        ],
        [
            pltpu.VMEM((length, width), LOW),
            pltpu.VMEM((rows, width), jnp.float32),
            pltpu.VMEM(weight.shape, LOW),
            pltpu.VMEM((length, hidden), LOW),
            pltpu.VMEM((hidden, width), LOW),
            pltpu.VMEM((length, hidden), LOW),
            pltpu.VMEM((length, hidden), LOW),
            pltpu.VMEM((groups, 2, hidden, part), LOW),
            pltpu.VMEM((2, length, part), LOW),
            pltpu.SemaphoreType.DMA((10,)),
            pltpu.SemaphoreType.DMA((chips,)),
        ]
        + Scatter.scratch(chips, rows, width)
        + Gather.scratch(chips)
        + Spread.scratch(groups),
        COST_FLOPS,
        in_hbm=(0, 2, 5),
        from_hbm=(1, 5, 6, 7, 8, 9, 10, 11),
    )


class PreparedScatter(Scatter):
    def __init__(self, place, work, scratch, prepare):
        super().__init__(place, work, scratch)
        self.prepare = prepare

    def produce(self, turn):
        self.prepare(turn, self.order(turn))
        super().produce(turn)


def scatter_triple(
    groups, chips, qkv, start, lse, context, context_grad, tables, weights, tokens, gain, shift,
    mid_grad, sums, normed, grads
):
    length, in_width = qkv[0].shape
    rows = length // (2 * chips)
    width = weights.shape[1]
    part = width // groups
    heads = in_width // HD
    tile = tables[0].shape[1]
    reach = LONGEST // rows

    def kernel(
        start_ref, lse_ref, gain_ref, shift_ref, sums_ref,
        q_hbm, k_hbm, v_hbm, cg_hbm, ctx_hbm, cos_hbm, sin_low_hbm, sin_high_hbm,
        w_hbm, x_hbm, mg_hbm, a_hbm, full_hbm,
        in_ref, small_ref, landed_qkv, landed_out,
        q_ref, k_ref, v_ref, cg_ref, ctx_ref, cos_ref, sin_low_ref, sin_high_ref,
        w_ref, x_ref, mg_ref, columns_in, load, load_columns,
        k_turned, dq_acc, dk_acc, dv_acc, delta, dq_ref, dk_ref, dv_ref, bias,
        total, staged_qkv, staged_out, early_spots, early_groups, late_spots, late_groups, *rest
    ):
        place = Place(groups, chips)
        scratch, one, two, sums_sems = split_refs(rest, Scatter.SCRATCH, 2, 2, 8)
        fetches = fetch_all(
            [
                (k_hbm, k_ref),
                (q_hbm, q_ref),
                (v_hbm, v_ref),
                (cg_hbm, cg_ref),
                (ctx_hbm, ctx_ref),
                (cos_hbm, cos_ref),
                (sin_low_hbm, sin_low_ref),
                (sin_high_hbm, sin_high_ref),
                (w_hbm, w_ref),
                (x_hbm, x_ref),
                (mg_hbm, mg_ref),
            ],
            load,
        )
        dq_acc[...] = jnp.zeros_like(dq_acc)
        dk_acc[...] = jnp.zeros_like(dk_acc)
        dv_acc[...] = jnp.zeros_like(dv_acc)
        bias[...] = jnp.zeros_like(bias)
        place.barrier(True, True)
        spots, count = place.spot, 2 * chips
        early_a = SmallSum(early_spots, spots, count, place.fellow, sums_sems[0:2])
        early_b = SmallSum(early_groups, place.group, groups, place.peer, sums_sems[2:4])
        late_a = SmallSum(late_spots, spots, count, place.fellow, sums_sems[4:6])
        late_b = SmallSum(late_groups, place.group, groups, place.peer, sums_sems[6:8])
        for copy in fetches[:9]:
            copy.wait()
        masks = head_masks(in_width, LOW)
        select = (
            lax.broadcasted_iota(jnp.int32, (8, in_width), 1) // HD
            == lax.broadcasted_iota(jnp.int32, (8, in_width), 0)
        ).astype(jnp.float32)

        def set_up(block):
            here = pl.ds(pl.multiple_of(block * rows, rows), rows)
            k_turned[:, here] = k_ref[here, :].T
            product = cg_ref[here, :].astype(jnp.float32) * ctx_ref[here, :].astype(jnp.float32)
            delta[:, here] = dot(select, product, NT, lax.Precision.HIGHEST)

        each(2 * chips, set_up)

        def attend_back(query_block, key_block):
            base_q = pl.multiple_of(query_block * rows, rows)
            base_k = pl.multiple_of(key_block * rows, rows)
            rows_q, rows_k = pl.ds(base_q, rows), pl.ds(base_k, rows)
            queries = (q_ref[rows_q, :] * 0.125).astype(LOW)
            incoming = cg_ref[rows_q, :]
            keys, vals = k_ref[rows_k, :], v_ref[rows_k, :]
            key_ids = base_k + lax.broadcasted_iota(jnp.int32, (rows, rows), 0)
            query_ids = base_q + lax.broadcasted_iota(jnp.int32, (1, rows), 1)
            visible = (key_ids >= start_ref[:, rows_q]) & (key_ids <= query_ids)
            dk, dv = dk_acc[rows_k, :], dv_acc[rows_k, :]
            for h in range(heads):
                masked, incoming_masked = queries * masks[h], incoming * masks[h]
                scores = dot(keys, masked, NT)
                prob = jnp.where(visible, jnp.exp(scores - lse_ref[h : h + 1, rows_q]), 0.0)
                dprob = dot(vals, incoming_masked, NT)
                dscore = (prob * (dprob - delta[h : h + 1, rows_q])).astype(LOW)
                dv = dv + dot(prob.astype(LOW), incoming_masked)
                dk = dk + dot(dscore, masked)
                band = slice(h * HD, (h + 1) * HD)
                dq_acc[band, rows_q] += dot(k_turned[band, rows_k], dscore)
            dk_acc[rows_k, :] = dk
            dv_acc[rows_k, :] = dv

        def turn_back(values, here):
            parts = [
                rope_tile(
                    values[:, t * tile : (t + 1) * tile],
                    cos_ref[here, :],
                    sin_low_ref[here, :],
                    sin_high_ref[here, :],
                    -1.0,
                )
                for t in range(in_width // tile)
            ]
            return jnp.concatenate(parts, axis=1) if len(parts) > 1 else parts[0]

        def prepare(turn, chip):
            def with_chip(other):
                done = 0
                for earlier in range(chips):
                    done = done + jnp.where(
                        (scatter.order(earlier) == other) & (earlier < turn), 1, 0
                    )
                upper, lower = jnp.maximum(chip, other), jnp.minimum(chip, other)

                @pl.when(done == 0)
                def _():
                    def one(number):
                        query_block = upper * 2 + number // 2
                        key_block = lower * 2 + number % 2
                        pl.when(
                            (key_block <= query_block) & (query_block - key_block <= reach)
                        )(lambda: attend_back(query_block, key_block))

                    each(4, one)

            each(chips, with_chip)

            def finish(core):
                here = pl.ds(pl.multiple_of((chip * 2 + core) * rows, rows), rows)
                dq = turn_back(dq_acc[:, here].T * 0.125, here).astype(LOW)
                dk = turn_back(dk_acc[here, :], here).astype(LOW)
                dv = dv_acc[here, :].astype(LOW)
                for number, (ref, values) in enumerate(((dq_ref, dq), (dk_ref, dk), (dv_ref, dv))):
                    ref[here, :] = values
                    bias[number : number + 1, :] += jnp.sum(
                        values.astype(jnp.float32), axis=0, keepdims=True
                    )

            each(2, finish)

        def work(chip, core):
            here = pl.ds(pl.multiple_of((chip * 2 + core) * rows, rows), rows)
            term = dot(dq_ref[here, :], w_ref[0], NT)
            term = term + dot(dk_ref[here, :], w_ref[1], NT)
            return term + dot(dv_ref[here, :], w_ref[2], NT)

        exchange_qkv = Exchange(place, staged_qkv, landed_qkv, one)
        exchange_out = Exchange(place, staged_out, landed_out, two)

        def columns_of(offset):
            block = lax.rem(place.group + offset, groups)
            return pl.ds(pl.multiple_of(block * part, part), part)

        def fetch(source, index):
            columns = columns_of(lax.rem(index + 1, groups))
            slot = lax.rem(index, 2)
            return pltpu.make_async_copy(
                source.at[:, columns], columns_in.at[slot], load_columns.at[slot]
            )

        def fill_out(index):
            fetch(full_hbm, index).wait()
            offset = lax.rem(index + 1, groups)
            staged_out[offset] = dot(ctx_ref[...], columns_in[lax.rem(index, 2)], TN).astype(LOW)
            pl.when(offset > 0)(lambda: exchange_out.copy(offset).start())
            pl.when(offset == 0)(lambda: exchange_out.stay().start())
            pl.when(index + 2 < groups)(lambda: fetch(full_hbm, index + 2).start())
            pl.when(index + 2 >= groups)(lambda: fetch(a_hbm, index + 2 - groups).start())

        def fill_qkv(index):
            fetch(a_hbm, index).wait()
            offset = lax.rem(index + 1, groups)
            values = columns_in[lax.rem(index, 2)]
            for number, ref in enumerate((dq_ref, dk_ref, dv_ref)):
                staged_qkv[offset, number] = dot(values, ref[...], TN).astype(LOW)
            pl.when(offset > 0)(lambda: exchange_qkv.copy(offset).start())
            pl.when(offset == 0)(lambda: exchange_qkv.stay().start())
            pl.when(index + 2 < groups)(lambda: fetch(a_hbm, index + 2).start())

        fetch(full_hbm, 0).start()
        fetch(full_hbm, 1).start()
        scatter = PreparedScatter(place, work, scratch, prepare)
        scatter.first()

        def step(number):
            scatter.slot(number)

            @pl.when(number == 0)
            def _():
                early_a.begin(sums_ref[...])
                for copy in fetches[9:]:
                    copy.wait()
                each(groups, fill_out)

        each(chips - 1, step)
        scatter.last()
        each(groups, fill_qkv)
        early_groups[place.group] = jnp.zeros(early_groups.shape[1:], jnp.float32)
        early_groups[place.group, 4:7, 0:in_width] = bias[0:3, :]
        early_groups[place.group, 0:2, :] = early_a.result()
        early_b.begin(early_groups[place.group])
        _, plain, inverse = layer_norm_parts(
            x_ref[...].astype(jnp.float32), gain_ref[...], shift_ref[...]
        )
        scatter.own(total)
        back, gain_grad, shift_grad = layer_norm_back(total[...], plain, inverse, gain_ref[...])
        late_a.begin(jnp.concatenate([gain_grad[None, :], shift_grad[None, :]], axis=0))
        in_ref[...] = (mg_ref[...] + back).astype(LOW)
        scatter.drain()
        late_b.begin(late_a.result())
        first = early_b.result()
        last = late_b.result()
        small_ref[...] = first
        small_ref[1:2, :] = first[0:1, :]
        small_ref[3:4, :] = first[1:2, :]
        small_ref[0:1, :] = last[0:1, :]
        small_ref[2:3, :] = last[1:2, :]
        exchange_qkv.wait()
        exchange_out.wait()

    devices = 2 * chips
    heads_kind = pltpu.VMEM((length, in_width), LOW)
    heads_sum = pltpu.VMEM((length, in_width), jnp.float32)
    return line_call(
        kernel,
        "scatter_triple",
        6,
        (
            start, lse, gain, shift, sums,
            *qkv, context_grad, context, *tables, weights, tokens, mid_grad, normed, grads,
        ),
        [
            shape((rows, width)),
            shape((8, width), jnp.float32),
            shape((groups, 3, part, in_width)),
            shape((groups, in_width, part)),
        ],
        [
            *(heads_kind for _ in range(5)),
            *(pltpu.VMEM((length, tile), jnp.float32) for _ in range(3)),
            pltpu.VMEM(weights.shape, LOW),
            pltpu.VMEM((rows, width), LOW),
            pltpu.VMEM((rows, width), jnp.float32),
            pltpu.VMEM((2, length, part), LOW),
            pltpu.SemaphoreType.DMA((11,)),
            pltpu.SemaphoreType.DMA((2,)),
            pltpu.VMEM((in_width, length), LOW),
            pltpu.VMEM((in_width, length), jnp.float32),
            heads_sum,
            heads_sum,
            pltpu.VMEM((8, length), jnp.float32),
            heads_kind,
            heads_kind,
            heads_kind,
            pltpu.VMEM((8, in_width), jnp.float32),
            pltpu.VMEM((rows, width), jnp.float32),
            pltpu.VMEM((groups, 3, part, in_width), LOW),
            pltpu.VMEM((groups, in_width, part), LOW),
            pltpu.VMEM((devices, 2, width), jnp.float32),
            pltpu.VMEM((groups, 8, width), jnp.float32),
            pltpu.VMEM((devices, 2, width), jnp.float32),
            pltpu.VMEM((groups, 2, width), jnp.float32),
        ]
        + Scatter.scratch(chips, rows, width)
        + Spread.scratch(groups) * 2
        + [pltpu.SemaphoreType.DMA((n,)) for n in (devices, devices, groups, groups) * 2],
        COST_FLOPS,
        in_hbm=(2, 3),
        from_hbm=tuple(range(5, 18)),
    )


def adam_update(master, gradient, moment_one, moment_two, correct_one, correct_two, rate):
    one_new = 0.9 * moment_one + 0.1 * gradient
    two_new = 0.999 * moment_two + 0.001 * gradient * gradient
    change = one_new / correct_one / (jnp.sqrt(two_new / correct_two) + 1e-08) + 0.1 * master
    return (master - rate * change, one_new, two_new)


def per_device(
    groups,
    chips,
    inputs,
    out_grad,
    segments,
    w_qkv,
    w_out,
    w_gate_up,
    w_down,
    qkv_bias,
    norm_gain,
    norm_bias,
    first_qkv,
    first_out,
    first_gate_up,
    first_down,
    first_bias,
    first_gain,
    first_shift,
    second_qkv,
    second_out,
    second_gate_up,
    second_down,
    second_bias,
    second_gain,
    second_shift,
):
    length = segments.shape[1]
    head_width = w_qkv.shape[2]
    gains = (norm_gain[0:1], norm_gain[1:2])
    shifts = (norm_bias[0:1], norm_bias[1:2])
    place = positions(segments)[0]
    start = jnp.arange(length, dtype=jnp.int32) - place
    start = start[None, :]
    tables = rotary_tables(place, min(head_width, 128))

    gate_up_turned = jnp.swapaxes(w_gate_up, 1, 2)
    normed_one_all, qkv_all, out_all, down_one, *qkv = gather_project(
        groups,
        chips,
        inputs,
        gains[0],
        shifts[0],
        (w_qkv, w_out, w_down),
        qkv_bias,
        tables,
    )
    middle, context_flat, lse, mlp_grad, pair_all, down_two = scatter_heads(
        groups, chips, qkv, start, out_all, inputs, out_grad, (gate_up_turned, w_down)
    )
    down_parts = (down_one, down_two)
    normed_two_all, hidden_low, gate_grad, up_grad, normed_two_grad, parts_down = hidden_layers(
        groups, chips, middle, gains[1], shifts[1], pair_all, down_parts, mlp_grad
    )
    attn_grad_all, context_grad, middle_grad, sums_two, outputs, parts_pair = (
        gather_context(
            groups,
            chips,
            middle,
            normed_two_grad,
            out_grad,
            gains[1],
            shifts[1],
            out_all,
            hidden_low,
            down_parts,
            normed_two_all,
            (gate_grad, up_grad),
        )
    )
    input_grad, small, parts_qkv, parts_out = scatter_triple(
        groups,
        chips,
        qkv,
        start,
        lse,
        context_flat,
        context_grad,
        tables,
        qkv_all,
        inputs,
        gains[0],
        shifts[0],
        middle_grad,
        sums_two,
        normed_one_all,
        attn_grad_all,
    )

    def add_parts(parts):
        total = parts[0].astype(jnp.float32)
        for offset in range(1, groups):
            total = total + parts[offset].astype(jnp.float32)
        return total

    grad_qkv, grad_out, grad_down = add_parts(parts_qkv), add_parts(parts_out), add_parts(parts_down)
    grad_gate_up = jnp.swapaxes(add_parts(parts_pair), 1, 2)
    grad_bias = small[4:7, :head_width]
    grad_gain, grad_shift = small[0:2], small[2:4]
    correct_one = 1.0 - 0.9**STEP
    correct_two = 1.0 - 0.999**STEP
    rates = (0.02, 0.3, 0.02, 0.02, 0.3, 0.3, 0.3)
    masters = (w_qkv, w_out, w_gate_up, w_down, qkv_bias, norm_gain, norm_bias)
    gradients = (grad_qkv, grad_out, grad_gate_up, grad_down, grad_bias, grad_gain, grad_shift)
    firsts = (first_qkv, first_out, first_gate_up, first_down, first_bias, first_gain, first_shift)
    seconds = (
        second_qkv,
        second_out,
        second_gate_up,
        second_down,
        second_bias,
        second_gain,
        second_shift,
    )
    updated = [
        adam_update(
            masters[number],
            gradients[number],
            firsts[number],
            seconds[number],
            correct_one,
            correct_two,
            rates[number],
        )
        for number in range(7)
    ]
    return (
        outputs,
        input_grad,
        grad_qkv,
        grad_out,
        grad_gate_up,
        grad_down,
        grad_bias,
        grad_gain,
        grad_shift,
        updated[0][0],
        updated[1][0],
        updated[2][0],
        updated[3][0],
        updated[4][0],
        updated[5][0],
        updated[6][0],
        updated[0][1],
        updated[1][1],
        updated[2][1],
        updated[3][1],
        updated[4][1],
        updated[5][1],
        updated[6][1],
        updated[0][2],
        updated[1][2],
        updated[2][2],
        updated[3][2],
        updated[4][2],
        updated[5][2],
        updated[6][2],
    )


def solution(mesh):
    in_specs = (
        P(("dp", "tensor"), None),
        P(("dp", "tensor"), None),
        P("dp", None),
        P(None, "dp", "tensor"),
        P("tensor", "dp"),
        P(None, "dp", "tensor"),
        P("tensor", "dp"),
        P(None, "tensor"),
        P(),
        P(),
        P(None, "dp", "tensor"),
        P("tensor", "dp"),
        P(None, "dp", "tensor"),
        P("tensor", "dp"),
        P(None, "tensor"),
        P(),
        P(),
        P(None, "dp", "tensor"),
        P("tensor", "dp"),
        P(None, "dp", "tensor"),
        P("tensor", "dp"),
        P(None, "tensor"),
        P(),
        P(),
    )
    out_specs = (
        P(("dp", "tensor"), None),
        P(("dp", "tensor"), None),
        P(None, "dp", "tensor"),
        P("tensor", "dp"),
        P(None, "dp", "tensor"),
        P("tensor", "dp"),
        P(None, "tensor"),
        P(),
        P(),
        P(None, "dp", "tensor"),
        P("tensor", "dp"),
        P(None, "dp", "tensor"),
        P("tensor", "dp"),
        P(None, "tensor"),
        P(),
        P(),
        P(None, "dp", "tensor"),
        P("tensor", "dp"),
        P(None, "dp", "tensor"),
        P("tensor", "dp"),
        P(None, "tensor"),
        P(),
        P(),
        P(None, "dp", "tensor"),
        P("tensor", "dp"),
        P(None, "dp", "tensor"),
        P("tensor", "dp"),
        P(None, "tensor"),
        P(),
        P(),
    )
    return jax.shard_map(
        functools.partial(per_device, mesh.shape["dp"], mesh.shape["tensor"] // 2),
        mesh=mesh, in_specs=in_specs, out_specs=out_specs, check_vma=False
    )
```

```python
import functools

import jax
import jax.numpy as jnp
from jax import lax
from jax.experimental import pallas as pl
from jax.experimental.pallas import tpu as pltpu
from jax.sharding import PartitionSpec as P

HD = 64
ROT = 16
STEP = 10


def layer_norm_parts(values, gain_row, shift_row):
    average = jnp.mean(values, axis=-1, keepdims=True)
    centred = values - average
    inverse = lax.rsqrt(jnp.mean(centred * centred, axis=-1, keepdims=True) + 1e-05)
    normed = centred * inverse
    return (normed * gain_row + shift_row, normed, inverse)


def layer_norm_back(incoming, normed, inverse, gain_row):
    scaled = incoming * gain_row
    inner = (
        scaled
        - jnp.mean(scaled, axis=-1, keepdims=True)
        - normed * jnp.mean(scaled * normed, axis=-1, keepdims=True)
    )
    return (inner * inverse, jnp.sum(incoming * normed, axis=0), jnp.sum(incoming, axis=0))


NEG = -1e30
BLK = 256
NT = (((1,), (1,)), ((), ()))
NN = (((1,), (0,)), ((), ()))


def dot(left, right, dims=NN, precision=None):
    return lax.dot_general(
        left, right, dims, preferred_element_type=jnp.float32, precision=precision
    )


def head_masks(width, dtype):
    lane = lax.broadcasted_iota(jnp.int32, (1, width), 1)
    return [(lane // HD == h).astype(dtype) for h in range(width // HD)]


def rope_tile(tile, cosine, sine, sign):
    width = tile.shape[-1]
    lane = lax.rem(lax.broadcasted_iota(jnp.int32, tile.shape, 1), HD)
    ahead = pltpu.roll(tile, width - ROT // 2, 1)
    behind = pltpu.roll(tile, ROT // 2, 1)
    return tile * cosine + sign * (jnp.where(lane < ROT // 2, ahead, behind) * sine)


def attend(number, size, k_ref, v_turned, masked, starts, query_ids, acc, stats):
    base = pl.multiple_of(number * 2 * size, 2 * size)
    keys = k_ref[pl.ds(base, 2 * size), :]
    key_ids = base + lax.broadcasted_iota(jnp.int32, (2 * size, size), 0)
    visible = (key_ids >= starts) & (key_ids <= query_ids)
    for h, queries in enumerate(masked):
        scores = jnp.where(visible, dot(keys, queries, NT), NEG)
        peak_old = stats[h : h + 1, :]
        peak = jnp.maximum(peak_old, jnp.max(scores, axis=0, keepdims=True))
        fade = jnp.exp(peak_old - peak)
        prob = jnp.exp(scores - peak)
        stats[h : h + 1, :] = peak
        stats[8 + h : 9 + h, :] = stats[8 + h : 9 + h, :] * fade + jnp.sum(
            prob, axis=0, keepdims=True
        )
        band = slice(h * HD, (h + 1) * HD)
        acc[band, :] = acc[band, :] * fade + dot(
            v_turned[band, pl.ds(base, 2 * size)], prob.astype(jnp.bfloat16)
        )


MESH = pl.DeviceIdType.MESH
VMEM_BYTES = (127 << 20) // 2
LONGEST = 1024
DOCUMENTS = 4
TN = (((0,), (0,)), ((), ()))
LOW = jnp.bfloat16


def remote(source, target, send, receive, device):
    return pltpu.make_async_remote_copy(
        src_ref=source,
        dst_ref=target,
        send_sem=send,
        recv_sem=receive,
        device_id=device,
        device_id_type=MESH,
    )


class Place:
    def __init__(self, groups, chips):
        self.groups, self.chips = groups, chips
        self.group = lax.axis_index("dp")
        self.spot = lax.axis_index("tensor")
        self.chip, self.core = self.spot // 2, self.spot % 2

    def at(self, chip, core):
        return (self.group, chip * 2 + core)

    def peer(self, offset):
        return (lax.rem(self.group + offset, self.groups), self.spot)

    def fellow(self, offset):
        return (self.group, lax.rem(self.spot + offset, 2 * self.chips))

    def barrier(self, with_groups=False, with_all_spots=False):
        semaphore = pltpu.get_barrier_semaphore()

        def greet(target):
            pl.semaphore_signal(semaphore, inc=1, device_id=target, device_id_type=MESH)

        if with_all_spots:
            for offset in range(1, 2 * self.chips):
                greet(self.fellow(offset))
            count = 2 * self.chips - 1
        else:
            greet(self.at(self.chip, 1 - self.core))
            pl.when(self.chip > 0)(lambda: greet(self.at(self.chip - 1, self.core)))
            pl.when(self.chip < self.chips - 1)(lambda: greet(self.at(self.chip + 1, self.core)))
            count = 1 + jnp.where(self.chip > 0, 1, 0) + jnp.where(self.chip < self.chips - 1, 1, 0)
        if with_groups:
            for offset in range(1, self.groups):
                greet(self.peer(offset))
            count = count + self.groups - 1
        pl.semaphore_wait(semaphore, count)


def each(count, use):
    def one(index, _):
        use(index)
        return 0

    lax.fori_loop(0, count, one, 0)


def block_of(ref, index, size):
    return ref.at[pl.ds(pl.multiple_of(index * size, size), size)]


def fetch_all(pairs, sems):
    copies = [pltpu.make_async_copy(a, b, sems.at[n]) for n, (a, b) in enumerate(pairs)]
    for copy in copies:
        copy.start()
    return copies


HALVES = 2


class Gather:
    SEMS = 5

    def __init__(self, place, full, sems, kept=None, keep_sem=None):
        self.place, self.full, self.kept, self.keep_sem = place, full, kept, keep_sem
        self.line_in, self.core_in, self.right_out, self.left_out, self.core_out = sems
        self.rows = full.shape[0] // (2 * place.chips)

    @classmethod
    def scratch(cls, chips):
        return [pltpu.SemaphoreType.DMA((chips * HALVES,)) for _ in range(cls.SEMS)]

    def own(self):
        return block_of(self.full, self.place.spot, self.rows)

    def block(self, chip, core, half):
        return block_of(self.full, (chip * 2 + core) * HALVES + half, self.rows // HALVES)

    def right(self, which, half):
        place, part = self.place, self.block(which, self.place.core, half)
        target = place.at(jnp.minimum(place.chip + 1, place.chips - 1), place.core)
        index = which * HALVES + half
        return remote(part, part, self.right_out.at[index], self.line_in.at[index], target)

    def left(self, which, half):
        place, part = self.place, self.block(which, self.place.core, half)
        target = place.at(jnp.maximum(place.chip - 1, 0), place.core)
        index = which * HALVES + half
        return remote(part, part, self.left_out.at[index], self.line_in.at[index], target)

    def across(self, which, core, half):
        place, part = self.place, self.block(which, core, half)
        target = place.at(place.chip, 1 - place.core)
        index = which * HALVES + half
        return remote(part, part, self.core_out.at[index], self.core_in.at[index], target)

    def begin(self, halves=range(HALVES)):
        chip, chips = self.place.chip, self.place.chips
        for half in halves:
            pl.when(chip < chips - 1)(lambda: self.right(chip, half).start())
            pl.when(chip > 0)(lambda: self.left(chip, half).start())
        for half in halves:
            self.across(chip, self.place.core, half).start()

    def pass_on(self, step, halves=range(HALVES)):
        chip, chips, core = self.place.chip, self.place.chips, self.place.core
        low, high = chip - 1 - step, chip + 1 + step
        for half in halves:

            @pl.when(low >= 0)
            def _():
                self.right(low, half).wait_recv()
                pl.when(chip < chips - 1)(lambda: self.right(low, half).start())
                self.across(low, core, half).start()

            @pl.when(high < chips)
            def _():
                self.left(high, half).wait_recv()
                pl.when(chip > 0)(lambda: self.left(high, half).start())
                self.across(high, core, half).start()

    def keep(self, which):
        part = block_of(self.full, which, 2 * self.rows)
        return pltpu.make_async_copy(
            part, block_of(self.kept, which, 2 * self.rows), self.keep_sem.at[which]
        )

    def wait_chip(self, which, halves=range(HALVES)):
        for half in halves:
            self.across(which, 1 - self.place.core, half).wait_recv()
        if self.kept is not None and HALVES - 1 in halves:
            self.keep(which).start()

    def each_new(self, step, use, halves=range(HALVES)):
        low, high = self.place.chip - 1 - step, self.place.chip + 1 + step

        @pl.when(low >= 0)
        def _():
            self.wait_chip(low, halves)
            use(low)

        @pl.when(high < self.place.chips)
        def _():
            self.wait_chip(high, halves)
            use(high)

    def drain(self):
        chip, chips, core = self.place.chip, self.place.chips, self.place.core

        def one(which):
            for half in range(HALVES):
                self.across(which, core, half).wait_send()
                pl.when((which <= chip) & (chip < chips - 1))(
                    lambda: self.right(which, half).wait_send()
                )
                pl.when((which >= chip) & (chip > 0))(lambda: self.left(which, half).wait_send())
            if self.kept is not None:
                self.keep(which).wait()

        each(chips, one)


class Scatter:
    def __init__(self, place, work, scratch, halves=HALVES):
        self.place, self.work, self.halves = place, work, halves
        self.out, self.side, self.line = scratch[:3]
        self.core_out, self.core_in, self.line_out, self.line_in = scratch[3:]
        self.part = self.out.shape[1] // halves
        chip, chips = place.chip, place.chips
        self.near = jnp.minimum(chip, chips - 1 - chip)
        self.alone = chips - 1 - 2 * self.near
        self.flip = jnp.where(chip * 2 < chips, 0, 1)
        self.lag = jnp.where(self.near > 0, 1, 0)

    @staticmethod
    def scratch(chips, rows, width):
        return [
            pltpu.VMEM((chips, rows, width), LOW),
            pltpu.VMEM((chips, rows, width), LOW),
            pltpu.VMEM((chips + 1, rows, width), LOW),
            pltpu.SemaphoreType.DMA((chips,)),
            pltpu.SemaphoreType.DMA((chips,)),
            pltpu.SemaphoreType.DMA((chips * HALVES,)),
            pltpu.SemaphoreType.DMA(((chips + 1) * HALVES,)),
        ]

    SCRATCH = 7

    def order(self, turn):
        chips = self.place.chips
        later = jnp.maximum(turn - self.alone, 0)
        pair = later // 2
        far = jnp.where(turn < self.alone, chips - 1 - turn, chips - 1 - self.alone - pair)
        which = jnp.where((turn >= self.alone) & (later % 2 == 1), pair, far)
        which = jnp.where(turn == chips - 1, self.near, which)
        return jnp.where(self.flip == 1, chips - 1 - which, which)

    def across(self, which):
        place = self.place
        return remote(
            self.out.at[which],
            self.side.at[which],
            self.core_out.at[which],
            self.core_in.at[which],
            place.at(place.chip, 1 - place.core),
        )

    def hop(self, which, slot, half, target):
        rows = slice(half * self.part, (half + 1) * self.part)
        return remote(
            self.out.at[which, rows],
            self.line.at[slot, rows],
            self.line_out.at[which * self.halves + half],
            self.line_in.at[slot * self.halves + half],
            self.place.at(target, self.place.core),
        )

    def right(self, which, half):
        place = self.place
        slot = jnp.where(which == place.chip + 1, place.chips, which)
        return self.hop(which, slot, half, jnp.minimum(place.chip + 1, place.chips - 1))

    def left(self, which, half):
        return self.hop(which, which, half, jnp.maximum(self.place.chip - 1, 0))

    def arrived(self, slot, half):
        place = self.place
        rows = slice(half * self.part, (half + 1) * self.part)
        part = self.line.at[slot, rows]
        other = place.at(place.chip, 1 - place.core)
        remote(
            part, part, self.line_out.at[0], self.line_in.at[slot * self.halves + half], other
        ).wait_recv()
        return self.line[slot, rows].astype(jnp.float32)

    def produce(self, turn):
        which = self.order(turn)
        self.out[which] = self.work(which, 1 - self.place.core).astype(LOW)
        self.across(which).start()

    def chip_sum(self, which):
        mine = self.work(which, self.place.core)
        self.across(which).wait()
        return mine + self.side[which].astype(jnp.float32)

    def send(self, which, upstream, copy):
        total = self.chip_sum(which)

        @pl.when(upstream)
        def _():
            for half in range(self.halves):
                rows = slice(half * self.part, (half + 1) * self.part)
                self.out[which, rows] = (total[rows] + self.arrived(which, half)).astype(LOW)
                copy(which, half).start()

        @pl.when(jnp.logical_not(upstream))
        def _():
            for half in range(self.halves):
                rows = slice(half * self.part, (half + 1) * self.part)
                self.out[which, rows] = total[rows].astype(LOW)
                copy(which, half).start()

    def first(self):
        pl.when(self.lag == 1)(lambda: self.produce(0))

    def slot(self, number, before_last=None):
        chip, chips = self.place.chip, self.place.chips
        if before_last is None:
            self.produce(number + self.lag)
        else:
            pl.when(self.lag == 0)(lambda: self.produce(number))
            pl.when((self.lag == 1) & (number == chips - 2))(before_last)
        right = chips - 1 - (number - chip)
        left = number - (chips - 1 - chip)
        pl.when((number >= chip) & (right > chip))(
            lambda: self.send(right, chip > 0, self.right)
        )
        pl.when((left >= 0) & (left < chip))(
            lambda: self.send(left, chip < chips - 1, self.left)
        )
        if before_last is not None:
            count = jnp.where(number < chips - 3, 1, jnp.where(number == chips - 3, 2, 0))
            pl.when(self.lag == 1)(
                lambda: each(count, lambda index: self.produce(number + 1 + index))
            )

    def last(self):
        pl.when(self.lag == 0)(lambda: self.produce(self.place.chips - 1))

    def own(self, total):
        chip, chips = self.place.chip, self.place.chips
        total[...] = self.chip_sum(chip)
        for half in range(self.halves):
            rows = slice(half * self.part, (half + 1) * self.part)

            @pl.when(chip > 0)
            def _():
                total[rows] += self.arrived(chips, half)

            @pl.when(chip < chips - 1)
            def _():
                total[rows] += self.arrived(chip, half)

    def drain(self):
        chip = self.place.chip

        def one(which):
            for half in range(self.halves):
                pl.when(which > chip)(lambda: self.right(which, half).wait_send())
                pl.when(which < chip)(lambda: self.left(which, half).wait_send())

        each(self.place.chips, one)


class StoredScatter(Scatter):
    def __init__(self, place, scratch, mine):
        super().__init__(place, None, scratch, 1)
        self.mine = mine

    def put(self, which, other, own):
        self.out[which] = other.astype(LOW)
        self.across(which).start()
        self.mine[which] = own.astype(LOW)

    def produce(self, turn):
        pass

    def chip_sum(self, which):
        self.across(which).wait()
        return self.mine[which].astype(jnp.float32) + self.side[which].astype(jnp.float32)


class Spread:
    def __init__(self, place, shard, staged, whole, axis, sems):
        self.place, self.staged, self.whole, self.sems = place, staged, whole, sems
        size = shard.shape[axis]
        here = pl.ds(pl.multiple_of(place.group * size, size), size)
        self.mine = whole.at[tuple(here if a == axis else slice(None) for a in range(len(shard.shape)))]
        staged[...] = shard[...].astype(LOW)

    @staticmethod
    def scratch(groups):
        return [pltpu.SemaphoreType.DMA((groups,)), pltpu.SemaphoreType.DMA((groups,))]

    def copy(self, offset):
        return remote(
            self.staged,
            self.mine,
            self.sems[0].at[offset],
            self.sems[1].at[offset],
            self.place.peer(offset),
        )

    def stay(self):
        return pltpu.make_async_copy(self.staged, self.mine, self.sems[0].at[0])

    def start(self):
        for offset in range(1, self.place.groups):
            self.copy(offset).start()
        self.stay().start()

    def wait(self):
        for offset in range(1, self.place.groups):
            self.copy(offset).wait()
        self.stay().wait()


class Exchange:
    def __init__(self, place, staged, landed, sems):
        self.place, self.staged, self.landed = place, staged, landed
        self.send, self.receive = sems

    def copy(self, offset):
        return remote(
            self.staged.at[offset],
            self.landed.at[offset],
            self.send.at[offset],
            self.receive.at[offset],
            self.place.peer(offset),
        )

    def stay(self):
        return pltpu.make_async_copy(self.staged.at[0], self.landed.at[0], self.send.at[0])

    def wait(self):
        def one(offset, _):
            self.copy(offset).wait()
            return 0

        lax.fori_loop(1, self.place.groups, one, 0)
        self.stay().wait()


class SmallSum:
    def __init__(self, slots, me, count, target, sems):
        self.slots, self.me, self.count, self.target = slots, me, count, target
        self.send, self.receive = sems

    def copy(self, offset):
        part = self.slots.at[self.me]
        return remote(
            part, part, self.send.at[offset], self.receive.at[self.me], self.target(offset)
        )

    def begin(self, rows):
        self.slots[self.me] = rows
        for offset in range(1, self.count):
            self.copy(offset).start()

    def result(self):
        for offset in range(1, self.count):
            source = lax.rem(self.me + offset, self.count)
            part = self.slots.at[source]
            remote(
                part, part, self.send.at[offset], self.receive.at[source], self.target(offset)
            ).wait_recv()
        total = self.slots[0]
        for index in range(1, self.count):
            total = total + self.slots[index]
        for offset in range(1, self.count):
            self.copy(offset).wait_send()
        return total


def pieces(number, groups, fill):
    @pl.when(number == 0)
    def _():
        each(groups - 1, lambda index: fill(index + 1))


def line_call(kernel, name, number, operands, out_shape, scratch, flops, in_hbm=(), from_hbm=()):
    whole, hbm = pl.BlockSpec(memory_space=pltpu.VMEM), pl.BlockSpec(memory_space=pl.ANY)
    ins = [hbm if n in from_hbm else whole for n in range(len(operands))]
    outs = [hbm if n in in_hbm else whole for n in range(len(out_shape))]
    return pl.pallas_call(
        kernel,
        out_shape=out_shape,
        in_specs=ins,
        out_specs=outs,
        scratch_shapes=scratch,
        compiler_params=pltpu.CompilerParams(
            collective_id=number, has_side_effects=True, vmem_limit_bytes=VMEM_BYTES
        ),
        cost_estimate=pl.CostEstimate(flops=flops, bytes_accessed=0, transcendentals=0),
        name=name,
    )(*operands)


COST_FLOPS = 80_000_000_000


def shape(dims, kind=LOW):
    return jax.ShapeDtypeStruct(dims, kind)


def split_refs(refs, *counts):
    parts, at = [], 0
    for count in counts:
        parts.append(refs[at : at + count])
        at += count
    return parts


def gather_project(groups, chips, tokens, gain, shift, shards, bias, segments, rates):
    rows, width = tokens.shape
    length = rows * 2 * chips
    qkv_shard, out_shard, down_shard = shards
    part, out_width = qkv_shard.shape[1:]
    upper = down_shard.shape[0] // 2
    tile = rates.shape[1]

    def kernel(
        x_ref, gain_ref, shift_ref, qkv_ref, out_ref, down_ref, bias_ref, segment_ref, rate_ref,
        kept, weights_kept, out_whole, down_whole, q_ref, k_ref, v_ref,
        k_turned, v_turned, start_ref, cos_ref, sin_ref,
        full, weights, qkv_staged, out_staged, down_staged, load, keep_sem, *sems
    ):
        place = Place(groups, chips)
        line, one, two, three = split_refs(sems, Gather.SEMS, 2, 2, 2)
        gather = Gather(place, full, line, kept, keep_sem)
        normed, _, _ = layer_norm_parts(
            x_ref[...].astype(jnp.float32), gain_ref[...], shift_ref[...]
        )
        gather.own()[...] = normed.astype(LOW)
        spread_qkv = Spread(place, qkv_ref, qkv_staged, weights, 1, one)
        place.barrier(True)
        gather.begin()
        spread_qkv.start()
        spread_out = Spread(place, out_ref, out_staged, out_whole, 1, two)
        spread_out.start()
        spread_down = Spread(place, down_ref.at[0:upper], down_staged, down_whole, 1, three)
        spread_down.start()

        def work(chip):
            base = pl.multiple_of(chip * 2 * rows, 2 * rows)
            here = pl.ds(base, 2 * rows)
            values = full[here, :]
            for number, ref in enumerate((q_ref, k_ref, v_ref)):
                result = dot(values, weights[number]) + bias_ref[number : number + 1, :]
                if number < 2:
                    parts = [
                        rope_tile(
                            result[:, t * tile : (t + 1) * tile],
                            cos_ref[here, :],
                            sin_ref[here, :],
                            1.0,
                        )
                        for t in range(out_width // tile)
                    ]
                    result = jnp.concatenate(parts, axis=1) if len(parts) > 1 else parts[0]
                result = result.astype(LOW)
                ref[here, :] = result
                if number > 0:
                    (k_turned, v_turned)[number - 1][:, here] = result.T

        segment = segment_ref[...]
        start = jnp.zeros_like(segment)
        for number in range(1, DOCUMENTS):
            before = jnp.sum(jnp.where(segment < number, 1, 0), axis=1, keepdims=True)
            start = jnp.where(segment == number, before, start)
        start_ref[...] = start
        lane = lax.rem(lax.broadcasted_iota(jnp.int32, (1, tile), 1), HD)
        for block in range(length // BLK):
            here = slice(block * BLK, (block + 1) * BLK)
            ids = block * BLK + lax.broadcasted_iota(jnp.int32, (1, BLK), 1)
            spot = (ids - start[:, here]).astype(jnp.float32)
            angle = jnp.broadcast_to(spot, (tile, BLK)).T * rate_ref[...]
            sine = jnp.sin(angle)
            cos_ref[here, :] = jnp.where(lane < ROT, jnp.cos(angle), 1.0)
            sin_ref[here, :] = jnp.where(
                lane < ROT // 2, -sine, jnp.where(lane < ROT, sine, 0.0)
            )
        gather.pass_on(0)
        spread_qkv.wait()
        weights_keep = pltpu.make_async_copy(weights, weights_kept, load.at[0])
        weights_keep.start()
        gather.wait_chip(place.chip)
        work(place.chip)

        def step(number):
            pl.when(number > 0)(lambda: gather.pass_on(number))
            gather.each_new(number, work)

        each(chips - 1, step)
        weights_keep.wait()
        spread_out.wait()
        spread_down.wait()
        gather.drain()

    head_shape = shape((length, out_width))
    return line_call(
        kernel,
        "gather_project",
        1,
        (tokens, gain, shift, *shards, bias, segments, rates),
        [
            shape((length, width)),
            shape((3, width, out_width)),
            shape((out_width, width)),
            shape((upper, width)),
            head_shape,
            head_shape,
            head_shape,
            shape((out_width, length)),
            shape((out_width, length)),
            shape((1, length), jnp.int32),
            *(shape((length, tile), jnp.float32) for _ in range(2)),
        ],
        [
            pltpu.VMEM((length, width), LOW),
            pltpu.VMEM((3, width, out_width), LOW),
            pltpu.VMEM(qkv_shard.shape, LOW),
            pltpu.VMEM(out_shard.shape, LOW),
            pltpu.VMEM((upper, down_shard.shape[1]), LOW),
            pltpu.SemaphoreType.DMA((1,)),
            pltpu.SemaphoreType.DMA((chips,)),
        ]
        + Gather.scratch(chips)
        + Spread.scratch(groups) * 3,
        COST_FLOPS,
        in_hbm=(0, 1, 2, 3),
    )


def scatter_heads(groups, chips, queries, keys, values_turned, start, weight, tokens, grads, shards):
    rows, width = tokens.shape
    length, head_width = queries.shape
    heads = head_width // HD
    pair_shard, down_shard = shards
    upper = down_shard.shape[0] // 2

    def kernel(
        q_hbm, k_hbm, v_hbm, w_hbm, x_hbm, og_hbm, start_ref, pair_ref, down_ref,
        mid_ref, ctx_ref, lse_ref, kept, pair_whole, down_whole,
        full, q_ref, k_ref, w_ref, x_ref, pair_staged, down_staged,
        load, keep_sem, v_turned, acc, stats, *rest
    ):
        place = Place(groups, chips)
        scratch, line, one, two = split_refs(rest, Scatter.SCRATCH, Gather.SEMS, 2, 2)
        gather = Gather(place, full, line, kept, keep_sem)
        fetches = fetch_all(
            [
                (og_hbm, gather.own()),
                (k_hbm, k_ref),
                (v_hbm, v_turned),
                (q_hbm, q_ref),
                (w_hbm, w_ref),
                (x_hbm, x_ref),
            ],
            load,
        )
        place.barrier(True)
        fetches[0].wait()
        gather.begin()
        spread_pair = Spread(place, pair_ref, pair_staged, pair_whole, 2, one)
        spread_pair.start()
        spread_down = Spread(place, down_ref.at[upper:], down_staged, down_whole, 1, two)
        spread_down.start()
        for copy in fetches[1:5]:
            copy.wait()
        masks = head_masks(head_width, LOW)

        def work(chip, core):
            block = chip * 2 + core
            base = pl.multiple_of(block * rows, rows)
            here = pl.ds(base, rows)
            values = (q_ref[here, :] * 0.125).astype(LOW)
            masked = [values * m for m in masks]
            starts = start_ref[:, here]
            query_ids = base + lax.broadcasted_iota(jnp.int32, (1, rows), 1)
            acc[...] = jnp.zeros_like(acc)
            stats[0:8, :] = jnp.full((8, rows), NEG, jnp.float32)
            stats[8:16, :] = jnp.zeros((8, rows), jnp.float32)

            def step(number, _):
                attend(number, rows, k_ref, v_turned, masked, starts, query_ids, acc, stats)
                return 0

            first = jnp.maximum(block - LONGEST // rows, 0) // 2
            lax.fori_loop(first, block // 2 + 1, step, 0)
            for h in range(heads):
                band = slice(h * HD, (h + 1) * HD)
                acc[band, :] = acc[band, :] / stats[8 + h : 9 + h, :]
            context = acc[...].T.astype(LOW)
            ctx_ref[here, :] = context
            total = jnp.where(stats[8:16, :] > 0, stats[8:16, :], 1.0)
            lse_ref[:, here] = stats[0:8, :] + jnp.log(total)
            return dot(context, w_ref[...])

        scatter = Scatter(place, work, scratch)
        scatter.first()

        def seen(chip):
            pass

        def step(number):
            scatter.slot(number)
            gather.pass_on(number)
            pl.when(number > 0)(lambda: gather.each_new(number - 1, seen))

        each(chips - 1, step)
        scatter.last()
        fetches[5].wait()
        gather.wait_chip(place.chip)
        gather.each_new(chips - 2, seen)
        scatter.own(mid_ref)
        mid_ref[...] += x_ref[...].astype(jnp.float32)
        gather.drain()
        scatter.drain()
        spread_pair.wait()
        spread_down.wait()

    return line_call(
        kernel,
        "scatter_heads",
        2,
        (queries, keys, values_turned, weight, tokens, grads, start, *shards),
        [
            shape((rows, width), jnp.float32),
            shape((length, head_width)),
            shape((8, length), jnp.float32),
            shape((length, width)),
            shape((2, pair_shard.shape[1], width)),
            shape((down_shard.shape[0] - upper, width)),
        ],
        [
            pltpu.VMEM((length, width), LOW),
            *(pltpu.VMEM((length, head_width), LOW) for _ in range(2)),
            pltpu.VMEM((head_width, width), LOW),
            pltpu.VMEM((rows, width), LOW),
            pltpu.VMEM(pair_shard.shape, LOW),
            pltpu.VMEM((down_shard.shape[0] - upper, down_shard.shape[1]), LOW),
            pltpu.SemaphoreType.DMA((6,)),
            pltpu.SemaphoreType.DMA((chips,)),
            pltpu.VMEM((head_width, length), LOW),
            pltpu.VMEM((head_width, rows), jnp.float32),
            pltpu.VMEM((16, rows), jnp.float32),
        ]
        + Scatter.scratch(chips, rows, width)
        + Gather.scratch(chips)
        + Spread.scratch(groups) * 2,
        COST_FLOPS,
        in_hbm=(3, 4, 5),
        from_hbm=(0, 1, 2, 3, 4, 5),
    )


def hidden_layers(groups, chips, middle, gain, shift, pair_weight, down_parts, grads):
    rows, width = middle.shape
    length = rows * 2 * chips
    hidden = pair_weight.shape[1]
    upper = down_parts[0].shape[0]
    part = width // groups
    size = rows // HALVES

    def kernel(
        gain_ref, shift_ref, mid_hbm, pair_hbm, down_one, down_two, og_hbm,
        kept, hid_kept, gg_kept, ug_kept, sum_ref, landed,
        full, og_ref, pair_ref, down_ref, hid_ref, held, staged, mine, load, keep_sem, store_sem, *rest
    ):
        place = Place(groups, chips)
        first, second, line, sems = split_refs(rest, Scatter.SCRATCH, Scatter.SCRATCH, Gather.SEMS, 2)
        fetches = fetch_all(
            [
                (mid_hbm, sum_ref),
                (pair_hbm, pair_ref),
                (down_one, down_ref.at[0:upper]),
                (down_two, down_ref.at[upper:hidden]),
                (og_hbm, og_ref),
            ],
            load,
        )
        gather = Gather(place, full, line, kept, keep_sem)
        scatters = [
            StoredScatter(place, scratch, mine.at[half])
            for half, scratch in enumerate((first, second))
        ]
        exchange = Exchange(place, staged, landed, sems)
        fetches[0].wait()
        normed, _, _ = layer_norm_parts(sum_ref[...], gain_ref[...], shift_ref[...])
        gather.own()[...] = normed.astype(LOW)
        place.barrier(True)
        at_end = (place.chip == 0) | (place.chip == chips - 1)
        gather.begin((0,))
        pl.when(at_end)(lambda: gather.begin((1,)))
        for copy in fetches[1:]:
            copy.wait()

        def work(chip, half):
            pieces_of = [
                pl.ds(pl.multiple_of((chip * 2 + core) * rows + half * size, size), size)
                for core in range(2)
            ]
            values = jnp.concatenate([full[here, :] for here in pieces_of], axis=0)
            gate = dot(values, pair_ref[0], NT)
            up = dot(values, pair_ref[1], NT)
            sigmoid = 1.0 / (1.0 + jnp.exp(-gate))
            activated = gate * sigmoid
            hidden_low = (activated * up).astype(LOW)
            hidden_grad = dot(
                jnp.concatenate([og_ref[here, :] for here in pieces_of], axis=0), down_ref[...], NT
            )
            slope = sigmoid * (1.0 + gate * (1.0 - sigmoid))
            gate_grad = (hidden_grad * (up * slope)).astype(LOW)
            up_grad = (hidden_grad * activated).astype(LOW)
            held[0] = gate_grad
            held[1] = up_grad
            copies = []
            for core, here in enumerate(pieces_of):
                hid_ref[here, :] = hidden_low[core * size : (core + 1) * size]
                from_held = pl.ds(core * size, size)
                copies += [
                    pltpu.make_async_copy(hid_ref.at[here], hid_kept.at[here], store_sem.at[core]),
                    pltpu.make_async_copy(
                        held.at[0, from_held], gg_kept.at[here], store_sem.at[2 + core]
                    ),
                    pltpu.make_async_copy(
                        held.at[1, from_held], ug_kept.at[here], store_sem.at[4 + core]
                    ),
                ]
            for copy in copies:
                copy.start()
            term = dot(gate_grad, pair_ref[0]) + dot(up_grad, pair_ref[1])
            low, high = term[0:size], term[size : 2 * size]
            scatters[half].put(
                chip,
                jnp.where(place.core == 0, high, low),
                jnp.where(place.core == 0, low, high),
            )
            for copy in copies:
                copy.wait()

        def fill(offset):
            block = lax.rem(place.group + offset, groups)
            columns = pl.ds(pl.multiple_of(block * part, part), part)
            staged[offset] = dot(hid_ref[...], og_ref[:, columns], TN).astype(LOW)

        def fill_send(offset):
            fill(offset)
            exchange.copy(offset).start()

        gather.wait_chip(place.chip, (0,))
        work(place.chip, 0)

        def gather_first(step):
            gather.pass_on(step, (0,))
            gather.each_new(step, lambda chip: work(chip, 0), (0,))

        each(chips - 1, gather_first)
        pl.when(jnp.logical_not(at_end))(lambda: gather.begin((1,)))

        def both(step):
            scatters[0].slot(step)

            @pl.when(step == 0)
            def _():
                gather.wait_chip(place.chip, (1,))
                work(place.chip, 1)

            gather.pass_on(step, (1,))
            gather.each_new(step, lambda chip: work(chip, 1), (1,))

        each(chips - 1, both)

        def scatter_second(step):
            scatters[1].slot(step)
            pieces(step, groups, fill_send)
            pl.when(step == 0)(lambda: scatters[0].own(sum_ref.at[0:size]))

        each(chips - 1, scatter_second)
        fill(0)
        exchange.stay().start()
        scatters[1].own(sum_ref.at[size:rows])
        gather.drain()
        scatters[0].drain()
        scatters[1].drain()
        exchange.wait()

    hidden_shape = shape((length, hidden))
    return line_call(
        kernel,
        "gather_hidden",
        3,
        (gain, shift, middle, pair_weight, *down_parts, grads),
        [
            shape((length, width)),
            hidden_shape,
            hidden_shape,
            hidden_shape,
            shape((rows, width), jnp.float32),
            shape((groups, hidden, part)),
        ],
        [
            pltpu.VMEM((length, width), LOW),
            pltpu.VMEM((length, width), LOW),
            pltpu.VMEM(pair_weight.shape, LOW),
            pltpu.VMEM((hidden, width), LOW),
            pltpu.VMEM((length, hidden), LOW),
            pltpu.VMEM((2, rows, hidden), LOW),
            pltpu.VMEM((groups, hidden, part), LOW),
            pltpu.VMEM((HALVES, chips, size, width), LOW),
            pltpu.SemaphoreType.DMA((5,)),
            pltpu.SemaphoreType.DMA((chips,)),
            pltpu.SemaphoreType.DMA((6,)),
        ]
        + Scatter.scratch(chips, size, width) * 2
        + Gather.scratch(chips)
        + Spread.scratch(groups),
        COST_FLOPS,
        in_hbm=(0, 1, 2, 3, 5),
        from_hbm=(2, 3, 4, 5, 6),
    )


def gather_context(
    groups, chips, middle, normed_grad, out_grad, gain, shift, weight, context, hidden_low, down_parts,
    normed, pair
):
    rows, width = middle.shape
    length = rows * 2 * chips
    out_width = weight.shape[0]
    hidden = hidden_low.shape[1]
    upper = down_parts[0].shape[0]
    part = width // groups

    def kernel(
        mid_ref, ng_hbm, og_ref, gain_ref, shift_ref, w_hbm, ctx_hbm, hid_hbm, down_one, down_two,
        a_ref, gg_hbm, ug_hbm,
        kept, cg_ref, mg_ref, sums_ref, out_ref, landed, delta_ref,
        full, total, w_ref, ctx_ref, hid_ref, down_ref, gg_ref, ug_ref, staged, columns_in, load, keep_sem, *rest
    ):
        place = Place(groups, chips)
        scratch, line, sems = split_refs(rest, Scatter.SCRATCH, Gather.SEMS, 2)

        def fetch(offset):
            block = lax.rem(place.group + offset, groups)
            columns = pl.ds(pl.multiple_of(block * part, part), part)
            slot = lax.rem(offset, 2)
            return pltpu.make_async_copy(a_ref.at[:, columns], columns_in.at[slot], load.at[slot])

        arrive = pltpu.make_async_copy(ng_hbm, total, load.at[3])
        arrive.start()
        late = [
            pltpu.make_async_copy(a, b, load.at[4 + n])
            for n, (a, b) in enumerate(
                (
                    (down_one, down_ref.at[0:upper]),
                    (down_two, down_ref.at[upper:hidden]),
                    (hid_hbm, hid_ref),
                    (w_hbm, w_ref),
                    (ctx_hbm, ctx_ref),
                    (gg_hbm, gg_ref),
                    (ug_hbm, ug_ref),
                )
            )
        ]
        for copy in late:
            copy.start()
        fetch(1).start()
        gather = Gather(place, full, line, kept, keep_sem)
        _, plain, inverse = layer_norm_parts(mid_ref[...], gain_ref[...], shift_ref[...])
        arrive.wait()
        back, gain_grad, shift_grad = layer_norm_back(total[...], plain, inverse, gain_ref[...])
        mid_grad = og_ref[...].astype(jnp.float32) + back
        total[...] = mid_grad
        keep = pltpu.make_async_copy(total, mg_ref, load.at[2])
        keep.start()
        gather.own()[...] = mid_grad.astype(LOW)
        place.barrier(True)
        gather.begin()
        sums_ref[0:1, :] = gain_grad[None, :]
        sums_ref[1:2, :] = shift_grad[None, :]

        select = (
            lax.broadcasted_iota(jnp.int32, (8, out_width), 1) // HD
            == lax.broadcasted_iota(jnp.int32, (8, out_width), 0)
        ).astype(LOW)

        def back_work(chip):
            here = pl.ds(pl.multiple_of(chip * 2 * rows, 2 * rows), 2 * rows)
            context_grad = dot(full[here, :], w_ref[...], NT).astype(LOW)
            cg_ref[here, :] = context_grad
            product = context_grad.astype(jnp.float32) * ctx_ref[here, :].astype(jnp.float32)
            upper_bits = product.astype(LOW)
            lower_bits = (product - upper_bits.astype(jnp.float32)).astype(LOW)
            delta_ref[:, here] = dot(select, upper_bits, NT) + dot(select, lower_bits, NT)

        def out_work(chip, core):
            here = pl.ds(pl.multiple_of((chip * 2 + core) * rows, rows), rows)
            return dot(hid_ref[here, :], down_ref[...])

        exchange = Exchange(place, staged, landed, sems)

        def fill(offset):
            fetch(offset).wait()
            pl.when(offset > 0)(lambda: fetch(lax.rem(offset + 1, groups)).start())
            values = columns_in[lax.rem(offset, 2)]
            staged[offset, 0] = dot(gg_ref[...], values, TN).astype(LOW)
            staged[offset, 1] = dot(ug_ref[...], values, TN).astype(LOW)

        def fill_send(offset):
            fill(offset)
            exchange.copy(offset).start()

        scatter = Scatter(place, out_work, scratch)
        for copy in late[:3]:
            copy.wait()
        scatter.first()
        for copy in late[3:]:
            copy.wait()

        def step(number):
            scatter.slot(number)
            pieces(number, groups, fill_send)
            gather.pass_on(number)

            @pl.when(number == 0)
            def _():
                gather.wait_chip(place.chip)
                back_work(place.chip)

            gather.each_new(number, back_work)

        each(chips - 1, step)
        scatter.last()
        fill(jnp.int32(0))
        exchange.stay().start()
        keep.wait()
        scatter.own(total)
        out_ref[...] = (mid_ref[...] + total[...]).astype(LOW)
        gather.drain()
        scatter.drain()
        exchange.wait()

    return line_call(
        kernel,
        "gather_context",
        5,
        (middle, normed_grad, out_grad, gain, shift, weight, context, hidden_low, *down_parts, normed, *pair),
        [
            shape((length, width)),
            shape((length, out_width)),
            shape((rows, width), jnp.float32),
            shape((2, width), jnp.float32),
            shape((rows, width)),
            shape((groups, 2, hidden, part)),
            shape((8, length), jnp.float32),
        ],
        [
            pltpu.VMEM((length, width), LOW),
            pltpu.VMEM((rows, width), jnp.float32),
            pltpu.VMEM(weight.shape, LOW),
            pltpu.VMEM((length, out_width), LOW),
            pltpu.VMEM((length, hidden), LOW),
            pltpu.VMEM((hidden, width), LOW),
            pltpu.VMEM((length, hidden), LOW),
            pltpu.VMEM((length, hidden), LOW),
            pltpu.VMEM((groups, 2, hidden, part), LOW),
            pltpu.VMEM((2, length, part), LOW),
            pltpu.SemaphoreType.DMA((11,)),
            pltpu.SemaphoreType.DMA((chips,)),
        ]
        + Scatter.scratch(chips, rows, width)
        + Gather.scratch(chips)
        + Spread.scratch(groups),
        COST_FLOPS,
        in_hbm=(0, 2, 5),
        from_hbm=(1, 5, 6, 7, 8, 9, 10, 11, 12),
    )


class PreparedScatter(Scatter):
    def __init__(self, place, work, scratch, prepare):
        super().__init__(place, work, scratch)
        self.prepare = prepare

    def produce(self, turn):
        self.prepare(turn, self.order(turn))
        super().produce(turn)


def scatter_triple(
    groups, chips, qkv, keys_turned, start, lse, delta, context, context_grad, tables, weights, tokens, gain, shift,
    mid_grad, sums, normed, grads
):
    length, in_width = qkv[0].shape
    rows = length // (2 * chips)
    width = weights.shape[1]
    part = width // groups
    heads = in_width // HD
    tile = tables[0].shape[1]
    reach = LONGEST // rows

    def kernel(
        start_ref, lse_ref, delta, gain_ref, shift_ref, sums_ref,
        q_hbm, k_hbm, v_hbm, turned_hbm, cg_hbm, ctx_hbm, cos_hbm, sin_hbm,
        w_hbm, x_hbm, mg_hbm, a_hbm, full_hbm,
        in_ref, small_ref, landed_qkv, landed_out,
        q_ref, k_ref, v_ref, cg_ref, ctx_ref, cos_ref, sin_ref,
        w_ref, x_ref, mg_ref, columns_in, load, load_columns,
        k_turned, dq_acc, dk_acc, dv_acc, dq_ref, dk_ref, dv_ref, bias,
        total, norm_sums, staged_qkv, staged_out, early_spots, early_groups, late_spots, late_groups, *rest
    ):
        place = Place(groups, chips)
        scratch, one, two, sums_sems = split_refs(rest, Scatter.SCRATCH, 2, 2, 8)
        fetches = fetch_all(
            [
                (k_hbm, k_ref),
                (q_hbm, q_ref),
                (v_hbm, v_ref),
                (cg_hbm, cg_ref),
                (turned_hbm, k_turned),
                (cos_hbm, cos_ref),
                (sin_hbm, sin_ref),
                (w_hbm, w_ref),
                (ctx_hbm, ctx_ref),
                (x_hbm, x_ref),
                (mg_hbm, mg_ref),
            ],
            load,
        )
        dq_acc[...] = jnp.zeros_like(dq_acc)
        dk_acc[...] = jnp.zeros_like(dk_acc)
        dv_acc[...] = jnp.zeros_like(dv_acc)
        bias[...] = jnp.zeros_like(bias)
        spots, count = place.spot, 2 * chips
        early_a = SmallSum(early_spots, spots, count, place.fellow, sums_sems[0:2])
        early_b = SmallSum(early_groups, place.group, groups, place.peer, sums_sems[2:4])
        late_a = SmallSum(late_spots, spots, count, place.fellow, sums_sems[4:6])
        late_b = SmallSum(late_groups, place.group, groups, place.peer, sums_sems[6:8])
        for copy in fetches[:8]:
            copy.wait()
        place.barrier(True, True)
        masks = head_masks(in_width, LOW)
        def attend_back(query_block, key_chip):
            base_q = pl.multiple_of(query_block * rows, rows)
            base_k = pl.multiple_of(key_chip * 2 * rows, 2 * rows)
            rows_q, rows_k = pl.ds(base_q, rows), pl.ds(base_k, 2 * rows)
            queries = (q_ref[rows_q, :] * 0.125).astype(LOW)
            incoming = cg_ref[rows_q, :]
            keys, vals = k_ref[rows_k, :], v_ref[rows_k, :]
            key_ids = base_k + lax.broadcasted_iota(jnp.int32, (2 * rows, rows), 0)
            query_ids = base_q + lax.broadcasted_iota(jnp.int32, (1, rows), 1)
            visible = (key_ids >= start_ref[:, rows_q]) & (key_ids <= query_ids)
            probs, dscores, all_queries, all_incoming = [], [], [], []
            for h in range(heads):
                masked, incoming_masked = queries * masks[h], incoming * masks[h]
                scores = dot(keys, masked, NT)
                prob = jnp.where(visible, jnp.exp(scores - lse_ref[h : h + 1, rows_q]), 0.0)
                dprob = dot(vals, incoming_masked, NT)
                dscore = (prob * (dprob - delta[h : h + 1, rows_q])).astype(LOW)
                band = slice(h * HD, (h + 1) * HD)
                dq_acc[band, rows_q] += dot(k_turned[band, rows_k], dscore)
                probs.append(prob.astype(LOW))
                dscores.append(dscore)
                all_queries.append(masked)
                all_incoming.append(incoming_masked)
            dv_acc[rows_k, :] += dot(
                jnp.concatenate(probs, axis=1), jnp.concatenate(all_incoming, axis=0)
            )
            dk_acc[rows_k, :] += dot(
                jnp.concatenate(dscores, axis=1), jnp.concatenate(all_queries, axis=0)
            )

        def turn_back(values, here):
            parts = [
                rope_tile(
                    values[:, t * tile : (t + 1) * tile],
                    cos_ref[here, :],
                    sin_ref[here, :],
                    -1.0,
                )
                for t in range(in_width // tile)
            ]
            return jnp.concatenate(parts, axis=1) if len(parts) > 1 else parts[0]

        def prepare(turn, chip):
            def with_chip(other):
                done = 0
                for earlier in range(chips):
                    done = done + jnp.where(
                        (scatter.order(earlier) == other) & (earlier < turn), 1, 0
                    )
                upper, lower = jnp.maximum(chip, other), jnp.minimum(chip, other)

                @pl.when(done == 0)
                def _():
                    def one(number):
                        query_block = upper * 2 + number
                        pl.when(query_block - (lower * 2 + 1) <= reach)(
                            lambda: attend_back(query_block, lower)
                        )

                    each(2, one)

            each(chips, with_chip)

            def finish(core):
                here = pl.ds(pl.multiple_of((chip * 2 + core) * rows, rows), rows)
                dq = turn_back(dq_acc[:, here].T * 0.125, here).astype(LOW)
                dk = turn_back(dk_acc[here, :], here).astype(LOW)
                dv = dv_acc[here, :].astype(LOW)
                for number, (ref, values) in enumerate(((dq_ref, dq), (dk_ref, dk), (dv_ref, dv))):
                    ref[here, :] = values
                    bias[number : number + 1, :] += jnp.sum(
                        values.astype(jnp.float32), axis=0, keepdims=True
                    )

            each(2, finish)

        def work(chip, core):
            here = pl.ds(pl.multiple_of((chip * 2 + core) * rows, rows), rows)
            term = dot(dq_ref[here, :], w_ref[0], NT)
            term = term + dot(dk_ref[here, :], w_ref[1], NT)
            return term + dot(dv_ref[here, :], w_ref[2], NT)

        exchange_qkv = Exchange(place, staged_qkv, landed_qkv, one)
        exchange_out = Exchange(place, staged_out, landed_out, two)

        def columns_of(offset):
            block = lax.rem(place.group + offset, groups)
            return pl.ds(pl.multiple_of(block * part, part), part)

        def fetch(source, index):
            columns = columns_of(lax.rem(index + 1, groups))
            slot = lax.rem(index, 2)
            return pltpu.make_async_copy(
                source.at[:, columns], columns_in.at[slot], load_columns.at[slot]
            )

        def fill_out(index):
            fetch(full_hbm, index).wait()
            offset = lax.rem(index + 1, groups)
            staged_out[offset] = dot(ctx_ref[...], columns_in[lax.rem(index, 2)], TN).astype(LOW)
            pl.when(offset > 0)(lambda: exchange_out.copy(offset).start())
            pl.when(offset == 0)(lambda: exchange_out.stay().start())
            pl.when(index + 2 < groups)(lambda: fetch(full_hbm, index + 2).start())
            pl.when(index + 2 >= groups)(lambda: fetch(a_hbm, index + 2 - groups).start())

        def fill_qkv(index):
            fetch(a_hbm, index).wait()
            offset = lax.rem(index + 1, groups)
            values = columns_in[lax.rem(index, 2)]
            for number, ref in enumerate((dq_ref, dk_ref, dv_ref)):
                staged_qkv[offset, number] = dot(values, ref[...], TN).astype(LOW)
            pl.when(offset > 0)(lambda: exchange_qkv.copy(offset).start())
            pl.when(offset == 0)(lambda: exchange_qkv.stay().start())
            pl.when(index + 2 < groups)(lambda: fetch(a_hbm, index + 2).start())

        fetch(full_hbm, 0).start()
        fetch(full_hbm, 1).start()
        scatter = PreparedScatter(place, work, scratch, prepare)
        scatter.first()

        def fills():
            each(groups, fill_qkv)

        def step(number):
            scatter.slot(number, fills)

            @pl.when(number == 0)
            def _():
                early_a.begin(sums_ref[...])
                for copy in fetches[8:]:
                    copy.wait()
                each(groups, fill_out)

        each(chips - 1, step)
        scatter.last()
        pl.when(scatter.lag == 0)(fills)
        early_groups[place.group] = jnp.zeros(early_groups.shape[1:], jnp.float32)
        early_groups[place.group, 4:7, 0:in_width] = bias[0:3, :]
        early_groups[place.group, 0:2, :] = early_a.result()
        early_b.begin(early_groups[place.group])
        scatter.own(total)
        size = rows // 4
        norm_sums[...] = jnp.zeros_like(norm_sums)

        def norm_back(block):
            here = pl.ds(pl.multiple_of(block * size, size), size)
            _, plain, inverse = layer_norm_parts(
                x_ref[here, :].astype(jnp.float32), gain_ref[...], shift_ref[...]
            )
            back, gain_grad, shift_grad = layer_norm_back(
                total[here, :], plain, inverse, gain_ref[...]
            )
            in_ref[here, :] = (mg_ref[here, :] + back).astype(LOW)
            norm_sums[0:1, :] += gain_grad[None, :]
            norm_sums[1:2, :] += shift_grad[None, :]

        each(4, norm_back)
        late_a.begin(norm_sums[...])
        scatter.drain()
        late_b.begin(late_a.result())
        first = early_b.result()
        last = late_b.result()
        small_ref[...] = first
        small_ref[1:2, :] = first[0:1, :]
        small_ref[3:4, :] = first[1:2, :]
        small_ref[0:1, :] = last[0:1, :]
        small_ref[2:3, :] = last[1:2, :]
        exchange_qkv.wait()
        exchange_out.wait()

    devices = 2 * chips
    heads_kind = pltpu.VMEM((length, in_width), LOW)
    heads_sum = pltpu.VMEM((length, in_width), jnp.float32)
    return line_call(
        kernel,
        "scatter_triple",
        6,
        (
            start, lse, delta, gain, shift, sums,
            *qkv, keys_turned, context_grad, context, *tables, weights, tokens, mid_grad, normed, grads,
        ),
        [
            shape((rows, width)),
            shape((8, width), jnp.float32),
            shape((groups, 3, part, in_width)),
            shape((groups, in_width, part)),
        ],
        [
            *(heads_kind for _ in range(5)),
            *(pltpu.VMEM((length, tile), jnp.float32) for _ in range(2)),
            pltpu.VMEM(weights.shape, LOW),
            pltpu.VMEM((rows, width), LOW),
            pltpu.VMEM((rows, width), jnp.float32),
            pltpu.VMEM((2, length, part), LOW),
            pltpu.SemaphoreType.DMA((11,)),
            pltpu.SemaphoreType.DMA((2,)),
            pltpu.VMEM((in_width, length), LOW),
            pltpu.VMEM((in_width, length), jnp.float32),
            heads_sum,
            heads_sum,
            heads_kind,
            heads_kind,
            heads_kind,
            pltpu.VMEM((8, in_width), jnp.float32),
            pltpu.VMEM((rows, width), jnp.float32),
            pltpu.VMEM((2, width), jnp.float32),
            pltpu.VMEM((groups, 3, part, in_width), LOW),
            pltpu.VMEM((groups, in_width, part), LOW),
            pltpu.VMEM((devices, 2, width), jnp.float32),
            pltpu.VMEM((groups, 8, width), jnp.float32),
            pltpu.VMEM((devices, 2, width), jnp.float32),
            pltpu.VMEM((groups, 2, width), jnp.float32),
        ]
        + Scatter.scratch(chips, rows, width)
        + Spread.scratch(groups) * 2
        + [pltpu.SemaphoreType.DMA((n,)) for n in (devices, devices, groups, groups) * 2],
        COST_FLOPS,
        in_hbm=(2, 3),
        from_hbm=tuple(range(6, 19)),
    )


def adam_update(master, gradient, moment_one, moment_two, correct_one, correct_two, rate):
    one_new = 0.9 * moment_one + 0.1 * gradient
    two_new = 0.999 * moment_two + 0.001 * gradient * gradient
    change = one_new / correct_one / (jnp.sqrt(two_new / correct_two) + 1e-08) + 0.1 * master
    return (master - rate * change, one_new, two_new)


def per_device(
    groups,
    chips,
    inputs,
    out_grad,
    segments,
    w_qkv,
    w_out,
    w_gate_up,
    w_down,
    qkv_bias,
    norm_gain,
    norm_bias,
    first_qkv,
    first_out,
    first_gate_up,
    first_down,
    first_bias,
    first_gain,
    first_shift,
    second_qkv,
    second_out,
    second_gate_up,
    second_down,
    second_bias,
    second_gain,
    second_shift,
):
    head_width = w_qkv.shape[2]
    gains = (norm_gain[0:1], norm_gain[1:2])
    shifts = (norm_bias[0:1], norm_bias[1:2])
    half = jnp.arange(ROT // 2, dtype=jnp.float32)
    rates = 10000.0 ** (-(2.0 * half) / ROT)
    rates = jnp.concatenate([rates, rates, jnp.zeros((HD - ROT,), jnp.float32)])
    rates = jnp.tile(rates, min(head_width, 128) // HD)[None, :]

    gate_up_turned = jnp.swapaxes(w_gate_up, 1, 2)
    normed_one_all, qkv_all, out_all, down_one, *rest = gather_project(
        groups,
        chips,
        inputs,
        gains[0],
        shifts[0],
        (w_qkv, w_out, w_down),
        qkv_bias,
        segments,
        rates,
    )
    qkv, (keys_turned, values_turned, start), tables = rest[:3], rest[3:6], rest[6:]
    middle, context_flat, lse, mlp_grad, pair_all, down_two = scatter_heads(
        groups,
        chips,
        qkv[0],
        qkv[1],
        values_turned,
        start,
        out_all,
        inputs,
        out_grad,
        (gate_up_turned, w_down),
    )
    down_parts = (down_one, down_two)
    normed_two_all, hidden_low, gate_grad, up_grad, normed_two_grad, parts_down = hidden_layers(
        groups, chips, middle, gains[1], shifts[1], pair_all, down_parts, mlp_grad
    )
    attn_grad_all, context_grad, middle_grad, sums_two, outputs, parts_pair, delta = (
        gather_context(
            groups,
            chips,
            middle,
            normed_two_grad,
            out_grad,
            gains[1],
            shifts[1],
            out_all,
            context_flat,
            hidden_low,
            down_parts,
            normed_two_all,
            (gate_grad, up_grad),
        )
    )
    input_grad, small, parts_qkv, parts_out = scatter_triple(
        groups,
        chips,
        qkv,
        keys_turned,
        start,
        lse,
        delta,
        context_flat,
        context_grad,
        tables,
        qkv_all,
        inputs,
        gains[0],
        shifts[0],
        middle_grad,
        sums_two,
        normed_one_all,
        attn_grad_all,
    )

    def add_parts(parts):
        total = parts[0].astype(jnp.float32)
        for offset in range(1, groups):
            total = total + parts[offset].astype(jnp.float32)
        return total

    grad_qkv, grad_out, grad_down = add_parts(parts_qkv), add_parts(parts_out), add_parts(parts_down)
    grad_gate_up = jnp.swapaxes(add_parts(parts_pair), 1, 2)
    grad_bias = small[4:7, :head_width]
    grad_gain, grad_shift = small[0:2], small[2:4]
    correct_one = 1.0 - 0.9**STEP
    correct_two = 1.0 - 0.999**STEP
    rates = (0.02, 0.3, 0.02, 0.02, 0.3, 0.3, 0.3)
    masters = (w_qkv, w_out, w_gate_up, w_down, qkv_bias, norm_gain, norm_bias)
    gradients = (grad_qkv, grad_out, grad_gate_up, grad_down, grad_bias, grad_gain, grad_shift)
    firsts = (first_qkv, first_out, first_gate_up, first_down, first_bias, first_gain, first_shift)
    seconds = (
        second_qkv,
        second_out,
        second_gate_up,
        second_down,
        second_bias,
        second_gain,
        second_shift,
    )
    updated = [
        adam_update(
            masters[number],
            gradients[number],
            firsts[number],
            seconds[number],
            correct_one,
            correct_two,
            rates[number],
        )
        for number in range(7)
    ]
    return (
        outputs,
        input_grad,
        grad_qkv,
        grad_out,
        grad_gate_up,
        grad_down,
        grad_bias,
        grad_gain,
        grad_shift,
        updated[0][0],
        updated[1][0],
        updated[2][0],
        updated[3][0],
        updated[4][0],
        updated[5][0],
        updated[6][0],
        updated[0][1],
        updated[1][1],
        updated[2][1],
        updated[3][1],
        updated[4][1],
        updated[5][1],
        updated[6][1],
        updated[0][2],
        updated[1][2],
        updated[2][2],
        updated[3][2],
        updated[4][2],
        updated[5][2],
        updated[6][2],
    )


def solution(mesh):
    in_specs = (
        P(("dp", "tensor"), None),
        P(("dp", "tensor"), None),
        P("dp", None),
        P(None, "dp", "tensor"),
        P("tensor", "dp"),
        P(None, "dp", "tensor"),
        P("tensor", "dp"),
        P(None, "tensor"),
        P(),
        P(),
        P(None, "dp", "tensor"),
        P("tensor", "dp"),
        P(None, "dp", "tensor"),
        P("tensor", "dp"),
        P(None, "tensor"),
        P(),
        P(),
        P(None, "dp", "tensor"),
        P("tensor", "dp"),
        P(None, "dp", "tensor"),
        P("tensor", "dp"),
        P(None, "tensor"),
        P(),
        P(),
    )
    out_specs = (
        P(("dp", "tensor"), None),
        P(("dp", "tensor"), None),
        P(None, "dp", "tensor"),
        P("tensor", "dp"),
        P(None, "dp", "tensor"),
        P("tensor", "dp"),
        P(None, "tensor"),
        P(),
        P(),
        P(None, "dp", "tensor"),
        P("tensor", "dp"),
        P(None, "dp", "tensor"),
        P("tensor", "dp"),
        P(None, "tensor"),
        P(),
        P(),
        P(None, "dp", "tensor"),
        P("tensor", "dp"),
        P(None, "dp", "tensor"),
        P("tensor", "dp"),
        P(None, "tensor"),
        P(),
        P(),
        P(None, "dp", "tensor"),
        P("tensor", "dp"),
        P(None, "dp", "tensor"),
        P("tensor", "dp"),
        P(None, "tensor"),
        P(),
        P(),
    )
    return jax.shard_map(
        functools.partial(per_device, mesh.shape["dp"], mesh.shape["tensor"] // 2),
        mesh=mesh, in_specs=in_specs, out_specs=out_specs, check_vma=False
    )
```

```python
import functools

import jax
import jax.numpy as jnp
from jax import lax
from jax.experimental import pallas as pl
from jax.experimental.pallas import tpu as pltpu
from jax.sharding import PartitionSpec as P

HD = 64
ROT = 16
STEP = 10


def layer_norm_parts(values, gain_row, shift_row):
    average = jnp.mean(values, axis=-1, keepdims=True)
    centred = values - average
    inverse = lax.rsqrt(jnp.mean(centred * centred, axis=-1, keepdims=True) + 1e-05)
    normed = centred * inverse
    return (normed * gain_row + shift_row, normed, inverse)


def layer_norm_back(incoming, normed, inverse, gain_row):
    scaled = incoming * gain_row
    inner = (
        scaled
        - jnp.mean(scaled, axis=-1, keepdims=True)
        - normed * jnp.mean(scaled * normed, axis=-1, keepdims=True)
    )
    return (inner * inverse, jnp.sum(incoming * normed, axis=0), jnp.sum(incoming, axis=0))


NEG = -1e30
BLK = 256
NT = (((1,), (1,)), ((), ()))
NN = (((1,), (0,)), ((), ()))


def dot(left, right, dims=NN, precision=None):
    return lax.dot_general(
        left, right, dims, preferred_element_type=jnp.float32, precision=precision
    )


def head_masks(width, dtype):
    lane = lax.broadcasted_iota(jnp.int32, (1, width), 1)
    return [(lane // HD == h).astype(dtype) for h in range(width // HD)]


def rope_tile(tile, cosine, sine, sign):
    width = tile.shape[-1]
    lane = lax.rem(lax.broadcasted_iota(jnp.int32, tile.shape, 1), HD)
    ahead = pltpu.roll(tile, width - ROT // 2, 1)
    behind = pltpu.roll(tile, ROT // 2, 1)
    return tile * cosine + sign * (jnp.where(lane < ROT // 2, ahead, behind) * sine)


def attend(number, size, k_ref, v_turned, masked, starts, query_ids, acc, stats):
    base = pl.multiple_of(number * 2 * size, 2 * size)
    keys = k_ref[pl.ds(base, 2 * size), :]
    key_ids = base + lax.broadcasted_iota(jnp.int32, (2 * size, size), 0)
    visible = (key_ids >= starts) & (key_ids <= query_ids)
    for h, queries in enumerate(masked):
        scores = jnp.where(visible, dot(keys, queries, NT), NEG)
        peak_old = stats[h : h + 1, :]
        peak = jnp.maximum(peak_old, jnp.max(scores, axis=0, keepdims=True))
        fade = jnp.exp(peak_old - peak)
        prob = jnp.exp(scores - peak)
        stats[h : h + 1, :] = peak
        stats[8 + h : 9 + h, :] = stats[8 + h : 9 + h, :] * fade + jnp.sum(
            prob, axis=0, keepdims=True
        )
        band = slice(h * HD, (h + 1) * HD)
        acc[band, :] = acc[band, :] * fade + dot(
            v_turned[band, pl.ds(base, 2 * size)], prob.astype(jnp.bfloat16)
        )


MESH = pl.DeviceIdType.MESH
VMEM_BYTES = (127 << 20) // 2
LONGEST = 1024
DOCUMENTS = 4
TN = (((0,), (0,)), ((), ()))
LOW = jnp.bfloat16


def remote(source, target, send, receive, device):
    return pltpu.make_async_remote_copy(
        src_ref=source,
        dst_ref=target,
        send_sem=send,
        recv_sem=receive,
        device_id=device,
        device_id_type=MESH,
    )


class Place:
    def __init__(self, groups, chips):
        self.groups, self.chips = groups, chips
        self.group = lax.axis_index("dp")
        self.spot = lax.axis_index("tensor")
        self.chip, self.core = self.spot // 2, self.spot % 2

    def at(self, chip, core):
        return (self.group, chip * 2 + core)

    def peer(self, offset):
        return (lax.rem(self.group + offset, self.groups), self.spot)

    def fellow(self, offset):
        return (self.group, lax.rem(self.spot + offset, 2 * self.chips))

    def greet(self, with_groups=False, with_all_spots=False):
        semaphore = pltpu.get_barrier_semaphore()

        def greet(target):
            pl.semaphore_signal(semaphore, inc=1, device_id=target, device_id_type=MESH)

        if with_all_spots:
            for offset in range(1, 2 * self.chips):
                greet(self.fellow(offset))
            count = 2 * self.chips - 1
        else:
            greet(self.at(self.chip, 1 - self.core))
            pl.when(self.chip > 0)(lambda: greet(self.at(self.chip - 1, self.core)))
            pl.when(self.chip < self.chips - 1)(lambda: greet(self.at(self.chip + 1, self.core)))
            count = 1 + jnp.where(self.chip > 0, 1, 0) + jnp.where(self.chip < self.chips - 1, 1, 0)
        if with_groups:
            for offset in range(1, self.groups):
                greet(self.peer(offset))
            count = count + self.groups - 1
        self.awaited = count

    def meet(self):
        pl.semaphore_wait(pltpu.get_barrier_semaphore(), self.awaited)


def each(count, use):
    def one(index, _):
        use(index)
        return 0

    lax.fori_loop(0, count, one, 0)


def block_of(ref, index, size):
    return ref.at[pl.ds(pl.multiple_of(index * size, size), size)]


def fetch_all(pairs, sems):
    copies = [pltpu.make_async_copy(a, b, sems.at[n]) for n, (a, b) in enumerate(pairs)]
    for copy in copies:
        copy.start()
    return copies


HALVES = 2


class Gather:
    SEMS = 5

    def __init__(self, place, full, sems, kept=None, keep_sem=None):
        self.place, self.full, self.kept, self.keep_sem = place, full, kept, keep_sem
        self.line_in, self.core_in, self.right_out, self.left_out, self.core_out = sems
        self.rows = full.shape[0] // (2 * place.chips)

    @classmethod
    def scratch(cls, chips):
        return [pltpu.SemaphoreType.DMA((chips * HALVES,)) for _ in range(cls.SEMS)]

    def own(self):
        return block_of(self.full, self.place.spot, self.rows)

    def block(self, chip, core, half):
        return block_of(self.full, (chip * 2 + core) * HALVES + half, self.rows // HALVES)

    def right(self, which, half):
        place, part = self.place, self.block(which, self.place.core, half)
        target = place.at(jnp.minimum(place.chip + 1, place.chips - 1), place.core)
        index = which * HALVES + half
        return remote(part, part, self.right_out.at[index], self.line_in.at[index], target)

    def left(self, which, half):
        place, part = self.place, self.block(which, self.place.core, half)
        target = place.at(jnp.maximum(place.chip - 1, 0), place.core)
        index = which * HALVES + half
        return remote(part, part, self.left_out.at[index], self.line_in.at[index], target)

    def across(self, which, core, half):
        place, part = self.place, self.block(which, core, half)
        target = place.at(place.chip, 1 - place.core)
        index = which * HALVES + half
        return remote(part, part, self.core_out.at[index], self.core_in.at[index], target)

    def begin(self, halves=range(HALVES)):
        chip, chips = self.place.chip, self.place.chips
        for half in halves:
            pl.when(chip < chips - 1)(lambda: self.right(chip, half).start())
            pl.when(chip > 0)(lambda: self.left(chip, half).start())
        for half in halves:
            self.across(chip, self.place.core, half).start()

    def pass_on(self, step, halves=range(HALVES)):
        chip, chips, core = self.place.chip, self.place.chips, self.place.core
        low, high = chip - 1 - step, chip + 1 + step
        for half in halves:

            @pl.when(low >= 0)
            def _():
                self.right(low, half).wait_recv()
                pl.when(chip < chips - 1)(lambda: self.right(low, half).start())
                self.across(low, core, half).start()

            @pl.when(high < chips)
            def _():
                self.left(high, half).wait_recv()
                pl.when(chip > 0)(lambda: self.left(high, half).start())
                self.across(high, core, half).start()

    def keep(self, which):
        part = block_of(self.full, which, 2 * self.rows)
        return pltpu.make_async_copy(
            part, block_of(self.kept, which, 2 * self.rows), self.keep_sem.at[which]
        )

    def wait_chip(self, which, halves=range(HALVES)):
        for half in halves:
            self.across(which, 1 - self.place.core, half).wait_recv()
        if self.kept is not None and HALVES - 1 in halves:
            self.keep(which).start()

    def each_new(self, step, use, halves=range(HALVES)):
        low, high = self.place.chip - 1 - step, self.place.chip + 1 + step

        @pl.when(low >= 0)
        def _():
            self.wait_chip(low, halves)
            use(low)

        @pl.when(high < self.place.chips)
        def _():
            self.wait_chip(high, halves)
            use(high)

    def drain(self):
        chip, chips, core = self.place.chip, self.place.chips, self.place.core

        def one(which):
            for half in range(HALVES):
                self.across(which, core, half).wait_send()
                pl.when((which <= chip) & (chip < chips - 1))(
                    lambda: self.right(which, half).wait_send()
                )
                pl.when((which >= chip) & (chip > 0))(lambda: self.left(which, half).wait_send())
            if self.kept is not None:
                self.keep(which).wait()

        each(chips, one)


class Scatter:
    def __init__(self, place, work, scratch, halves=HALVES):
        self.place, self.work, self.halves = place, work, halves
        self.out, self.side, self.line = scratch[:3]
        self.core_out, self.core_in, self.line_out, self.line_in = scratch[3:]
        self.part = self.out.shape[1] // halves
        chip, chips = place.chip, place.chips
        self.near = jnp.minimum(chip, chips - 1 - chip)
        self.alone = chips - 1 - 2 * self.near
        self.flip = jnp.where(chip * 2 < chips, 0, 1)
        self.lag = jnp.where(self.near > 0, 1, 0)

    @staticmethod
    def scratch(chips, rows, width):
        return [
            pltpu.VMEM((chips, rows, width), LOW),
            pltpu.VMEM((chips, rows, width), LOW),
            pltpu.VMEM((chips + 1, rows, width), LOW),
            pltpu.SemaphoreType.DMA((chips,)),
            pltpu.SemaphoreType.DMA((chips,)),
            pltpu.SemaphoreType.DMA((chips * HALVES,)),
            pltpu.SemaphoreType.DMA(((chips + 1) * HALVES,)),
        ]

    SCRATCH = 7

    def order(self, turn):
        chips = self.place.chips
        later = jnp.maximum(turn - self.alone, 0)
        pair = later // 2
        far = jnp.where(turn < self.alone, chips - 1 - turn, chips - 1 - self.alone - pair)
        which = jnp.where((turn >= self.alone) & (later % 2 == 1), pair, far)
        which = jnp.where(turn == chips - 1, self.near, which)
        return jnp.where(self.flip == 1, chips - 1 - which, which)

    def across(self, which):
        place = self.place
        return remote(
            self.out.at[which],
            self.side.at[which],
            self.core_out.at[which],
            self.core_in.at[which],
            place.at(place.chip, 1 - place.core),
        )

    def hop(self, which, slot, half, target):
        rows = slice(half * self.part, (half + 1) * self.part)
        return remote(
            self.out.at[which, rows],
            self.line.at[slot, rows],
            self.line_out.at[which * self.halves + half],
            self.line_in.at[slot * self.halves + half],
            self.place.at(target, self.place.core),
        )

    def right(self, which, half):
        place = self.place
        slot = jnp.where(which == place.chip + 1, place.chips, which)
        return self.hop(which, slot, half, jnp.minimum(place.chip + 1, place.chips - 1))

    def left(self, which, half):
        return self.hop(which, which, half, jnp.maximum(self.place.chip - 1, 0))

    def arrived(self, slot, half):
        place = self.place
        rows = slice(half * self.part, (half + 1) * self.part)
        part = self.line.at[slot, rows]
        other = place.at(place.chip, 1 - place.core)
        remote(
            part, part, self.line_out.at[0], self.line_in.at[slot * self.halves + half], other
        ).wait_recv()
        return self.line[slot, rows].astype(jnp.float32)

    def produce(self, turn):
        which = self.order(turn)
        self.out[which] = self.work(which, 1 - self.place.core).astype(LOW)
        self.across(which).start()

    def chip_sum(self, which):
        mine = self.work(which, self.place.core)
        self.across(which).wait()
        return mine + self.side[which].astype(jnp.float32)

    def send(self, which, upstream, copy):
        total = self.chip_sum(which)

        @pl.when(upstream)
        def _():
            for half in range(self.halves):
                rows = slice(half * self.part, (half + 1) * self.part)
                self.out[which, rows] = (total[rows] + self.arrived(which, half)).astype(LOW)
                copy(which, half).start()

        @pl.when(jnp.logical_not(upstream))
        def _():
            for half in range(self.halves):
                rows = slice(half * self.part, (half + 1) * self.part)
                self.out[which, rows] = total[rows].astype(LOW)
                copy(which, half).start()

    def first(self):
        pl.when(self.lag == 1)(lambda: self.produce(0))

    def slot(self, number, before_last=None):
        chip, chips = self.place.chip, self.place.chips
        if before_last is None:
            self.produce(number + self.lag)
        else:
            pl.when(self.lag == 0)(lambda: self.produce(number))
            pl.when((self.lag == 1) & (number == chips - 2))(before_last)
        right = chips - 1 - (number - chip)
        left = number - (chips - 1 - chip)
        pl.when((number >= chip) & (right > chip))(
            lambda: self.send(right, chip > 0, self.right)
        )
        pl.when((left >= 0) & (left < chip))(
            lambda: self.send(left, chip < chips - 1, self.left)
        )
        if before_last is not None:
            count = jnp.where(number < chips - 3, 1, jnp.where(number == chips - 3, 2, 0))
            pl.when(self.lag == 1)(
                lambda: each(count, lambda index: self.produce(number + 1 + index))
            )

    def last(self):
        pl.when(self.lag == 0)(lambda: self.produce(self.place.chips - 1))

    def own(self, total):
        chip, chips = self.place.chip, self.place.chips
        total[...] = self.chip_sum(chip)
        for half in range(self.halves):
            rows = slice(half * self.part, (half + 1) * self.part)

            @pl.when(chip > 0)
            def _():
                total[rows] += self.arrived(chips, half)

            @pl.when(chip < chips - 1)
            def _():
                total[rows] += self.arrived(chip, half)

    def drain(self):
        chip = self.place.chip

        def one(which):
            for half in range(self.halves):
                pl.when(which > chip)(lambda: self.right(which, half).wait_send())
                pl.when(which < chip)(lambda: self.left(which, half).wait_send())

        each(self.place.chips, one)


class StoredScatter(Scatter):
    def __init__(self, place, scratch, mine):
        super().__init__(place, None, scratch, 1)
        self.mine = mine

    def put(self, which, other, own):
        self.out[which] = other.astype(LOW)
        self.across(which).start()
        self.mine[which] = own.astype(LOW)

    def produce(self, turn):
        pass

    def chip_sum(self, which):
        self.across(which).wait()
        return self.mine[which].astype(jnp.float32) + self.side[which].astype(jnp.float32)


class Spread:
    def __init__(self, place, shard, staged, whole, axis, sems):
        self.place, self.staged, self.whole, self.sems = place, staged, whole, sems
        size = shard.shape[axis]
        here = pl.ds(pl.multiple_of(place.group * size, size), size)
        self.mine = whole.at[tuple(here if a == axis else slice(None) for a in range(len(shard.shape)))]
        staged[...] = shard[...].astype(LOW)

    @staticmethod
    def scratch(groups):
        return [pltpu.SemaphoreType.DMA((groups,)), pltpu.SemaphoreType.DMA((groups,))]

    def copy(self, offset):
        return remote(
            self.staged,
            self.mine,
            self.sems[0].at[offset],
            self.sems[1].at[offset],
            self.place.peer(offset),
        )

    def stay(self):
        return pltpu.make_async_copy(self.staged, self.mine, self.sems[0].at[0])

    def start(self):
        for offset in range(1, self.place.groups):
            self.copy(offset).start()
        self.stay().start()

    def wait(self):
        for offset in range(1, self.place.groups):
            self.copy(offset).wait()
        self.stay().wait()


class Exchange:
    def __init__(self, place, staged, landed, sems):
        self.place, self.staged, self.landed = place, staged, landed
        self.send, self.receive = sems

    def copy(self, offset):
        return remote(
            self.staged.at[offset],
            self.landed.at[offset],
            self.send.at[offset],
            self.receive.at[offset],
            self.place.peer(offset),
        )

    def stay(self):
        return pltpu.make_async_copy(self.staged.at[0], self.landed.at[0], self.send.at[0])

    def wait(self):
        def one(offset, _):
            self.copy(offset).wait()
            return 0

        lax.fori_loop(1, self.place.groups, one, 0)
        self.stay().wait()


class SmallSum:
    def __init__(self, slots, me, count, target, sems):
        self.slots, self.me, self.count, self.target = slots, me, count, target
        self.send, self.receive = sems

    def copy(self, offset):
        part = self.slots.at[self.me]
        return remote(
            part, part, self.send.at[offset], self.receive.at[self.me], self.target(offset)
        )

    def begin(self, rows):
        self.slots[self.me] = rows
        for offset in range(1, self.count):
            self.copy(offset).start()

    def result(self):
        for offset in range(1, self.count):
            source = lax.rem(self.me + offset, self.count)
            part = self.slots.at[source]
            remote(
                part, part, self.send.at[offset], self.receive.at[source], self.target(offset)
            ).wait_recv()
        total = self.slots[0]
        for index in range(1, self.count):
            total = total + self.slots[index]
        for offset in range(1, self.count):
            self.copy(offset).wait_send()
        return total


def pieces(number, groups, fill):
    @pl.when(number == 0)
    def _():
        each(groups - 1, lambda index: fill(index + 1))


def line_call(kernel, name, number, operands, out_shape, scratch, flops, in_hbm=(), from_hbm=()):
    whole, hbm = pl.BlockSpec(memory_space=pltpu.VMEM), pl.BlockSpec(memory_space=pl.ANY)
    ins = [hbm if n in from_hbm else whole for n in range(len(operands))]
    outs = [hbm if n in in_hbm else whole for n in range(len(out_shape))]
    return pl.pallas_call(
        kernel,
        out_shape=out_shape,
        in_specs=ins,
        out_specs=outs,
        scratch_shapes=scratch,
        compiler_params=pltpu.CompilerParams(
            collective_id=number, has_side_effects=True, vmem_limit_bytes=VMEM_BYTES
        ),
        cost_estimate=pl.CostEstimate(flops=flops, bytes_accessed=0, transcendentals=0),
        name=name,
    )(*operands)


COST_FLOPS = 80_000_000_000


def shape(dims, kind=LOW):
    return jax.ShapeDtypeStruct(dims, kind)


def split_refs(refs, *counts):
    parts, at = [], 0
    for count in counts:
        parts.append(refs[at : at + count])
        at += count
    return parts


def gather_project(groups, chips, tokens, gain, shift, shards, bias, segments, rates):
    rows, width = tokens.shape
    length = rows * 2 * chips
    qkv_shard, out_shard, down_shard = shards
    part, out_width = qkv_shard.shape[1:]
    upper = down_shard.shape[0] // 2
    tile = rates.shape[1]

    def kernel(
        x_ref, gain_ref, shift_ref, qkv_ref, out_ref, down_ref, bias_ref, segment_ref, rate_ref,
        kept, weights_kept, out_whole, down_whole, q_ref, k_ref, v_ref,
        k_turned, v_turned, start_ref, cos_ref, sin_ref,
        full, weights, qkv_staged, out_staged, down_staged, load, keep_sem, *sems
    ):
        place = Place(groups, chips)
        place.greet(True)
        line, one, two, three = split_refs(sems, Gather.SEMS, 2, 2, 2)
        gather = Gather(place, full, line, kept, keep_sem)
        size = rows // HALVES
        for half in range(HALVES):
            normed, _, _ = layer_norm_parts(
                x_ref[half * size : (half + 1) * size, :].astype(jnp.float32),
                gain_ref[...],
                shift_ref[...],
            )
            gather.block(place.chip, place.core, half)[...] = normed.astype(LOW)
            if half == 0:
                place.meet()
            gather.begin((half,))
        spread_qkv = Spread(place, qkv_ref, qkv_staged, weights, 1, one)
        spread_qkv.start()
        spread_out = Spread(place, out_ref, out_staged, out_whole, 1, two)
        spread_out.start()
        spread_down = Spread(place, down_ref.at[0:upper], down_staged, down_whole, 1, three)
        spread_down.start()

        def work(chip):
            base = pl.multiple_of(chip * 2 * rows, 2 * rows)
            here = pl.ds(base, 2 * rows)
            values = full[here, :]
            for number, ref in enumerate((q_ref, k_ref, v_ref)):
                result = dot(values, weights[number]) + bias_ref[number : number + 1, :]
                if number < 2:
                    parts = [
                        rope_tile(
                            result[:, t * tile : (t + 1) * tile],
                            cos_ref[here, :],
                            sin_ref[here, :],
                            1.0,
                        )
                        for t in range(out_width // tile)
                    ]
                    result = jnp.concatenate(parts, axis=1) if len(parts) > 1 else parts[0]
                result = result.astype(LOW)
                ref[here, :] = result
                if number > 0:
                    (k_turned, v_turned)[number - 1][:, here] = result.T

        segment = segment_ref[...]
        start = jnp.zeros_like(segment)
        for number in range(1, DOCUMENTS):
            before = jnp.sum(jnp.where(segment < number, 1, 0), axis=1, keepdims=True)
            start = jnp.where(segment == number, before, start)
        start_ref[...] = start
        lane = lax.rem(lax.broadcasted_iota(jnp.int32, (1, tile), 1), HD)
        for block in range(length // BLK):
            here = slice(block * BLK, (block + 1) * BLK)
            ids = block * BLK + lax.broadcasted_iota(jnp.int32, (1, BLK), 1)
            spot = (ids - start[:, here]).astype(jnp.float32)
            angle = jnp.broadcast_to(spot, (tile, BLK)).T * rate_ref[...]
            sine = jnp.sin(angle)
            cos_ref[here, :] = jnp.where(lane < ROT, jnp.cos(angle), 1.0)
            sin_ref[here, :] = jnp.where(
                lane < ROT // 2, -sine, jnp.where(lane < ROT, sine, 0.0)
            )
        gather.pass_on(0)
        spread_qkv.wait()
        weights_keep = pltpu.make_async_copy(weights, weights_kept, load.at[0])
        weights_keep.start()
        gather.wait_chip(place.chip)
        work(place.chip)

        def step(number):
            pl.when(number > 0)(lambda: gather.pass_on(number))
            gather.each_new(number, work)

        each(chips - 1, step)
        weights_keep.wait()
        spread_out.wait()
        spread_down.wait()
        gather.drain()

    head_shape = shape((length, out_width))
    return line_call(
        kernel,
        "gather_project",
        1,
        (tokens, gain, shift, *shards, bias, segments, rates),
        [
            shape((length, width)),
            shape((3, width, out_width)),
            shape((out_width, width)),
            shape((upper, width)),
            head_shape,
            head_shape,
            head_shape,
            shape((out_width, length)),
            shape((out_width, length)),
            shape((1, length), jnp.int32),
            *(shape((length, tile), jnp.float32) for _ in range(2)),
        ],
        [
            pltpu.VMEM((length, width), LOW),
            pltpu.VMEM((3, width, out_width), LOW),
            pltpu.VMEM(qkv_shard.shape, LOW),
            pltpu.VMEM(out_shard.shape, LOW),
            pltpu.VMEM((upper, down_shard.shape[1]), LOW),
            pltpu.SemaphoreType.DMA((1,)),
            pltpu.SemaphoreType.DMA((chips,)),
        ]
        + Gather.scratch(chips)
        + Spread.scratch(groups) * 3,
        COST_FLOPS,
        in_hbm=(0, 1, 2, 3),
    )


def scatter_heads(groups, chips, queries, keys, values_turned, start, weight, tokens, grads, shards):
    rows, width = tokens.shape
    length, head_width = queries.shape
    heads = head_width // HD
    pair_shard, down_shard = shards
    upper = down_shard.shape[0] // 2

    def kernel(
        q_hbm, k_hbm, v_hbm, w_hbm, x_hbm, og_hbm, start_ref, pair_ref, down_ref,
        mid_ref, ctx_ref, lse_ref, kept, pair_whole, down_whole,
        full, q_ref, k_ref, w_ref, x_ref, pair_staged, down_staged,
        load, keep_sem, v_turned, acc, stats, *rest
    ):
        place = Place(groups, chips)
        place.greet(True)
        scratch, line, one, two = split_refs(rest, Scatter.SCRATCH, Gather.SEMS, 2, 2)
        gather = Gather(place, full, line, kept, keep_sem)
        fetches = fetch_all(
            [
                (og_hbm, gather.own()),
                (k_hbm, k_ref),
                (v_hbm, v_turned),
                (q_hbm, q_ref),
                (w_hbm, w_ref),
                (x_hbm, x_ref),
            ],
            load,
        )
        fetches[0].wait()
        place.meet()
        gather.begin()
        spread_pair = Spread(place, pair_ref, pair_staged, pair_whole, 2, one)
        spread_pair.start()
        spread_down = Spread(place, down_ref.at[upper:], down_staged, down_whole, 1, two)
        spread_down.start()
        for copy in fetches[1:5]:
            copy.wait()
        masks = head_masks(head_width, LOW)

        def work(chip, core):
            block = chip * 2 + core
            base = pl.multiple_of(block * rows, rows)
            here = pl.ds(base, rows)
            values = (q_ref[here, :] * 0.125).astype(LOW)
            masked = [values * m for m in masks]
            starts = start_ref[:, here]
            query_ids = base + lax.broadcasted_iota(jnp.int32, (1, rows), 1)
            acc[...] = jnp.zeros_like(acc)
            stats[0:8, :] = jnp.full((8, rows), NEG, jnp.float32)
            stats[8:16, :] = jnp.zeros((8, rows), jnp.float32)

            def step(number, _):
                attend(number, rows, k_ref, v_turned, masked, starts, query_ids, acc, stats)
                return 0

            first = jnp.maximum(block - LONGEST // rows, 0) // 2
            lax.fori_loop(first, block // 2 + 1, step, 0)
            for h in range(heads):
                band = slice(h * HD, (h + 1) * HD)
                acc[band, :] = acc[band, :] / stats[8 + h : 9 + h, :]
            context = acc[...].T.astype(LOW)
            ctx_ref[here, :] = context
            total = jnp.where(stats[8:16, :] > 0, stats[8:16, :], 1.0)
            lse_ref[:, here] = stats[0:8, :] + jnp.log(total)
            return dot(context, w_ref[...])

        scatter = Scatter(place, work, scratch)
        scatter.first()

        def seen(chip):
            pass

        def step(number):
            scatter.slot(number)
            gather.pass_on(number)
            pl.when(number > 0)(lambda: gather.each_new(number - 1, seen))

        each(chips - 1, step)
        scatter.last()
        fetches[5].wait()
        gather.wait_chip(place.chip)
        gather.each_new(chips - 2, seen)
        scatter.own(mid_ref)
        mid_ref[...] += x_ref[...].astype(jnp.float32)
        gather.drain()
        scatter.drain()
        spread_pair.wait()
        spread_down.wait()

    return line_call(
        kernel,
        "scatter_heads",
        2,
        (queries, keys, values_turned, weight, tokens, grads, start, *shards),
        [
            shape((rows, width), jnp.float32),
            shape((length, head_width)),
            shape((8, length), jnp.float32),
            shape((length, width)),
            shape((2, pair_shard.shape[1], width)),
            shape((down_shard.shape[0] - upper, width)),
        ],
        [
            pltpu.VMEM((length, width), LOW),
            *(pltpu.VMEM((length, head_width), LOW) for _ in range(2)),
            pltpu.VMEM((head_width, width), LOW),
            pltpu.VMEM((rows, width), LOW),
            pltpu.VMEM(pair_shard.shape, LOW),
            pltpu.VMEM((down_shard.shape[0] - upper, down_shard.shape[1]), LOW),
            pltpu.SemaphoreType.DMA((6,)),
            pltpu.SemaphoreType.DMA((chips,)),
            pltpu.VMEM((head_width, length), LOW),
            pltpu.VMEM((head_width, rows), jnp.float32),
            pltpu.VMEM((16, rows), jnp.float32),
        ]
        + Scatter.scratch(chips, rows, width)
        + Gather.scratch(chips)
        + Spread.scratch(groups) * 2,
        COST_FLOPS,
        in_hbm=(3, 4, 5),
        from_hbm=(0, 1, 2, 3, 4, 5),
    )


def hidden_layers(groups, chips, middle, gain, shift, pair_weight, down_parts, grads):
    rows, width = middle.shape
    length = rows * 2 * chips
    hidden = pair_weight.shape[1]
    upper = down_parts[0].shape[0]
    part = width // groups
    size = rows // HALVES

    def kernel(
        gain_ref, shift_ref, mid_hbm, pair_hbm, down_one, down_two, og_hbm,
        kept, hid_kept, gg_kept, ug_kept, sum_ref, landed,
        full, og_ref, pair_ref, down_ref, hid_ref, held, staged, mine, load, keep_sem, store_sem, *rest
    ):
        place = Place(groups, chips)
        place.greet(True)
        first, second, line, sems = split_refs(rest, Scatter.SCRATCH, Scatter.SCRATCH, Gather.SEMS, 2)
        fetches = fetch_all(
            [
                (mid_hbm, sum_ref),
                (pair_hbm, pair_ref),
                (down_one, down_ref.at[0:upper]),
                (down_two, down_ref.at[upper:hidden]),
                (og_hbm, og_ref),
            ],
            load,
        )
        gather = Gather(place, full, line, kept, keep_sem)
        scatters = [
            StoredScatter(place, scratch, mine.at[half])
            for half, scratch in enumerate((first, second))
        ]
        exchange = Exchange(place, staged, landed, sems)
        fetches[0].wait()
        at_end = (place.chip == 0) | (place.chip == chips - 1)
        for half in range(HALVES):
            normed, _, _ = layer_norm_parts(
                sum_ref[half * size : (half + 1) * size, :], gain_ref[...], shift_ref[...]
            )
            gather.block(place.chip, place.core, half)[...] = normed.astype(LOW)
            if half == 0:
                place.meet()
                gather.begin((0,))
        pl.when(at_end)(lambda: gather.begin((1,)))
        for copy in fetches[1:]:
            copy.wait()

        def work(chip, half):
            pieces_of = [
                pl.ds(pl.multiple_of((chip * 2 + core) * rows + half * size, size), size)
                for core in range(2)
            ]
            values = jnp.concatenate([full[here, :] for here in pieces_of], axis=0)
            gate = dot(values, pair_ref[0], NT)
            up = dot(values, pair_ref[1], NT)
            sigmoid = 1.0 / (1.0 + jnp.exp(-gate))
            activated = gate * sigmoid
            hidden_low = (activated * up).astype(LOW)
            hidden_grad = dot(
                jnp.concatenate([og_ref[here, :] for here in pieces_of], axis=0), down_ref[...], NT
            )
            slope = sigmoid * (1.0 + gate * (1.0 - sigmoid))
            gate_grad = (hidden_grad * (up * slope)).astype(LOW)
            up_grad = (hidden_grad * activated).astype(LOW)
            held[0] = gate_grad
            held[1] = up_grad
            copies = []
            for core, here in enumerate(pieces_of):
                hid_ref[here, :] = hidden_low[core * size : (core + 1) * size]
                from_held = pl.ds(core * size, size)
                copies += [
                    pltpu.make_async_copy(hid_ref.at[here], hid_kept.at[here], store_sem.at[core]),
                    pltpu.make_async_copy(
                        held.at[0, from_held], gg_kept.at[here], store_sem.at[2 + core]
                    ),
                    pltpu.make_async_copy(
                        held.at[1, from_held], ug_kept.at[here], store_sem.at[4 + core]
                    ),
                ]
            for copy in copies:
                copy.start()
            term = dot(gate_grad, pair_ref[0]) + dot(up_grad, pair_ref[1])
            low, high = term[0:size], term[size : 2 * size]
            scatters[half].put(
                chip,
                jnp.where(place.core == 0, high, low),
                jnp.where(place.core == 0, low, high),
            )
            for copy in copies:
                copy.wait()

        def fill(offset):
            block = lax.rem(place.group + offset, groups)
            columns = pl.ds(pl.multiple_of(block * part, part), part)
            staged[offset] = dot(hid_ref[...], og_ref[:, columns], TN).astype(LOW)

        def fill_send(offset):
            fill(offset)
            exchange.copy(offset).start()

        gather.wait_chip(place.chip, (0,))
        work(place.chip, 0)

        def gather_first(step):
            gather.pass_on(step, (0,))
            gather.each_new(step, lambda chip: work(chip, 0), (0,))

        each(chips - 1, gather_first)
        pl.when(jnp.logical_not(at_end))(lambda: gather.begin((1,)))

        def both(step):
            scatters[0].slot(step)

            @pl.when(step == 0)
            def _():
                gather.wait_chip(place.chip, (1,))
                work(place.chip, 1)

            gather.pass_on(step, (1,))
            gather.each_new(step, lambda chip: work(chip, 1), (1,))

        each(chips - 1, both)

        def scatter_second(step):
            scatters[1].slot(step)
            pieces(step, groups, fill_send)
            pl.when(step == 0)(lambda: scatters[0].own(sum_ref.at[0:size]))

        each(chips - 1, scatter_second)
        fill(0)
        exchange.stay().start()
        scatters[1].own(sum_ref.at[size:rows])
        gather.drain()
        scatters[0].drain()
        scatters[1].drain()
        exchange.wait()

    hidden_shape = shape((length, hidden))
    return line_call(
        kernel,
        "gather_hidden",
        3,
        (gain, shift, middle, pair_weight, *down_parts, grads),
        [
            shape((length, width)),
            hidden_shape,
            hidden_shape,
            hidden_shape,
            shape((rows, width), jnp.float32),
            shape((groups, hidden, part)),
        ],
        [
            pltpu.VMEM((length, width), LOW),
            pltpu.VMEM((length, width), LOW),
            pltpu.VMEM(pair_weight.shape, LOW),
            pltpu.VMEM((hidden, width), LOW),
            pltpu.VMEM((length, hidden), LOW),
            pltpu.VMEM((2, rows, hidden), LOW),
            pltpu.VMEM((groups, hidden, part), LOW),
            pltpu.VMEM((HALVES, chips, size, width), LOW),
            pltpu.SemaphoreType.DMA((5,)),
            pltpu.SemaphoreType.DMA((chips,)),
            pltpu.SemaphoreType.DMA((6,)),
        ]
        + Scatter.scratch(chips, size, width) * 2
        + Gather.scratch(chips)
        + Spread.scratch(groups),
        COST_FLOPS,
        in_hbm=(0, 1, 2, 3, 5),
        from_hbm=(2, 3, 4, 5, 6),
    )


def gather_context(
    groups, chips, middle, normed_grad, out_grad, gain, shift, weight, context, hidden_low, down_parts,
    normed, pair
):
    rows, width = middle.shape
    length = rows * 2 * chips
    out_width = weight.shape[0]
    hidden = hidden_low.shape[1]
    upper = down_parts[0].shape[0]
    part = width // groups

    def kernel(
        mid_ref, ng_hbm, og_ref, gain_ref, shift_ref, w_hbm, ctx_hbm, hid_hbm, down_one, down_two,
        a_ref, gg_hbm, ug_hbm,
        kept, cg_ref, mg_ref, sums_ref, out_ref, landed, delta_ref,
        full, total, w_ref, ctx_ref, hid_ref, down_ref, gg_ref, ug_ref, staged, columns_in, load, keep_sem, *rest
    ):
        place = Place(groups, chips)
        place.greet(True)
        scratch, line, sems = split_refs(rest, Scatter.SCRATCH, Gather.SEMS, 2)

        def fetch(offset):
            block = lax.rem(place.group + offset, groups)
            columns = pl.ds(pl.multiple_of(block * part, part), part)
            slot = lax.rem(offset, 2)
            return pltpu.make_async_copy(a_ref.at[:, columns], columns_in.at[slot], load.at[slot])

        arrive = pltpu.make_async_copy(ng_hbm, total, load.at[3])
        arrive.start()
        late = [
            pltpu.make_async_copy(a, b, load.at[4 + n])
            for n, (a, b) in enumerate(
                (
                    (down_one, down_ref.at[0:upper]),
                    (down_two, down_ref.at[upper:hidden]),
                    (hid_hbm, hid_ref),
                    (w_hbm, w_ref),
                    (ctx_hbm, ctx_ref),
                    (gg_hbm, gg_ref),
                    (ug_hbm, ug_ref),
                )
            )
        ]
        for copy in late:
            copy.start()
        fetch(1).start()
        gather = Gather(place, full, line, kept, keep_sem)
        arrive.wait()
        size = rows // HALVES
        for half in range(HALVES):
            here = slice(half * size, (half + 1) * size)
            _, plain, inverse = layer_norm_parts(mid_ref[here, :], gain_ref[...], shift_ref[...])
            back, gain_grad, shift_grad = layer_norm_back(
                total[here, :], plain, inverse, gain_ref[...]
            )
            mid_grad = og_ref[here, :].astype(jnp.float32) + back
            total[here, :] = mid_grad
            gather.block(place.chip, place.core, half)[...] = mid_grad.astype(LOW)
            if half == 0:
                place.meet()
                sums_ref[0:1, :] = gain_grad[None, :]
                sums_ref[1:2, :] = shift_grad[None, :]
            else:
                sums_ref[0:1, :] += gain_grad[None, :]
                sums_ref[1:2, :] += shift_grad[None, :]
            gather.begin((half,))
        keep = pltpu.make_async_copy(total, mg_ref, load.at[2])
        keep.start()

        select = (
            lax.broadcasted_iota(jnp.int32, (8, out_width), 1) // HD
            == lax.broadcasted_iota(jnp.int32, (8, out_width), 0)
        ).astype(LOW)

        def back_work(chip):
            here = pl.ds(pl.multiple_of(chip * 2 * rows, 2 * rows), 2 * rows)
            context_grad = dot(full[here, :], w_ref[...], NT).astype(LOW)
            cg_ref[here, :] = context_grad
            product = context_grad.astype(jnp.float32) * ctx_ref[here, :].astype(jnp.float32)
            upper_bits = product.astype(LOW)
            lower_bits = (product - upper_bits.astype(jnp.float32)).astype(LOW)
            delta_ref[:, here] = dot(select, upper_bits, NT) + dot(select, lower_bits, NT)

        def out_work(chip, core):
            here = pl.ds(pl.multiple_of((chip * 2 + core) * rows, rows), rows)
            return dot(hid_ref[here, :], down_ref[...])

        exchange = Exchange(place, staged, landed, sems)

        def fill(offset):
            fetch(offset).wait()
            pl.when(offset > 0)(lambda: fetch(lax.rem(offset + 1, groups)).start())
            values = columns_in[lax.rem(offset, 2)]
            staged[offset, 0] = dot(gg_ref[...], values, TN).astype(LOW)
            staged[offset, 1] = dot(ug_ref[...], values, TN).astype(LOW)

        def fill_send(offset):
            fill(offset)
            exchange.copy(offset).start()

        scatter = Scatter(place, out_work, scratch)
        for copy in late[:3]:
            copy.wait()
        scatter.first()
        for copy in late[3:]:
            copy.wait()

        def step(number):
            scatter.slot(number)
            pieces(number, groups, fill_send)
            gather.pass_on(number)

            @pl.when(number == 0)
            def _():
                gather.wait_chip(place.chip)
                back_work(place.chip)

            gather.each_new(number, back_work)

        each(chips - 1, step)
        scatter.last()
        fill(jnp.int32(0))
        exchange.stay().start()
        keep.wait()
        scatter.own(total)
        out_ref[...] = (mid_ref[...] + total[...]).astype(LOW)
        gather.drain()
        scatter.drain()
        exchange.wait()

    return line_call(
        kernel,
        "gather_context",
        5,
        (middle, normed_grad, out_grad, gain, shift, weight, context, hidden_low, *down_parts, normed, *pair),
        [
            shape((length, width)),
            shape((length, out_width)),
            shape((rows, width), jnp.float32),
            shape((2, width), jnp.float32),
            shape((rows, width)),
            shape((groups, 2, hidden, part)),
            shape((8, length), jnp.float32),
        ],
        [
            pltpu.VMEM((length, width), LOW),
            pltpu.VMEM((rows, width), jnp.float32),
            pltpu.VMEM(weight.shape, LOW),
            pltpu.VMEM((length, out_width), LOW),
            pltpu.VMEM((length, hidden), LOW),
            pltpu.VMEM((hidden, width), LOW),
            pltpu.VMEM((length, hidden), LOW),
            pltpu.VMEM((length, hidden), LOW),
            pltpu.VMEM((groups, 2, hidden, part), LOW),
            pltpu.VMEM((2, length, part), LOW),
            pltpu.SemaphoreType.DMA((11,)),
            pltpu.SemaphoreType.DMA((chips,)),
        ]
        + Scatter.scratch(chips, rows, width)
        + Gather.scratch(chips)
        + Spread.scratch(groups),
        COST_FLOPS,
        in_hbm=(0, 2, 5),
        from_hbm=(1, 5, 6, 7, 8, 9, 10, 11, 12),
    )


class PreparedScatter(Scatter):
    def __init__(self, place, work, scratch, prepare):
        super().__init__(place, work, scratch)
        self.prepare = prepare

    def produce(self, turn):
        self.prepare(turn, self.order(turn))
        super().produce(turn)


def scatter_triple(
    groups, chips, qkv, keys_turned, start, lse, delta, context, context_grad, tables, weights, tokens, gain, shift,
    mid_grad, sums, normed, grads
):
    length, in_width = qkv[0].shape
    rows = length // (2 * chips)
    width = weights.shape[1]
    part = width // groups
    heads = in_width // HD
    tile = tables[0].shape[1]
    reach = LONGEST // rows

    def kernel(
        start_ref, lse_ref, delta, gain_ref, shift_ref, sums_ref,
        q_hbm, k_hbm, v_hbm, turned_hbm, cg_hbm, ctx_hbm, cos_hbm, sin_hbm,
        w_hbm, x_hbm, mg_hbm, a_hbm, full_hbm,
        in_ref, small_ref, landed_qkv, landed_out,
        q_ref, k_ref, v_ref, cg_ref, ctx_ref, cos_ref, sin_ref,
        w_ref, x_ref, mg_ref, columns_in, load, load_columns,
        k_turned, dq_acc, dk_acc, dv_acc, dq_ref, dk_ref, dv_ref, bias,
        total, norm_sums, staged_qkv, staged_out, early_spots, early_groups, late_spots, late_groups, *rest
    ):
        place = Place(groups, chips)
        place.greet(True, True)
        scratch, one, two, sums_sems = split_refs(rest, Scatter.SCRATCH, 2, 2, 8)
        fetches = fetch_all(
            [
                (k_hbm, k_ref),
                (q_hbm, q_ref),
                (v_hbm, v_ref),
                (cg_hbm, cg_ref),
                (turned_hbm, k_turned),
                (cos_hbm, cos_ref),
                (sin_hbm, sin_ref),
                (w_hbm, w_ref),
                (ctx_hbm, ctx_ref),
                (x_hbm, x_ref),
                (mg_hbm, mg_ref),
            ],
            load,
        )
        dq_acc[...] = jnp.zeros_like(dq_acc)
        dk_acc[...] = jnp.zeros_like(dk_acc)
        dv_acc[...] = jnp.zeros_like(dv_acc)
        bias[...] = jnp.zeros_like(bias)
        spots, count = place.spot, 2 * chips
        early_a = SmallSum(early_spots, spots, count, place.fellow, sums_sems[0:2])
        early_b = SmallSum(early_groups, place.group, groups, place.peer, sums_sems[2:4])
        late_a = SmallSum(late_spots, spots, count, place.fellow, sums_sems[4:6])
        late_b = SmallSum(late_groups, place.group, groups, place.peer, sums_sems[6:8])
        for copy in fetches[:8]:
            copy.wait()
        place.meet()
        masks = head_masks(in_width, LOW)
        def attend_back(query_block, key_chip):
            base_q = pl.multiple_of(query_block * rows, rows)
            base_k = pl.multiple_of(key_chip * 2 * rows, 2 * rows)
            rows_q, rows_k = pl.ds(base_q, rows), pl.ds(base_k, 2 * rows)
            queries = (q_ref[rows_q, :] * 0.125).astype(LOW)
            incoming = cg_ref[rows_q, :]
            keys, vals = k_ref[rows_k, :], v_ref[rows_k, :]
            key_ids = base_k + lax.broadcasted_iota(jnp.int32, (2 * rows, rows), 0)
            query_ids = base_q + lax.broadcasted_iota(jnp.int32, (1, rows), 1)
            visible = (key_ids >= start_ref[:, rows_q]) & (key_ids <= query_ids)
            probs, dscores, all_queries, all_incoming = [], [], [], []
            for h in range(heads):
                masked, incoming_masked = queries * masks[h], incoming * masks[h]
                scores = dot(keys, masked, NT)
                prob = jnp.where(visible, jnp.exp(scores - lse_ref[h : h + 1, rows_q]), 0.0)
                dprob = dot(vals, incoming_masked, NT)
                dscore = (prob * (dprob - delta[h : h + 1, rows_q])).astype(LOW)
                band = slice(h * HD, (h + 1) * HD)
                dq_acc[band, rows_q] += dot(k_turned[band, rows_k], dscore)
                probs.append(prob.astype(LOW))
                dscores.append(dscore)
                all_queries.append(masked)
                all_incoming.append(incoming_masked)
            dv_acc[rows_k, :] += dot(
                jnp.concatenate(probs, axis=1), jnp.concatenate(all_incoming, axis=0)
            )
            dk_acc[rows_k, :] += dot(
                jnp.concatenate(dscores, axis=1), jnp.concatenate(all_queries, axis=0)
            )

        def turn_back(values, here):
            parts = [
                rope_tile(
                    values[:, t * tile : (t + 1) * tile],
                    cos_ref[here, :],
                    sin_ref[here, :],
                    -1.0,
                )
                for t in range(in_width // tile)
            ]
            return jnp.concatenate(parts, axis=1) if len(parts) > 1 else parts[0]

        def prepare(turn, chip):
            def with_chip(other):
                done = 0
                for earlier in range(chips):
                    done = done + jnp.where(
                        (scatter.order(earlier) == other) & (earlier < turn), 1, 0
                    )
                upper, lower = jnp.maximum(chip, other), jnp.minimum(chip, other)

                @pl.when(done == 0)
                def _():
                    def one(number):
                        query_block = upper * 2 + number
                        pl.when(query_block - (lower * 2 + 1) <= reach)(
                            lambda: attend_back(query_block, lower)
                        )

                    each(2, one)

            each(chips, with_chip)

            def finish(core):
                here = pl.ds(pl.multiple_of((chip * 2 + core) * rows, rows), rows)
                dq = turn_back(dq_acc[:, here].T * 0.125, here).astype(LOW)
                dk = turn_back(dk_acc[here, :], here).astype(LOW)
                dv = dv_acc[here, :].astype(LOW)
                for number, (ref, values) in enumerate(((dq_ref, dq), (dk_ref, dk), (dv_ref, dv))):
                    ref[here, :] = values
                    bias[number : number + 1, :] += jnp.sum(
                        values.astype(jnp.float32), axis=0, keepdims=True
                    )

            each(2, finish)

        def work(chip, core):
            here = pl.ds(pl.multiple_of((chip * 2 + core) * rows, rows), rows)
            term = dot(dq_ref[here, :], w_ref[0], NT)
            term = term + dot(dk_ref[here, :], w_ref[1], NT)
            return term + dot(dv_ref[here, :], w_ref[2], NT)

        exchange_qkv = Exchange(place, staged_qkv, landed_qkv, one)
        exchange_out = Exchange(place, staged_out, landed_out, two)

        def columns_of(offset):
            block = lax.rem(place.group + offset, groups)
            return pl.ds(pl.multiple_of(block * part, part), part)

        def fetch(source, index):
            columns = columns_of(lax.rem(index + 1, groups))
            slot = lax.rem(index, 2)
            return pltpu.make_async_copy(
                source.at[:, columns], columns_in.at[slot], load_columns.at[slot]
            )

        def fill_out(index):
            fetch(full_hbm, index).wait()
            offset = lax.rem(index + 1, groups)
            staged_out[offset] = dot(ctx_ref[...], columns_in[lax.rem(index, 2)], TN).astype(LOW)
            pl.when(offset > 0)(lambda: exchange_out.copy(offset).start())
            pl.when(offset == 0)(lambda: exchange_out.stay().start())
            pl.when(index + 2 < groups)(lambda: fetch(full_hbm, index + 2).start())
            pl.when(index + 2 >= groups)(lambda: fetch(a_hbm, index + 2 - groups).start())

        def fill_qkv(index):
            fetch(a_hbm, index).wait()
            offset = lax.rem(index + 1, groups)
            values = columns_in[lax.rem(index, 2)]
            for number, ref in enumerate((dq_ref, dk_ref, dv_ref)):
                staged_qkv[offset, number] = dot(values, ref[...], TN).astype(LOW)
            pl.when(offset > 0)(lambda: exchange_qkv.copy(offset).start())
            pl.when(offset == 0)(lambda: exchange_qkv.stay().start())
            pl.when(index + 2 < groups)(lambda: fetch(a_hbm, index + 2).start())

        fetch(full_hbm, 0).start()
        fetch(full_hbm, 1).start()
        scatter = PreparedScatter(place, work, scratch, prepare)
        scatter.first()

        def fills():
            each(groups, fill_qkv)

        def step(number):
            scatter.slot(number, fills)

            @pl.when(number == 0)
            def _():
                early_a.begin(sums_ref[...])
                for copy in fetches[8:]:
                    copy.wait()
                each(groups, fill_out)

        each(chips - 1, step)
        scatter.last()
        pl.when(scatter.lag == 0)(fills)
        early_groups[place.group] = jnp.zeros(early_groups.shape[1:], jnp.float32)
        early_groups[place.group, 4:7, 0:in_width] = bias[0:3, :]
        early_groups[place.group, 0:2, :] = early_a.result()
        early_b.begin(early_groups[place.group])
        scatter.own(total)
        size = rows // 4
        norm_sums[...] = jnp.zeros_like(norm_sums)

        def norm_back(block):
            here = pl.ds(pl.multiple_of(block * size, size), size)
            _, plain, inverse = layer_norm_parts(
                x_ref[here, :].astype(jnp.float32), gain_ref[...], shift_ref[...]
            )
            back, gain_grad, shift_grad = layer_norm_back(
                total[here, :], plain, inverse, gain_ref[...]
            )
            in_ref[here, :] = (mg_ref[here, :] + back).astype(LOW)
            norm_sums[0:1, :] += gain_grad[None, :]
            norm_sums[1:2, :] += shift_grad[None, :]

        each(4, norm_back)
        late_a.begin(norm_sums[...])
        scatter.drain()
        late_b.begin(late_a.result())
        first = early_b.result()
        last = late_b.result()
        small_ref[...] = first
        small_ref[1:2, :] = first[0:1, :]
        small_ref[3:4, :] = first[1:2, :]
        small_ref[0:1, :] = last[0:1, :]
        small_ref[2:3, :] = last[1:2, :]
        exchange_qkv.wait()
        exchange_out.wait()

    devices = 2 * chips
    heads_kind = pltpu.VMEM((length, in_width), LOW)
    heads_sum = pltpu.VMEM((length, in_width), jnp.float32)
    return line_call(
        kernel,
        "scatter_triple",
        6,
        (
            start, lse, delta, gain, shift, sums,
            *qkv, keys_turned, context_grad, context, *tables, weights, tokens, mid_grad, normed, grads,
        ),
        [
            shape((rows, width)),
            shape((8, width), jnp.float32),
            shape((groups, 3, part, in_width)),
            shape((groups, in_width, part)),
        ],
        [
            *(heads_kind for _ in range(5)),
            *(pltpu.VMEM((length, tile), jnp.float32) for _ in range(2)),
            pltpu.VMEM(weights.shape, LOW),
            pltpu.VMEM((rows, width), LOW),
            pltpu.VMEM((rows, width), jnp.float32),
            pltpu.VMEM((2, length, part), LOW),
            pltpu.SemaphoreType.DMA((11,)),
            pltpu.SemaphoreType.DMA((2,)),
            pltpu.VMEM((in_width, length), LOW),
            pltpu.VMEM((in_width, length), jnp.float32),
            heads_sum,
            heads_sum,
            heads_kind,
            heads_kind,
            heads_kind,
            pltpu.VMEM((8, in_width), jnp.float32),
            pltpu.VMEM((rows, width), jnp.float32),
            pltpu.VMEM((2, width), jnp.float32),
            pltpu.VMEM((groups, 3, part, in_width), LOW),
            pltpu.VMEM((groups, in_width, part), LOW),
            pltpu.VMEM((devices, 2, width), jnp.float32),
            pltpu.VMEM((groups, 8, width), jnp.float32),
            pltpu.VMEM((devices, 2, width), jnp.float32),
            pltpu.VMEM((groups, 2, width), jnp.float32),
        ]
        + Scatter.scratch(chips, rows, width)
        + Spread.scratch(groups) * 2
        + [pltpu.SemaphoreType.DMA((n,)) for n in (devices, devices, groups, groups) * 2],
        COST_FLOPS,
        in_hbm=(2, 3),
        from_hbm=tuple(range(6, 19)),
    )


def adam_update(master, gradient, moment_one, moment_two, correct_one, correct_two, rate):
    one_new = 0.9 * moment_one + 0.1 * gradient
    two_new = 0.999 * moment_two + 0.001 * gradient * gradient
    change = one_new / correct_one / (jnp.sqrt(two_new / correct_two) + 1e-08) + 0.1 * master
    return (master - rate * change, one_new, two_new)


def per_device(
    groups,
    chips,
    inputs,
    out_grad,
    segments,
    w_qkv,
    w_out,
    w_gate_up,
    w_down,
    qkv_bias,
    norm_gain,
    norm_bias,
    first_qkv,
    first_out,
    first_gate_up,
    first_down,
    first_bias,
    first_gain,
    first_shift,
    second_qkv,
    second_out,
    second_gate_up,
    second_down,
    second_bias,
    second_gain,
    second_shift,
):
    head_width = w_qkv.shape[2]
    gains = (norm_gain[0:1], norm_gain[1:2])
    shifts = (norm_bias[0:1], norm_bias[1:2])
    half = jnp.arange(ROT // 2, dtype=jnp.float32)
    rates = 10000.0 ** (-(2.0 * half) / ROT)
    rates = jnp.concatenate([rates, rates, jnp.zeros((HD - ROT,), jnp.float32)])
    rates = jnp.tile(rates, min(head_width, 128) // HD)[None, :]

    gate_up_turned = jnp.swapaxes(w_gate_up, 1, 2)
    normed_one_all, qkv_all, out_all, down_one, *rest = gather_project(
        groups,
        chips,
        inputs,
        gains[0],
        shifts[0],
        (w_qkv, w_out, w_down),
        qkv_bias,
        segments,
        rates,
    )
    qkv, (keys_turned, values_turned, start), tables = rest[:3], rest[3:6], rest[6:]
    middle, context_flat, lse, mlp_grad, pair_all, down_two = scatter_heads(
        groups,
        chips,
        qkv[0],
        qkv[1],
        values_turned,
        start,
        out_all,
        inputs,
        out_grad,
        (gate_up_turned, w_down),
    )
    down_parts = (down_one, down_two)
    normed_two_all, hidden_low, gate_grad, up_grad, normed_two_grad, parts_down = hidden_layers(
        groups, chips, middle, gains[1], shifts[1], pair_all, down_parts, mlp_grad
    )
    attn_grad_all, context_grad, middle_grad, sums_two, outputs, parts_pair, delta = (
        gather_context(
            groups,
            chips,
            middle,
            normed_two_grad,
            out_grad,
            gains[1],
            shifts[1],
            out_all,
            context_flat,
            hidden_low,
            down_parts,
            normed_two_all,
            (gate_grad, up_grad),
        )
    )
    input_grad, small, parts_qkv, parts_out = scatter_triple(
        groups,
        chips,
        qkv,
        keys_turned,
        start,
        lse,
        delta,
        context_flat,
        context_grad,
        tables,
        qkv_all,
        inputs,
        gains[0],
        shifts[0],
        middle_grad,
        sums_two,
        normed_one_all,
        attn_grad_all,
    )

    def add_parts(parts):
        total = parts[0].astype(jnp.float32)
        for offset in range(1, groups):
            total = total + parts[offset].astype(jnp.float32)
        return total

    grad_qkv, grad_out, grad_down = add_parts(parts_qkv), add_parts(parts_out), add_parts(parts_down)
    grad_gate_up = jnp.swapaxes(add_parts(parts_pair), 1, 2)
    grad_bias = small[4:7, :head_width]
    grad_gain, grad_shift = small[0:2], small[2:4]
    correct_one = 1.0 - 0.9**STEP
    correct_two = 1.0 - 0.999**STEP
    rates = (0.02, 0.3, 0.02, 0.02, 0.3, 0.3, 0.3)
    masters = (w_qkv, w_out, w_gate_up, w_down, qkv_bias, norm_gain, norm_bias)
    gradients = (grad_qkv, grad_out, grad_gate_up, grad_down, grad_bias, grad_gain, grad_shift)
    firsts = (first_qkv, first_out, first_gate_up, first_down, first_bias, first_gain, first_shift)
    seconds = (
        second_qkv,
        second_out,
        second_gate_up,
        second_down,
        second_bias,
        second_gain,
        second_shift,
    )
    updated = [
        adam_update(
            masters[number],
            gradients[number],
            firsts[number],
            seconds[number],
            correct_one,
            correct_two,
            rates[number],
        )
        for number in range(7)
    ]
    return (
        outputs,
        input_grad,
        grad_qkv,
        grad_out,
        grad_gate_up,
        grad_down,
        grad_bias,
        grad_gain,
        grad_shift,
        updated[0][0],
        updated[1][0],
        updated[2][0],
        updated[3][0],
        updated[4][0],
        updated[5][0],
        updated[6][0],
        updated[0][1],
        updated[1][1],
        updated[2][1],
        updated[3][1],
        updated[4][1],
        updated[5][1],
        updated[6][1],
        updated[0][2],
        updated[1][2],
        updated[2][2],
        updated[3][2],
        updated[4][2],
        updated[5][2],
        updated[6][2],
    )


def solution(mesh):
    in_specs = (
        P(("dp", "tensor"), None),
        P(("dp", "tensor"), None),
        P("dp", None),
        P(None, "dp", "tensor"),
        P("tensor", "dp"),
        P(None, "dp", "tensor"),
        P("tensor", "dp"),
        P(None, "tensor"),
        P(),
        P(),
        P(None, "dp", "tensor"),
        P("tensor", "dp"),
        P(None, "dp", "tensor"),
        P("tensor", "dp"),
        P(None, "tensor"),
        P(),
        P(),
        P(None, "dp", "tensor"),
        P("tensor", "dp"),
        P(None, "dp", "tensor"),
        P("tensor", "dp"),
        P(None, "tensor"),
        P(),
        P(),
    )
    out_specs = (
        P(("dp", "tensor"), None),
        P(("dp", "tensor"), None),
        P(None, "dp", "tensor"),
        P("tensor", "dp"),
        P(None, "dp", "tensor"),
        P("tensor", "dp"),
        P(None, "tensor"),
        P(),
        P(),
        P(None, "dp", "tensor"),
        P("tensor", "dp"),
        P(None, "dp", "tensor"),
        P("tensor", "dp"),
        P(None, "tensor"),
        P(),
        P(),
        P(None, "dp", "tensor"),
        P("tensor", "dp"),
        P(None, "dp", "tensor"),
        P("tensor", "dp"),
        P(None, "tensor"),
        P(),
        P(),
        P(None, "dp", "tensor"),
        P("tensor", "dp"),
        P(None, "dp", "tensor"),
        P("tensor", "dp"),
        P(None, "tensor"),
        P(),
        P(),
    )
    return jax.shard_map(
        functools.partial(per_device, mesh.shape["dp"], mesh.shape["tensor"] // 2),
        mesh=mesh, in_specs=in_specs, out_specs=out_specs, check_vma=False
    )
```
